32 devices in a mesh: tile: 8 (over y, x, core), depth: 4 (over z).
Axes of the slice: x: 2, y: 2, z: 4, core: 2. Of those that a mesh axis runs over, the one named last changes fastest.
Arguments:
- coefficients: float32 [8, 4, 8, 32, 128], P(None, 'depth', 'tile'), may hold values from -24 to 24
- keep_count: int32 [4, 8, 32, 128], P('depth', 'tile'), may hold values from 1 to 8, as said below
- view_flip: int32 [8], P('tile'), may hold values from 0 to 1
Outputs:
- image: float32 [4, 128, 512], P(None, 'tile', 'depth')
The draws below stay inside these ranges and needn't reach their ends.
Inputs may be any that keep to these rules, and one draw needn't show every extreme that they name: `keep_count`: along the block rows, blocks 2 j and 2 j + 1 of every brick and block column retain 8 + 1 slots together.
All inputs are finite; a program needn't handle non-finite values.
Results may differ from the reference program's by a relative error of at most 0.0003.
Values sent between devices are 32-bit elements; how exact they have to be, the bound alone decides.
No kernel may reach another device: no remote copies, remote signals or barrier semaphores. Data moves between devices by JAX's collectives and lax.ppermute only.
A program may use at most 64 MiB of HBM per device.

```python
import math
import jax
import jax.numpy as jnp
import numpy as np
from jax import lax

KMAX = 8
GY = 512
GX = 128
GZ = 128
TXB = 4
GXB = 32
GYB = 128
N_TILE = 8
N_DEPTH = 4


def draw_keep_count(key, part):
    first = jax.random.randint(jax.random.fold_in(key, 11), (N_DEPTH, N_TILE, GXB, GYB // 2), 1, KMAX + 1)
    second = KMAX + 1 - first
    return jnp.stack([first, second], axis=-1).reshape(N_DEPTH, N_TILE, GXB, GYB).astype(jnp.int32)


def set_ends(values, key, low, top_value):
    dims = values.shape
    place = [jax.random.randint(jax.random.fold_in(key, axis), (), 0, dims[axis]) for axis in range(len(dims))]
    values = values.at[tuple(place)].set(low)
    longest = dims.index(max(dims))
    place[longest] = (place[longest] + 1) % dims[longest]
    return values.at[tuple(place)].set(top_value)


def levels(own_key, shape, shards, smallest, top_value):
    loudness = 1.0
    for dim, blocks in shards:
        draws = jax.random.uniform(jax.random.fold_in(jax.random.fold_in(own_key, 6), dim), (blocks,), jnp.float32, smallest / len(shards), top_value / len(shards))
        loudness = loudness * jnp.repeat(jnp.exp(draws), shape[dim] // blocks).reshape((-1,) + (1,) * (len(shape) - 1 - dim))
    return loudness


def gaussian(key, dims, scale, most, cuts=(), kind=jnp.bfloat16):
    array = jax.random.normal(key, dims, jnp.float32) * scale
    if len(cuts) > 0:
        array = levels(key, dims, cuts, -0.22, 0.18) * array
    return jnp.clip(array, min=-most, max=most).astype(kind)


def setup_inputs(seed: int = 0) -> dict:
    arg_keys = jax.random.split(jax.random.key(seed), 4)
    coefficients = gaussian(arg_keys[0], (KMAX, N_DEPTH, N_TILE, GXB, GYB), 4.0, 24.0, ((1, 4), (2, 8)), jnp.float32)
    keep_count = draw_keep_count(jax.random.fold_in(arg_keys[3], 71), 0)
    view_flip = set_ends(jax.random.randint(arg_keys[2], (N_TILE,), 0, 2), jax.random.fold_in(arg_keys[2], 1), 0, 1).astype(jnp.int32)
    return {"coefficients": coefficients, "keep_count": keep_count, "view_flip": view_flip}


slot_frequencies = ((0, 0, 0), (0, 0, 1), (0, 1, 0), (1, 0, 0), (0, 0, 2), (0, 1, 1), (0, 2, 0), (1, 0, 1))

def cosine_rows():
    result = np.zeros((4, 4))
    for frequency in range(4):
        factor = 0.5 if frequency == 0 else math.sqrt(0.5)
        for position in range(4):
            result[frequency, position] = factor * math.cos(math.pi * (2 * position + 1) * frequency / 8.0)
    return result

def basis_matrix(slot_count):
    rows_table = cosine_rows()
    result = np.zeros((4, 4, 4, slot_count))
    for slot_index in range(slot_count):
        freq_z, freq_x, freq_y = slot_frequencies[slot_index]
        result[:, :, :, slot_index] = rows_table[freq_z][:, None, None] * rows_table[freq_x][None, :, None] * rows_table[freq_y][None, None, :]
    return jnp.asarray(result.reshape(64, slot_count), dtype=jnp.float32)

def render_columns(block_coef, basis_rows, flipped, sample_count):
    slot_count, zblocks, column_count = block_coef.shape
    flat_coef = block_coef.reshape(slot_count, zblocks * column_count)
    cell_values = jnp.dot(basis_rows, flat_coef, precision=lax.Precision.HIGHEST, preferred_element_type=jnp.float32)
    cell_values = cell_values.reshape(4, 16, zblocks, column_count)
    density = jnp.transpose(cell_values, (2, 0, 1, 3)).reshape(zblocks * 4, 16, column_count)
    optical = 1.5 * jax.nn.softplus(2.0 * density) / sample_count
    inclusive = jnp.cumsum(optical, axis=0)
    total_depth = inclusive[-1]
    entering = jnp.where(flipped > 0, total_depth[None] - inclusive, inclusive - optical)
    weights = jnp.exp(-entering) * -jnp.expm1(-optical)
    red_sum = lax.optimization_barrier(jnp.sum(weights * jax.nn.sigmoid(2.0 * density), axis=0))
    green_sum = lax.optimization_barrier(jnp.sum(weights * jnp.exp(-density * density), axis=0))
    blue_sum = lax.optimization_barrier(jnp.sum(weights * jax.nn.sigmoid(1.5 - density), axis=0))
    opacity = -jnp.expm1(-total_depth)
    return jnp.stack([red_sum, green_sum, blue_sum, opacity])

def to_image(layer, strip_blocks, column_blocks):
    spread = layer.reshape(4, 4, 4, strip_blocks, column_blocks)
    return jnp.transpose(spread, (0, 3, 1, 4, 2)).reshape(4, strip_blocks * 4, column_blocks * 4)

def composite(layers, flipped, layer_axis):
    clearance = 1.0 - layers[3:4]
    piece_count = layers.shape[layer_axis]
    forward = jnp.cumprod(clearance, axis=layer_axis)
    backward = jnp.flip(jnp.cumprod(jnp.flip(clearance, layer_axis), axis=layer_axis), layer_axis)
    unit_slice = jnp.ones_like(lax.slice_in_dim(clearance, 0, 1, axis=layer_axis))
    before_forward = jnp.concatenate([unit_slice, lax.slice_in_dim(forward, 0, piece_count - 1, axis=layer_axis)], axis=layer_axis)
    before_backward = jnp.concatenate([lax.slice_in_dim(backward, 1, piece_count, axis=layer_axis), unit_slice], axis=layer_axis)
    passing = jnp.where(flipped > 0, before_backward, before_forward)
    return lax.optimization_barrier(jnp.sum(passing * layers, axis=layer_axis))

def reference(coefficients, keep_count, view_flip):
    slot_index = lax.broadcasted_iota(jnp.int32, coefficients.shape, 0)
    masked = jnp.where(slot_index < keep_count[None], coefficients, jnp.float32(0.0))
    basis_rows = basis_matrix(KMAX)
    bricks = masked.reshape(KMAX, N_DEPTH, N_TILE, N_TILE, TXB, GYB)
    bricks = jnp.transpose(bricks, (3, 1, 0, 2, 4, 5)).reshape(N_TILE, N_DEPTH, KMAX, N_TILE, TXB * GYB)

    def per_tile(inputs):
        tile_bricks, flipped = inputs

        def per_brick(brick_coef):
            layer = render_columns(brick_coef, basis_rows, flipped, GZ)
            return to_image(layer, TXB, GYB)
        layers = lax.map(per_brick, tile_bricks)
        layers = jnp.moveaxis(layers, 0, 1)
        return composite(layers, flipped, 1)
    strips = lax.map(per_tile, (bricks, view_flip))
    return jnp.transpose(strips, (1, 0, 2, 3)).reshape(4, GX, GY)
```

```python
import math

import jax
import jax.numpy as jnp
from jax import lax
from jax.experimental import pallas as pl
from jax.experimental.pallas import tpu as pltpu
from jax.sharding import PartitionSpec as P

LOG2E = math.log2(math.e)
EDGE = 4


def cosine(frequency, position):
    factor = 0.5 if frequency == 0 else math.sqrt(0.5)
    return factor * math.cos(math.pi * (2 * position + 1) * frequency / 8.0)


def pack_kernel(coef_ref, keep_ref, out_ref, *, tiles, depths):
    slots, columns, rows = coef_ref.shape
    strip = columns // tiles
    band = rows // depths
    slot_index = lax.broadcasted_iota(jnp.int32, (slots, rows), 0)
    for t in range(tiles):
        masked = []
        for b in range(strip):
            c = t * strip + b
            keep = jnp.broadcast_to(keep_ref[pl.ds(c, 1), :], (slots, rows))
            masked.append(jnp.where(slot_index < keep, coef_ref[:, c, :], 0.0))
        for d in range(depths):
            out_ref[d * tiles + t] = jnp.concatenate(
                [m[:, d * band : (d + 1) * band] for m in masked], axis=1
            )


def render_kernel(flip_ref, coef_ref, out_ref, *, strip, band, samples):
    zblocks, slots, lanes = coef_ref.shape
    flipped = flip_ref[0] > 0
    b1 = [cosine(1, i) for i in range(EDGE)]
    row = lax.broadcasted_iota(jnp.int32, (2 * EDGE, lanes), 0)
    x = row % EDGE
    y = row // EDGE

    def table(position, values):
        result = jnp.full((2 * EDGE, lanes), values[0], jnp.float32)
        for i in range(1, len(values)):
            result = jnp.where(position == i, jnp.float32(values[i]), result)
        return result

    x1 = table(x, b1)
    x2 = table(x, [cosine(2, i) for i in range(EDGE)])
    y1 = table(y, b1[:2])
    y2 = table(y, [cosine(2, i) for i in range(2)])
    sign = jnp.where(flipped, jnp.float32(-1.0), jnp.float32(1.0))
    c_dc = 0.125 * LOG2E
    c_x1 = (0.25 * LOG2E) * x1
    c_x2 = (0.25 * LOG2E) * x2
    c_y1 = (0.25 * LOG2E) * y1
    c_y2 = (0.25 * LOG2E) * y2
    c_xy = (0.5 * LOG2E) * x1 * y1
    c_z = jnp.full((2 * EDGE, lanes), 0.25 * LOG2E * b1[0], jnp.float32) * sign
    c_zy = (0.5 * LOG2E * b1[0]) * y1 * sign
    ratio = b1[1] / b1[0]
    blue_factor = math.exp(-1.5)
    fade = -1.5 / samples

    def block(step, state):
        zb = jnp.where(flipped, zblocks - 1 - step, step)
        a = [
            jnp.broadcast_to(coef_ref[zb, pl.ds(k, 1), :], (2 * EDGE, lanes)) for k in range(slots)
        ]
        even = a[0] * c_dc + a[2] * c_x1 + a[4] * c_y2 + a[6] * c_x2
        odd = a[1] * c_y1 + a[5] * c_xy
        g_even = a[3] * c_z
        g_odd = a[7] * c_zy
        halves = []
        for h in range(2):
            depth, before, red, green, blue = state[h]
            base = even + odd if h == 0 else even - odd
            g = g_even + g_odd if h == 0 else g_even - g_odd
            near = g * ratio
            for f in (base + g, base + near, base - near, base - g):
                v = jnp.exp2(f)
                one_u = 1.0 + v * v
                depth = depth + jnp.log2(one_u)
                after = jnp.exp2(fade * depth)
                weight = before - after
                before = after
                red = red + weight / one_u
                green = green + weight * jnp.exp2(f * (f * (-1.0 / LOG2E)))
                blue = blue + weight / (1.0 + blue_factor * v)
            halves.append((depth, before, red, green, blue))
        return tuple(halves)

    zero = jnp.zeros((2 * EDGE, lanes), jnp.float32)
    one = jnp.ones((2 * EDGE, lanes), jnp.float32)
    start = (zero, one, zero, zero, zero)
    state = lax.fori_loop(0, zblocks, block, (start, start), unroll=4)

    width = band * EDGE
    pick = lax.broadcasted_iota(jnp.int32, (2 * EDGE, width), 1)
    y_out = pick % EDGE
    place = pick // EDGE
    outs = []
    for _, before, red, green, blue in state:
        opacity = 1.0 - before
        outs.append((opacity - red, green, blue, opacity))
    for ch in range(4):
        for b in range(strip):
            index = place + b * band
            low = jnp.take_along_axis(outs[0][ch], index, axis=1)
            high = jnp.take_along_axis(outs[1][ch], index, axis=1)
            both = jnp.where(y_out < 2, low, high)
            first, second = both[:EDGE], both[EDGE:]
            use_first = (y_out[:EDGE] == 0) | (y_out[:EDGE] == 3)
            out_ref[ch, pl.ds(b * EDGE, EDGE), :] = jnp.where(use_first, first, second)


def per_device(coefficients, keep_count, view_flip):
    tiles = lax.axis_size("tile")
    depths = lax.axis_size("depth")
    slots, _, _, columns, rows = coefficients.shape
    strip = columns // tiles
    band = rows // depths
    zblocks = tiles * depths
    vmem = pl.BlockSpec(memory_space=pltpu.VMEM)
    smem = pl.BlockSpec(memory_space=pltpu.SMEM)
    outgoing = pl.pallas_call(
        lambda *refs: pack_kernel(*refs, tiles=tiles, depths=depths),
        out_shape=jax.ShapeDtypeStruct((zblocks, slots, strip * band), jnp.float32),
        in_specs=[vmem, vmem],
        out_specs=vmem,
        name="pack",
    )(coefficients.reshape(slots, columns, rows), keep_count.reshape(columns, rows))
    arrived = lax.all_to_all(outgoing, ("depth", "tile"), split_axis=0, concat_axis=0, tiled=True)
    return pl.pallas_call(
        lambda *refs: render_kernel(*refs, strip=strip, band=band, samples=EDGE * zblocks),
        out_shape=jax.ShapeDtypeStruct((4, strip * EDGE, band * EDGE), jnp.float32),
        in_specs=[smem, vmem],
        out_specs=vmem,
        name="render",
    )(view_flip, arrived)


def solution(mesh):
    placed = (P(None, "depth", "tile", None, None), P("depth", "tile", None, None), P("tile"))
    return jax.shard_map(
        per_device, mesh=mesh, in_specs=placed, out_specs=P(None, "tile", "depth"), check_vma=False
    )
```

```python
import math

import jax
import jax.numpy as jnp
from jax import lax
from jax.experimental import pallas as pl
from jax.experimental.pallas import tpu as pltpu
from jax.sharding import PartitionSpec as P

LOG2E = math.log2(math.e)
EDGE = 4


def cosine(frequency, position):
    factor = 0.5 if frequency == 0 else math.sqrt(0.5)
    return factor * math.cos(math.pi * (2 * position + 1) * frequency / 8.0)


def pack_kernel(coef_hbm, keep_hbm, out_ref, coef_ref, keep_ref, arrival, *, tiles, depths):
    slots, columns, rows = coef_ref.shape
    strip = columns // tiles
    band = rows // depths
    fetches = [
        pltpu.make_async_copy(coef_hbm, coef_ref, arrival.at[0]),
        pltpu.make_async_copy(keep_hbm, keep_ref, arrival.at[1]),
    ]
    for fetch in fetches:
        fetch.start()
    for fetch in fetches:
        fetch.wait()
    slot_index = lax.broadcasted_iota(jnp.int32, (slots, rows), 0)
    for t in range(tiles):
        masked = []
        for b in range(strip):
            c = t * strip + b
            keep = jnp.broadcast_to(keep_ref[pl.ds(c, 1), :], (slots, rows))
            masked.append(jnp.where(slot_index < keep, coef_ref[:, c, :], 0.0))
        for d in range(depths):
            out_ref[d * tiles + t] = jnp.concatenate(
                [m[:, d * band : (d + 1) * band] for m in masked], axis=1
            )


def render_kernel(flip_ref, coef_ref, out_ref, *, strip, band, samples):
    zblocks, slots, lanes = coef_ref.shape
    flipped = flip_ref[0] > 0
    sign = jnp.where(flipped, jnp.float32(-1.0), jnp.float32(1.0))
    b1 = [cosine(1, i) for i in range(EDGE)]
    row = lax.broadcasted_iota(jnp.int32, (2 * EDGE, lanes), 0)
    x = row % EDGE
    y = row // EDGE

    def table(position, values):
        result = jnp.full((2 * EDGE, lanes), values[0], jnp.float32)
        for i in range(1, len(values)):
            result = jnp.where(position == i, jnp.float32(values[i]), result)
        return result

    x1 = table(x, b1)
    x2 = table(x, [cosine(2, i) for i in range(EDGE)])
    y1 = table(y, b1[:2])
    y2 = table(y, [cosine(2, i) for i in range(2)])
    c_dc = 0.125 * LOG2E
    c_x1 = (0.25 * LOG2E) * x1
    c_x2 = (0.25 * LOG2E) * x2
    c_y1 = (0.25 * LOG2E) * y1
    c_y2 = (0.25 * LOG2E) * y2
    c_xy = (0.5 * LOG2E) * x1 * y1
    c_z = jnp.full((2 * EDGE, lanes), 0.25 * LOG2E * b1[0], jnp.float32) * sign
    c_zy = (0.5 * LOG2E * b1[0]) * y1 * sign
    ratio = b1[1] / b1[0]
    blue_factor = math.exp(-1.5)
    fade = -1.5 / samples

    def block(step, state):
        zb = jnp.where(flipped, zblocks - 1 - step, step)
        a = [
            jnp.broadcast_to(coef_ref[zb, pl.ds(k, 1), :], (2 * EDGE, lanes)) for k in range(slots)
        ]
        even = a[0] * c_dc + a[2] * c_x1 + a[4] * c_y2 + a[6] * c_x2
        odd = a[1] * c_y1 + a[5] * c_xy
        g_even = a[3] * c_z
        g_odd = a[7] * c_zy
        halves = []
        for h in range(2):
            depth, before, red, green, blue = state[h]
            base = even + odd if h == 0 else even - odd
            g = g_even + g_odd if h == 0 else g_even - g_odd
            near = g * ratio
            for f in (base + g, base + near, base - near, base - g):
                v = jnp.exp2(f)
                one_u = 1.0 + v * v
                depth = depth + jnp.log2(one_u)
                after = jnp.exp2(fade * depth)
                weight = before - after
                before = after
                red = red + weight / one_u
                green = green + weight * jnp.exp2(f * (f * (-1.0 / LOG2E)))
                blue = blue + weight / (1.0 + blue_factor * v)
            halves.append((depth, before, red, green, blue))
        return tuple(halves)

    zero = jnp.zeros((2 * EDGE, lanes), jnp.float32)
    one = jnp.ones((2 * EDGE, lanes), jnp.float32)
    start = (zero, one, zero, zero, zero)
    state = lax.fori_loop(0, zblocks, block, (start, start), unroll=4)

    width = band * EDGE
    pick = lax.broadcasted_iota(jnp.int32, (2 * EDGE, width), 1)
    y_out = pick % EDGE
    place = pick // EDGE
    outs = []
    for _, before, red, green, blue in state:
        opacity = 1.0 - before
        outs.append((opacity - red, green, blue, opacity))
    for ch in range(4):
        for b in range(strip):
            index = place + b * band
            low = jnp.take_along_axis(outs[0][ch], index, axis=1)
            high = jnp.take_along_axis(outs[1][ch], index, axis=1)
            both = jnp.where(y_out < 2, low, high)
            first, second = both[:EDGE], both[EDGE:]
            use_first = (y_out[:EDGE] == 0) | (y_out[:EDGE] == 3)
            out_ref[ch, pl.ds(b * EDGE, EDGE), :] = jnp.where(use_first, first, second)


def per_device(coefficients, keep_count, view_flip):
    tiles = lax.axis_size("tile")
    depths = lax.axis_size("depth")
    slots, _, _, columns, rows = coefficients.shape
    strip = columns // tiles
    band = rows // depths
    zblocks = tiles * depths
    vmem = pl.BlockSpec(memory_space=pltpu.VMEM)
    params = pltpu.CompilerParams(vmem_limit_bytes=4 * 1024 * 1024)
    outgoing = pl.pallas_call(
        lambda *refs: pack_kernel(*refs, tiles=tiles, depths=depths),
        out_shape=jax.ShapeDtypeStruct((zblocks, slots, strip * band), jnp.float32),
        in_specs=[pl.BlockSpec(memory_space=pltpu.HBM)] * 2,
        out_specs=vmem,
        scratch_shapes=[
            pltpu.VMEM((slots, columns, rows), jnp.float32),
            pltpu.VMEM((columns, rows), jnp.int32),
            pltpu.SemaphoreType.DMA((2,)),
        ],
        compiler_params=params,
        name="pack",
    )(coefficients.reshape(slots, columns, rows), keep_count.reshape(columns, rows))
    arrived = lax.all_to_all(outgoing, ("depth", "tile"), split_axis=0, concat_axis=0, tiled=True)
    return pl.pallas_call(
        lambda *refs: render_kernel(*refs, strip=strip, band=band, samples=EDGE * zblocks),
        out_shape=jax.ShapeDtypeStruct((4, strip * EDGE, band * EDGE), jnp.float32),
        in_specs=[pl.BlockSpec(memory_space=pltpu.SMEM), vmem],
        out_specs=vmem,
        compiler_params=params,
        name="render",
    )(view_flip, arrived)


def solution(mesh):
    placed = (P(None, "depth", "tile", None, None), P("depth", "tile", None, None), P("tile"))
    return jax.shard_map(
        per_device, mesh=mesh, in_specs=placed, out_specs=P(None, "tile", "depth"), check_vma=False
    )
```

```python
import math

import jax
import jax.numpy as jnp
from jax import lax
from jax.experimental import pallas as pl
from jax.experimental.pallas import tpu as pltpu
from jax.sharding import PartitionSpec as P

LOG2E = math.log2(math.e)
EDGE = 4


def cosine(frequency, position):
    factor = 0.5 if frequency == 0 else math.sqrt(0.5)
    return factor * math.cos(math.pi * (2 * position + 1) * frequency / 8.0)


def swap_halves(values):
    half = values.shape[1] // 2
    if values.shape[1] % 128 == 0:
        return pltpu.roll(values, half, 1)
    return jnp.concatenate([values[:, half:], values[:, :half]], axis=1)


def pack_kernel(coef_ref, keep_ref, out_ref, *, tiles, depths):
    _, columns, rows = coef_ref.shape
    strip = columns // tiles
    band = rows // depths
    lane = lax.broadcasted_iota(jnp.int32, (tiles, rows), 1)
    even = lane % 2 == 0

    def take(values, index):
        return jnp.take_along_axis(values, index, axis=1)

    other = lane + 1 - 2 * (lane % 2)
    packed = []
    for b in range(strip):
        mine = pl.ds(b, tiles, stride=strip)
        keep = keep_ref[mine, :]
        slot = [coef_ref[k, mine, :] for k in range(8)]
        result = [slot[0]]
        for q in (1, 2, 3, 4):
            result.append(jnp.where(keep > q, slot[q], take(slot[8 - q], other)))
        result[4] = jnp.where(even, result[4], (9 - keep).astype(jnp.float32))
        packed.append(result)
    half = strip * band // 2
    parity = lane // half % 2
    column = lane // (band // 2) % strip
    source = lane % (band // 2) * 2 + parity
    for d in range(depths):
        for q in range(5):
            gathered = [take(packed[b][q], source + d * band) for b in range(strip)]
            merged = gathered[0]
            for b in range(1, strip):
                merged = jnp.where(column == b, gathered[b], merged)
            out_ref[pl.ds(d * tiles, tiles), q, 0, :] = merged[:, : 2 * half]


def unpack(packed_ref, coef_ref):
    zblocks, _, _, lanes = packed_ref.shape
    first = lax.broadcasted_iota(jnp.int32, (zblocks, lanes), 1) < lanes // 2
    row = [packed_ref[:, q, 0, :] for q in range(5)]
    turned = [None] + [swap_halves(row[q]) for q in (1, 2, 3, 4)]
    keep = jnp.where(first, turned[4], 9.0 - row[4])
    slot = [row[0]] + [jnp.where(keep > q, row[q], 0.0) for q in (1, 2, 3)]
    slot.append(jnp.where(keep > 4, jnp.where(first, row[4], turned[4]), 0.0))
    slot += [jnp.where(keep > k, turned[8 - k], 0.0) for k in (5, 6, 7)]
    for k in range(8):
        coef_ref[k] = slot[k]


def render_kernel(flip_ref, packed_ref, out_ref, coef_ref, *, strip, band, samples):
    unpack(packed_ref, coef_ref)
    slots, zblocks, lanes = coef_ref.shape
    flipped = flip_ref[0] > 0
    sign = jnp.where(flipped, jnp.float32(-1.0), jnp.float32(1.0))
    b1 = [cosine(1, i) for i in range(EDGE)]
    row = lax.broadcasted_iota(jnp.int32, (2 * EDGE, lanes), 0)
    x = row % EDGE
    y = row // EDGE

    def table(position, values):
        result = jnp.full((2 * EDGE, lanes), values[0], jnp.float32)
        for i in range(1, len(values)):
            result = jnp.where(position == i, jnp.float32(values[i]), result)
        return result

    x1 = table(x, b1)
    x2 = table(x, [cosine(2, i) for i in range(EDGE)])
    y1 = table(y, b1[:2])
    y2 = table(y, [cosine(2, i) for i in range(2)])
    c_dc = 0.125 * LOG2E
    c_x1 = (0.25 * LOG2E) * x1
    c_x2 = (0.25 * LOG2E) * x2
    c_y1 = (0.25 * LOG2E) * y1
    c_y2 = (0.25 * LOG2E) * y2
    c_xy = (0.5 * LOG2E) * x1 * y1
    c_z = jnp.full((2 * EDGE, lanes), 0.25 * LOG2E * b1[0], jnp.float32) * sign
    c_zy = (0.5 * LOG2E * b1[0]) * y1 * sign
    ratio = b1[1] / b1[0]
    blue_factor = math.exp(-1.5)
    fade = -1.5 / samples

    def block(step, state):
        zb = jnp.where(flipped, zblocks - 1 - step, step)
        a = [
            jnp.broadcast_to(coef_ref[k, pl.ds(zb, 1), :], (2 * EDGE, lanes)) for k in range(slots)
        ]
        even = a[0] * c_dc + a[2] * c_x1 + a[4] * c_y2 + a[6] * c_x2
        odd = a[1] * c_y1 + a[5] * c_xy
        g_even = a[3] * c_z
        g_odd = a[7] * c_zy
        halves = []
        for h in range(2):
            depth, before, red, green, blue = state[h]
            base = even + odd if h == 0 else even - odd
            g = g_even + g_odd if h == 0 else g_even - g_odd
            near = g * ratio
            for f in (base + g, base + near, base - near, base - g):
                v = jnp.exp2(f)
                one_u = 1.0 + v * v
                depth = depth + jnp.log2(one_u)
                after = jnp.exp2(fade * depth)
                weight = before - after
                before = after
                red = red + weight / one_u
                green = green + weight * jnp.exp2(f * (f * (-1.0 / LOG2E)))
                blue = blue + weight / (1.0 + blue_factor * v)
            halves.append((depth, before, red, green, blue))
        return tuple(halves)

    zero = jnp.zeros((2 * EDGE, lanes), jnp.float32)
    one = jnp.ones((2 * EDGE, lanes), jnp.float32)
    start = (zero, one, zero, zero, zero)
    state = lax.fori_loop(0, zblocks, block, (start, start), unroll=4)

    width = band * EDGE
    pick = lax.broadcasted_iota(jnp.int32, (2 * EDGE, width), 1)
    y_out = pick % EDGE
    place = pick // EDGE
    place = place % 2 * (lanes // 2) + place // 2
    outs = []
    for _, before, red, green, blue in state:
        opacity = 1.0 - before
        outs.append((opacity - red, green, blue, opacity))
    for ch in range(4):
        for b in range(strip):
            index = place + b * (band // 2)
            low = jnp.take_along_axis(outs[0][ch], index, axis=1)
            high = jnp.take_along_axis(outs[1][ch], index, axis=1)
            both = jnp.where(y_out < 2, low, high)
            first, second = both[:EDGE], both[EDGE:]
            use_first = (y_out[:EDGE] == 0) | (y_out[:EDGE] == 3)
            out_ref[ch, pl.ds(b * EDGE, EDGE), :] = jnp.where(use_first, first, second)


def per_device(coefficients, keep_count, view_flip):
    tiles = lax.axis_size("tile")
    depths = lax.axis_size("depth")
    slots, _, _, columns, rows = coefficients.shape
    strip = columns // tiles
    band = rows // depths
    zblocks = tiles * depths
    vmem = pl.BlockSpec(memory_space=pltpu.VMEM)
    smem = pl.BlockSpec(memory_space=pltpu.SMEM)
    lanes = strip * band
    outgoing = pl.pallas_call(
        lambda *refs: pack_kernel(*refs, tiles=tiles, depths=depths),
        out_shape=jax.ShapeDtypeStruct((zblocks, 5, 1, lanes), jnp.float32),
        in_specs=[vmem, vmem],
        out_specs=vmem,
        name="pack",
    )(coefficients.reshape(slots, columns, rows), keep_count.reshape(columns, rows))
    arrived = lax.all_to_all(outgoing, ("depth", "tile"), split_axis=0, concat_axis=0, tiled=True)
    return pl.pallas_call(
        lambda *refs: render_kernel(*refs, strip=strip, band=band, samples=EDGE * zblocks),
        out_shape=jax.ShapeDtypeStruct((4, strip * EDGE, band * EDGE), jnp.float32),
        in_specs=[smem, vmem],
        out_specs=vmem,
        scratch_shapes=[pltpu.VMEM((slots, zblocks, lanes), jnp.float32)],
        compiler_params=pltpu.CompilerParams(vmem_limit_bytes=8 * 1024 * 1024),
        name="render",
    )(view_flip, arrived)


def solution(mesh):
    placed = (P(None, "depth", "tile", None, None), P("depth", "tile", None, None), P("tile"))
    return jax.shard_map(
        per_device, mesh=mesh, in_specs=placed, out_specs=P(None, "tile", "depth"), check_vma=False
    )
```

```python
import math

import jax
import jax.numpy as jnp
from jax import lax
from jax.experimental import pallas as pl
from jax.experimental.pallas import tpu as pltpu
from jax.sharding import PartitionSpec as P

LOG2E = math.log2(math.e)
EDGE = 4


def cosine(frequency, position):
    factor = 0.5 if frequency == 0 else math.sqrt(0.5)
    return factor * math.cos(math.pi * (2 * position + 1) * frequency / 8.0)


def swap_halves(values):
    half = values.shape[1] // 2
    if values.shape[1] % 128 == 0:
        return pltpu.roll(values, half, 1)
    return jnp.concatenate([values[:, half:], values[:, :half]], axis=1)


def pack_kernel(coef_ref, keep_ref, out_ref, *, tiles, depths):
    _, columns, rows = coef_ref.shape
    strip = columns // tiles
    band = rows // depths
    lane = lax.broadcasted_iota(jnp.int32, (tiles, rows), 1)
    even = lane % 2 == 0

    def take(values, index):
        return jnp.take_along_axis(values, index, axis=1)

    other = lane + 1 - 2 * (lane % 2)
    packed = []
    for b in range(strip):
        mine = pl.ds(b, tiles, stride=strip)
        keep = keep_ref[mine, :]
        slot = [coef_ref[k, mine, :] for k in range(8)]
        result = [slot[0]]
        for q in (1, 2, 3, 4):
            result.append(jnp.where(keep > q, slot[q], take(slot[8 - q], other)))
        result[4] = jnp.where(even, result[4], (9 - keep).astype(jnp.float32))
        packed.append(result)
    half = strip * band // 2
    parity = lane // half % 2
    column = lane // (band // 2) % strip
    source = lane % (band // 2) * 2 + parity
    for d in range(depths):
        for q in range(5):
            gathered = [take(packed[b][q], source + d * band) for b in range(strip)]
            merged = gathered[0]
            for b in range(1, strip):
                merged = jnp.where(column == b, gathered[b], merged)
            out_ref[pl.ds(d * tiles, tiles), q, 0, :] = merged[:, : 2 * half]


def unpack(packed_ref, coef_ref):
    zblocks, _, _, lanes = packed_ref.shape
    first = lax.broadcasted_iota(jnp.int32, (zblocks, lanes), 1) < lanes // 2
    row = [packed_ref[:, q, 0, :] for q in range(5)]
    turned = [None] + [swap_halves(row[q]) for q in (1, 2, 3, 4)]
    keep = jnp.where(first, turned[4], 9.0 - row[4])
    slot = [row[0]] + [jnp.where(keep > q, row[q], 0.0) for q in (1, 2, 3)]
    slot.append(jnp.where(keep > 4, jnp.where(first, row[4], turned[4]), 0.0))
    slot += [jnp.where(keep > k, turned[8 - k], 0.0) for k in (5, 6, 7)]
    for k in range(8):
        coef_ref[k] = slot[k]


def render_kernel(flip_ref, packed_ref, out_ref, coef_ref, *, strip, band, samples):
    unpack(packed_ref, coef_ref)
    slots, zblocks, lanes = coef_ref.shape
    flipped = flip_ref[0] > 0
    sign = jnp.where(flipped, jnp.float32(-1.0), jnp.float32(1.0))
    b1 = [cosine(1, i) for i in range(EDGE)]
    row = lax.broadcasted_iota(jnp.int32, (2 * EDGE, lanes), 0)
    x = row % EDGE
    y = row // EDGE

    def table(position, values):
        result = jnp.full((2 * EDGE, lanes), values[0], jnp.float32)
        for i in range(1, len(values)):
            result = jnp.where(position == i, jnp.float32(values[i]), result)
        return result

    x1 = table(x, b1)
    x2 = table(x, [cosine(2, i) for i in range(EDGE)])
    y1 = table(y, b1[:2])
    y2 = table(y, [cosine(2, i) for i in range(2)])
    c_dc = 0.125 * LOG2E
    c_x1 = (0.25 * LOG2E) * x1
    c_x2 = (0.25 * LOG2E) * x2
    c_y1 = (0.25 * LOG2E) * y1
    c_y2 = (0.25 * LOG2E) * y2
    c_xy = (0.5 * LOG2E) * x1 * y1
    c_z = jnp.full((2 * EDGE, lanes), 0.25 * LOG2E * b1[0], jnp.float32) * sign
    c_zy = (0.5 * LOG2E * b1[0]) * y1 * sign
    ratio = b1[1] / b1[0]
    blue_factor = math.exp(-1.5)
    fade = -1.5 / samples

    def block(step, state):
        zb = jnp.where(flipped, zblocks - 1 - step, step)
        a = [
            jnp.broadcast_to(coef_ref[k, pl.ds(zb, 1), :], (2 * EDGE, lanes)) for k in range(slots)
        ]
        even = a[0] * c_dc + a[2] * c_x1 + a[4] * c_y2 + a[6] * c_x2
        odd = a[1] * c_y1 + a[5] * c_xy
        g_even = a[3] * c_z
        g_odd = a[7] * c_zy
        halves = []
        for h in range(2):
            depth, before, red, green, blue = state[h]
            base = even + odd if h == 0 else even - odd
            g = g_even + g_odd if h == 0 else g_even - g_odd
            near = g * ratio
            for f in (base + g, base + near, base - near, base - g):
                v = jnp.exp2(f)
                one_u = 1.0 + v * v
                depth = depth + jnp.log2(one_u)
                after = jnp.exp2(fade * depth)
                weight = before - after
                before = after
                red = red + weight * pl.reciprocal(one_u, approx=True)
                green = green + weight * jnp.exp2(f * (f * (-1.0 / LOG2E)))
                blue = blue + weight * pl.reciprocal(1.0 + blue_factor * v, approx=True)
            halves.append((depth, before, red, green, blue))
        return tuple(halves)

    zero = jnp.zeros((2 * EDGE, lanes), jnp.float32)
    one = jnp.ones((2 * EDGE, lanes), jnp.float32)
    start = (zero, one, zero, zero, zero)
    state = lax.fori_loop(0, zblocks, block, (start, start), unroll=4)

    width = band * EDGE
    pick = lax.broadcasted_iota(jnp.int32, (2 * EDGE, width), 1)
    y_out = pick % EDGE
    place = pick // EDGE
    place = place % 2 * (lanes // 2) + place // 2
    outs = []
    for _, before, red, green, blue in state:
        opacity = 1.0 - before
        outs.append((opacity - red, green, blue, opacity))
    for ch in range(4):
        for b in range(strip):
            index = place + b * (band // 2)
            low = jnp.take_along_axis(outs[0][ch], index, axis=1)
            high = jnp.take_along_axis(outs[1][ch], index, axis=1)
            both = jnp.where(y_out < 2, low, high)
            first, second = both[:EDGE], both[EDGE:]
            use_first = (y_out[:EDGE] == 0) | (y_out[:EDGE] == 3)
            out_ref[ch, pl.ds(b * EDGE, EDGE), :] = jnp.where(use_first, first, second)


def per_device(coefficients, keep_count, view_flip):
    tiles = lax.axis_size("tile")
    depths = lax.axis_size("depth")
    slots, _, _, columns, rows = coefficients.shape
    strip = columns // tiles
    band = rows // depths
    zblocks = tiles * depths
    vmem = pl.BlockSpec(memory_space=pltpu.VMEM)
    smem = pl.BlockSpec(memory_space=pltpu.SMEM)
    lanes = strip * band
    outgoing = pl.pallas_call(
        lambda *refs: pack_kernel(*refs, tiles=tiles, depths=depths),
        out_shape=jax.ShapeDtypeStruct((zblocks, 5, 1, lanes), jnp.float32),
        in_specs=[vmem, vmem],
        out_specs=vmem,
        name="pack",
    )(coefficients.reshape(slots, columns, rows), keep_count.reshape(columns, rows))
    arrived = lax.all_to_all(outgoing, ("depth", "tile"), split_axis=0, concat_axis=0, tiled=True)
    return pl.pallas_call(
        lambda *refs: render_kernel(*refs, strip=strip, band=band, samples=EDGE * zblocks),
        out_shape=jax.ShapeDtypeStruct((4, strip * EDGE, band * EDGE), jnp.float32),
        in_specs=[smem, vmem],
        out_specs=vmem,
        scratch_shapes=[pltpu.VMEM((slots, zblocks, lanes), jnp.float32)],
        compiler_params=pltpu.CompilerParams(vmem_limit_bytes=8 * 1024 * 1024),
        name="render",
    )(view_flip, arrived)


def solution(mesh):
    placed = (P(None, "depth", "tile", None, None), P("depth", "tile", None, None), P("tile"))
    return jax.shard_map(
        per_device, mesh=mesh, in_specs=placed, out_specs=P(None, "tile", "depth"), check_vma=False
    )
```

```python
import math

import jax
import jax.numpy as jnp
from jax import lax
from jax.experimental import pallas as pl
from jax.experimental.pallas import tpu as pltpu
from jax.sharding import PartitionSpec as P

LOG2E = math.log2(math.e)
EDGE = 4


def cosine(frequency, position):
    factor = 0.5 if frequency == 0 else math.sqrt(0.5)
    return factor * math.cos(math.pi * (2 * position + 1) * frequency / 8.0)


def swap_halves(values):
    half = values.shape[1] // 2
    if values.shape[1] % 128 == 0:
        return pltpu.roll(values, half, 1)
    return jnp.concatenate([values[:, half:], values[:, :half]], axis=1)


def pack_kernel(coef_ref, keep_ref, *out_refs, tiles, depths):
    _, columns, rows = coef_ref.shape
    strip = columns // tiles
    band = rows // depths
    lane = lax.broadcasted_iota(jnp.int32, (tiles, rows), 1)
    even = lane % 2 == 0

    def take(values, index):
        return jnp.take_along_axis(values, index, axis=1)

    other = lane + 1 - 2 * (lane % 2)
    packed = []
    for b in range(strip):
        mine = pl.ds(b, tiles, stride=strip)
        keep = keep_ref[mine, :]
        slot = [coef_ref[k, mine, :] for k in range(8)]
        result = [slot[0]]
        for q in (1, 2, 3, 4):
            result.append(jnp.where(keep > q, slot[q], take(slot[8 - q], other)))
        result[4] = jnp.where(even, result[4], (9 - keep).astype(jnp.float32))
        packed.append(result)
    half = strip * band // 2
    parity = lane // half % 2
    column = lane // (band // 2) % strip
    source = lane % (band // 2) * 2 + parity
    me = lax.axis_index("depth")
    for m in range(depths):
        d = me ^ m
        for q in range(5):
            gathered = [take(packed[b][q], source + d * band) for b in range(strip)]
            merged = gathered[0]
            for b in range(1, strip):
                merged = jnp.where(column == b, gathered[b], merged)
            out_refs[m][:, q, 0, :] = merged[:, : 2 * half]


def chips_kernel(*refs, pairs):
    depths = len(refs) - pairs
    me = lax.axis_index("tile") // 2
    for n in range(pairs):
        for m in range(depths):
            refs[depths + n][m] = refs[m][pl.ds((me ^ n) * 2, 2)]


def cores_kernel(*refs):
    pairs = len(refs) - 2
    me = lax.axis_index("tile") % 2
    for n in range(pairs):
        for m in range(refs[n].shape[0]):
            for other in range(2):
                refs[pairs + other][n, m] = refs[n][m, me ^ other]


def unpack(packed_refs, coef_ref):
    pairs, depths, _, _, lanes = packed_refs[0].shape
    zblocks = pairs * depths
    first = lax.broadcasted_iota(jnp.int32, (zblocks, lanes), 1) < lanes // 2
    for other in range(2):
        row = [packed_refs[other][:, :, q, 0, :].reshape(zblocks, lanes) for q in range(5)]
        turned = [None] + [swap_halves(row[q]) for q in (1, 2, 3, 4)]
        keep = jnp.where(first, turned[4], 9.0 - row[4])
        slot = [row[0]] + [jnp.where(keep > q, row[q], 0.0) for q in (1, 2, 3)]
        slot.append(jnp.where(keep > 4, jnp.where(first, row[4], turned[4]), 0.0))
        slot += [jnp.where(keep > k, turned[8 - k], 0.0) for k in (5, 6, 7)]
        for k in range(8):
            coef_ref[k, pl.ds(other * zblocks, zblocks), :] = slot[k]


def render_kernel(flip_ref, own_ref, other_ref, out_ref, coef_ref, *, strip, band, samples):
    unpack((own_ref, other_ref), coef_ref)
    slots, zblocks, lanes = coef_ref.shape
    pairs, depths = own_ref.shape[:2]
    tile = lax.axis_index("tile")
    depth_index = lax.axis_index("depth")
    flipped = flip_ref[0] > 0
    sign = jnp.where(flipped, jnp.float32(-1.0), jnp.float32(1.0))
    b1 = [cosine(1, i) for i in range(EDGE)]
    row = lax.broadcasted_iota(jnp.int32, (2 * EDGE, lanes), 0)
    x = row % EDGE
    y = row // EDGE

    def table(position, values):
        result = jnp.full((2 * EDGE, lanes), values[0], jnp.float32)
        for i in range(1, len(values)):
            result = jnp.where(position == i, jnp.float32(values[i]), result)
        return result

    x1 = table(x, b1)
    x2 = table(x, [cosine(2, i) for i in range(EDGE)])
    y1 = table(y, b1[:2])
    y2 = table(y, [cosine(2, i) for i in range(2)])
    c_dc = 0.125 * LOG2E
    c_x1 = (0.25 * LOG2E) * x1
    c_x2 = (0.25 * LOG2E) * x2
    c_y1 = (0.25 * LOG2E) * y1
    c_y2 = (0.25 * LOG2E) * y2
    c_xy = (0.5 * LOG2E) * x1 * y1
    c_z = jnp.full((2 * EDGE, lanes), 0.25 * LOG2E * b1[0], jnp.float32) * sign
    c_zy = (0.5 * LOG2E * b1[0]) * y1 * sign
    ratio = b1[1] / b1[0]
    blue_factor = math.exp(-1.5)
    fade = -1.5 / samples

    def block(step, state):
        source = jnp.where(flipped, zblocks - 1 - step, step)
        t = (source % (2 * pairs)) ^ tile
        zb = ((t % 2) * pairs + t // 2) * depths + ((source // (2 * pairs)) ^ depth_index)
        a = [
            jnp.broadcast_to(coef_ref[k, pl.ds(zb, 1), :], (2 * EDGE, lanes)) for k in range(slots)
        ]
        even = a[0] * c_dc + a[2] * c_x1 + a[4] * c_y2 + a[6] * c_x2
        odd = a[1] * c_y1 + a[5] * c_xy
        g_even = a[3] * c_z
        g_odd = a[7] * c_zy
        halves = []
        for h in range(2):
            depth, before, red, green, blue = state[h]
            base = even + odd if h == 0 else even - odd
            g = g_even + g_odd if h == 0 else g_even - g_odd
            near = g * ratio
            for f in (base + g, base + near, base - near, base - g):
                v = jnp.exp2(f)
                one_u = 1.0 + v * v
                depth = depth + jnp.log2(one_u)
                after = jnp.exp2(fade * depth)
                weight = before - after
                before = after
                red = red + weight / one_u
                green = green + weight * jnp.exp2(f * (f * (-1.0 / LOG2E)))
                blue = blue + weight / (1.0 + blue_factor * v)
            halves.append((depth, before, red, green, blue))
        return tuple(halves)

    zero = jnp.zeros((2 * EDGE, lanes), jnp.float32)
    one = jnp.ones((2 * EDGE, lanes), jnp.float32)
    start = (zero, one, zero, zero, zero)
    state = lax.fori_loop(0, zblocks, block, (start, start), unroll=4)

    width = band * EDGE
    pick = lax.broadcasted_iota(jnp.int32, (2 * EDGE, width), 1)
    y_out = pick % EDGE
    place = pick // EDGE
    place = place % 2 * (lanes // 2) + place // 2
    outs = []
    for _, before, red, green, blue in state:
        opacity = 1.0 - before
        outs.append((opacity - red, green, blue, opacity))
    for ch in range(4):
        for b in range(strip):
            index = place + b * (band // 2)
            low = jnp.take_along_axis(outs[0][ch], index, axis=1)
            high = jnp.take_along_axis(outs[1][ch], index, axis=1)
            both = jnp.where(y_out < 2, low, high)
            first, second = both[:EDGE], both[EDGE:]
            use_first = (y_out[:EDGE] == 0) | (y_out[:EDGE] == 3)
            out_ref[ch, pl.ds(b * EDGE, EDGE), :] = jnp.where(use_first, first, second)


def per_device(coefficients, keep_count, view_flip):
    tiles = lax.axis_size("tile")
    depths = lax.axis_size("depth")
    slots, _, _, columns, rows = coefficients.shape
    strip = columns // tiles
    band = rows // depths
    zblocks = tiles * depths
    vmem = pl.BlockSpec(memory_space=pltpu.VMEM)
    smem = pl.BlockSpec(memory_space=pltpu.SMEM)
    lanes = strip * band
    params = pltpu.CompilerParams(vmem_limit_bytes=8 * 1024 * 1024)
    pairs = tiles // 2

    def shaped(*dims):
        return jax.ShapeDtypeStruct((*dims, 5, 1, lanes), jnp.float32)

    def partners(axis, change):
        return [(i, i ^ change) for i in range(lax.axis_size(axis))]

    def swap(values, axis, change):
        return lax.ppermute(values, axis, partners(axis, change))

    parts = pl.pallas_call(
        lambda *refs: pack_kernel(*refs, tiles=tiles, depths=depths),
        out_shape=[shaped(tiles)] * depths,
        in_specs=[vmem, vmem],
        out_specs=[vmem] * depths,
        compiler_params=params,
        name="pack",
    )(coefficients.reshape(slots, columns, rows), keep_count.reshape(columns, rows))
    parts = [parts[0]] + [swap(parts[m], "depth", m) for m in range(1, depths)]
    parts = pl.pallas_call(
        lambda *refs: chips_kernel(*refs, pairs=pairs),
        out_shape=[shaped(depths, 2)] * pairs,
        in_specs=[vmem] * depths,
        out_specs=[vmem] * pairs,
        compiler_params=params,
        name="chips",
    )(*parts)
    parts = [parts[0]] + [swap(parts[n], "tile", 2 * n) for n in range(1, pairs)]
    own, other = pl.pallas_call(
        cores_kernel,
        out_shape=[shaped(pairs, depths)] * 2,
        in_specs=[vmem] * pairs,
        out_specs=[vmem] * 2,
        compiler_params=params,
        name="cores",
    )(*parts)
    return pl.pallas_call(
        lambda *refs: render_kernel(*refs, strip=strip, band=band, samples=EDGE * zblocks),
        out_shape=jax.ShapeDtypeStruct((4, strip * EDGE, band * EDGE), jnp.float32),
        in_specs=[smem, vmem, vmem],
        out_specs=vmem,
        scratch_shapes=[pltpu.VMEM((slots, zblocks, lanes), jnp.float32)],
        compiler_params=params,
        name="render",
    )(view_flip, own, swap(other, "tile", 1))


def solution(mesh):
    placed = (P(None, "depth", "tile", None, None), P("depth", "tile", None, None), P("tile"))
    return jax.shard_map(
        per_device, mesh=mesh, in_specs=placed, out_specs=P(None, "tile", "depth"), check_vma=False
    )
```

```python
import math

import jax
import jax.numpy as jnp
from jax import lax
from jax.experimental import pallas as pl
from jax.experimental.pallas import tpu as pltpu
from jax.sharding import PartitionSpec as P

LOG2E = math.log2(math.e)
EDGE = 4


def cosine(frequency, position):
    factor = 0.5 if frequency == 0 else math.sqrt(0.5)
    return factor * math.cos(math.pi * (2 * position + 1) * frequency / 8.0)


def swap_halves(values):
    half = values.shape[1] // 2
    if values.shape[1] % 128 == 0:
        return pltpu.roll(values, half, 1)
    return jnp.concatenate([values[:, half:], values[:, :half]], axis=1)


def pack_kernel(flip_ref, coef_ref, keep_ref, out_ref, sign_ref, *, tiles, depths):
    _, columns, rows = coef_ref.shape
    strip = columns // tiles
    band = rows // depths
    lane = lax.broadcasted_iota(jnp.int32, (tiles, rows), 1)
    even = lane % 2 == 0

    def take(values, index):
        return jnp.take_along_axis(values, index, axis=1)

    other = lane + 1 - 2 * (lane % 2)
    packed = []
    for b in range(strip):
        mine = pl.ds(b, tiles, stride=strip)
        keep = keep_ref[mine, :]
        slot = [coef_ref[k, mine, :] for k in range(8)]
        result = [slot[0]]
        for q in (1, 2, 3, 4):
            result.append(jnp.where(keep > q, slot[q], take(slot[8 - q], other)))
        result[4] = jnp.where(even, result[4], (9 - keep).astype(jnp.float32))
        packed.append(result)
    sign_ref[...] = jnp.full(sign_ref.shape, 1 - 2 * flip_ref[0], jnp.int32).astype(jnp.float32)
    half = strip * band // 2
    parity = lane // half % 2
    column = lane // (band // 2) % strip
    source = lane % (band // 2) * 2 + parity
    for d in range(depths):
        for q in range(5):
            gathered = [take(packed[b][q], source + d * band) for b in range(strip)]
            merged = gathered[0]
            for b in range(1, strip):
                merged = jnp.where(column == b, gathered[b], merged)
            out_ref[pl.ds(d * tiles, tiles), q, 0, :] = merged[:, : 2 * half]


def unpack(packed_ref, coef_ref):
    zblocks, _, _, lanes = packed_ref.shape
    first = lax.broadcasted_iota(jnp.int32, (zblocks, lanes), 1) < lanes // 2
    row = [packed_ref[:, q, 0, :] for q in range(5)]
    turned = [None] + [swap_halves(row[q]) for q in (1, 2, 3, 4)]
    keep = jnp.where(first, turned[4], 9.0 - row[4])
    slot = [row[0]] + [jnp.where(keep > q, row[q], 0.0) for q in (1, 2, 3)]
    slot.append(jnp.where(keep > 4, jnp.where(first, row[4], turned[4]), 0.0))
    slot += [jnp.where(keep > k, turned[8 - k], 0.0) for k in (5, 6, 7)]
    for k in range(8):
        coef_ref[k] = slot[k]


def render_kernel(sign_ref, packed_ref, out_ref, coef_ref, *, strip, band, samples):
    unpack(packed_ref, coef_ref)
    slots, zblocks, lanes = coef_ref.shape
    sign = sign_ref[...]
    flipped = jnp.max(sign) < 0.0
    b1 = [cosine(1, i) for i in range(EDGE)]
    row = lax.broadcasted_iota(jnp.int32, (2 * EDGE, lanes), 0)
    x = row % EDGE
    y = row // EDGE

    def table(position, values):
        result = jnp.full((2 * EDGE, lanes), values[0], jnp.float32)
        for i in range(1, len(values)):
            result = jnp.where(position == i, jnp.float32(values[i]), result)
        return result

    x1 = table(x, b1)
    x2 = table(x, [cosine(2, i) for i in range(EDGE)])
    y1 = table(y, b1[:2])
    y2 = table(y, [cosine(2, i) for i in range(2)])
    c_dc = 0.125 * LOG2E
    c_x1 = (0.25 * LOG2E) * x1
    c_x2 = (0.25 * LOG2E) * x2
    c_y1 = (0.25 * LOG2E) * y1
    c_y2 = (0.25 * LOG2E) * y2
    c_xy = (0.5 * LOG2E) * x1 * y1
    c_z = jnp.full((2 * EDGE, lanes), 0.25 * LOG2E * b1[0], jnp.float32) * sign
    c_zy = (0.5 * LOG2E * b1[0]) * y1 * sign
    ratio = b1[1] / b1[0]
    blue_factor = math.exp(-1.5)
    fade = -1.5 / samples

    def block(step, state):
        zb = jnp.where(flipped, zblocks - 1 - step, step)
        a = [
            jnp.broadcast_to(coef_ref[k, pl.ds(zb, 1), :], (2 * EDGE, lanes)) for k in range(slots)
        ]
        even = a[0] * c_dc + a[2] * c_x1 + a[4] * c_y2 + a[6] * c_x2
        odd = a[1] * c_y1 + a[5] * c_xy
        g_even = a[3] * c_z
        g_odd = a[7] * c_zy
        halves = []
        for h in range(2):
            depth, before, red, green, blue = state[h]
            base = even + odd if h == 0 else even - odd
            g = g_even + g_odd if h == 0 else g_even - g_odd
            near = g * ratio
            for f in (base + g, base + near, base - near, base - g):
                v = jnp.exp2(f)
                one_u = 1.0 + v * v
                depth = depth + jnp.log2(one_u)
                after = jnp.exp2(fade * depth)
                weight = before - after
                before = after
                red = red + weight / one_u
                green = green + weight * jnp.exp2(f * (f * (-1.0 / LOG2E)))
                blue = blue + weight / (1.0 + blue_factor * v)
            halves.append((depth, before, red, green, blue))
        return tuple(halves)

    zero = jnp.zeros((2 * EDGE, lanes), jnp.float32)
    one = jnp.ones((2 * EDGE, lanes), jnp.float32)
    start = (zero, one, zero, zero, zero)
    state = lax.fori_loop(0, zblocks, block, (start, start), unroll=4)

    width = band * EDGE
    pick = lax.broadcasted_iota(jnp.int32, (2 * EDGE, width), 1)
    y_out = pick % EDGE
    place = pick // EDGE
    place = place % 2 * (lanes // 2) + place // 2
    outs = []
    for _, before, red, green, blue in state:
        opacity = 1.0 - before
        outs.append((opacity - red, green, blue, opacity))
    for ch in range(4):
        for b in range(strip):
            index = place + b * (band // 2)
            low = jnp.take_along_axis(outs[0][ch], index, axis=1)
            high = jnp.take_along_axis(outs[1][ch], index, axis=1)
            both = jnp.where(y_out < 2, low, high)
            first, second = both[:EDGE], both[EDGE:]
            use_first = (y_out[:EDGE] == 0) | (y_out[:EDGE] == 3)
            out_ref[ch, pl.ds(b * EDGE, EDGE), :] = jnp.where(use_first, first, second)


def per_device(coefficients, keep_count, view_flip):
    tiles = lax.axis_size("tile")
    depths = lax.axis_size("depth")
    slots, _, _, columns, rows = coefficients.shape
    strip = columns // tiles
    band = rows // depths
    zblocks = tiles * depths
    vmem = pl.BlockSpec(memory_space=pltpu.VMEM)
    params = pltpu.CompilerParams(vmem_limit_bytes=8 * 1024 * 1024)
    lanes = strip * band
    outgoing, sign = pl.pallas_call(
        lambda *refs: pack_kernel(*refs, tiles=tiles, depths=depths),
        out_shape=[
            jax.ShapeDtypeStruct((zblocks, 5, 1, lanes), jnp.float32),
            jax.ShapeDtypeStruct((2 * EDGE, lanes), jnp.float32),
        ],
        in_specs=[pl.BlockSpec(memory_space=pltpu.SMEM), vmem, vmem],
        out_specs=[vmem, vmem],
        compiler_params=params,
        name="pack",
    )(view_flip, coefficients.reshape(slots, columns, rows), keep_count.reshape(columns, rows))
    arrived = lax.all_to_all(outgoing, ("depth", "tile"), split_axis=0, concat_axis=0, tiled=True)
    return pl.pallas_call(
        lambda *refs: render_kernel(*refs, strip=strip, band=band, samples=EDGE * zblocks),
        out_shape=jax.ShapeDtypeStruct((4, strip * EDGE, band * EDGE), jnp.float32),
        in_specs=[vmem, vmem],
        out_specs=vmem,
        scratch_shapes=[pltpu.VMEM((slots, zblocks, lanes), jnp.float32)],
        compiler_params=params,
        name="render",
    )(sign, arrived)


def solution(mesh):
    placed = (P(None, "depth", "tile", None, None), P("depth", "tile", None, None), P("tile"))
    return jax.shard_map(
        per_device, mesh=mesh, in_specs=placed, out_specs=P(None, "tile", "depth"), check_vma=False
    )
```

```python
import math

import jax
import jax.numpy as jnp
from jax import lax
from jax.experimental import pallas as pl
from jax.experimental.pallas import tpu as pltpu
from jax.sharding import PartitionSpec as P

LOG2E = math.log2(math.e)
EDGE = 4


def cosine(frequency, position):
    factor = 0.5 if frequency == 0 else math.sqrt(0.5)
    return factor * math.cos(math.pi * (2 * position + 1) * frequency / 8.0)


def swap_halves(values):
    half = values.shape[1] // 2
    if values.shape[1] % 128 == 0:
        return pltpu.roll(values, half, 1)
    return jnp.concatenate([values[:, half:], values[:, :half]], axis=1)


def pack_kernel(coef_hbm, keep_hbm, out_ref, coef_ref, keep_ref, arrival, *, tiles, depths):
    _, columns, rows = coef_ref.shape
    strip = columns // tiles
    band = rows // depths
    moves = ((coef_hbm, coef_ref), (keep_hbm, keep_ref))
    fetches = [pltpu.make_async_copy(a, b, arrival.at[i]) for i, (a, b) in enumerate(moves)]
    for fetch in fetches:
        fetch.start()
    for fetch in fetches:
        fetch.wait()
    lane = lax.broadcasted_iota(jnp.int32, (tiles, rows), 1)
    even = lane % 2 == 0

    def take(values, index):
        return jnp.take_along_axis(values, index, axis=1)

    other = lane + 1 - 2 * (lane % 2)
    packed = []
    for b in range(strip):
        mine = pl.ds(b, tiles, stride=strip)
        keep = keep_ref[mine, :]
        slot = [coef_ref[k, mine, :] for k in range(8)]
        result = [slot[0]]
        for q in (1, 2, 3, 4):
            result.append(jnp.where(keep > q, slot[q], take(slot[8 - q], other)))
        result[4] = jnp.where(even, result[4], (9 - keep).astype(jnp.float32))
        packed.append(result)
    half = strip * band // 2
    parity = lane // half % 2
    column = lane // (band // 2) % strip
    source = lane % (band // 2) * 2 + parity
    for d in range(depths):
        for q in range(5):
            gathered = [take(packed[b][q], source + d * band) for b in range(strip)]
            merged = gathered[0]
            for b in range(1, strip):
                merged = jnp.where(column == b, gathered[b], merged)
            out_ref[pl.ds(d * tiles, tiles), q, 0, :] = merged[:, : 2 * half]


def unpack(packed_ref, coef_ref):
    zblocks, _, _, lanes = packed_ref.shape
    first = lax.broadcasted_iota(jnp.int32, (zblocks, lanes), 1) < lanes // 2
    row = [packed_ref[:, q, 0, :] for q in range(5)]
    turned = [None] + [swap_halves(row[q]) for q in (1, 2, 3, 4)]
    keep = jnp.where(first, turned[4], 9.0 - row[4])
    slot = [row[0]] + [jnp.where(keep > q, row[q], 0.0) for q in (1, 2, 3)]
    slot.append(jnp.where(keep > 4, jnp.where(first, row[4], turned[4]), 0.0))
    slot += [jnp.where(keep > k, turned[8 - k], 0.0) for k in (5, 6, 7)]
    for k in range(8):
        coef_ref[k] = slot[k]


def render_kernel(flip_ref, packed_ref, out_ref, coef_ref, *, strip, band, samples):
    unpack(packed_ref, coef_ref)
    slots, zblocks, lanes = coef_ref.shape
    flipped = flip_ref[0] > 0
    sign = jnp.where(flipped, jnp.float32(-1.0), jnp.float32(1.0))
    b1 = [cosine(1, i) for i in range(EDGE)]
    row = lax.broadcasted_iota(jnp.int32, (2 * EDGE, lanes), 0)
    x = row % EDGE
    y = row // EDGE

    def table(position, values):
        result = jnp.full((2 * EDGE, lanes), values[0], jnp.float32)
        for i in range(1, len(values)):
            result = jnp.where(position == i, jnp.float32(values[i]), result)
        return result

    x1 = table(x, b1)
    x2 = table(x, [cosine(2, i) for i in range(EDGE)])
    y1 = table(y, b1[:2])
    y2 = table(y, [cosine(2, i) for i in range(2)])
    c_dc = 0.125 * LOG2E
    c_x1 = (0.25 * LOG2E) * x1
    c_x2 = (0.25 * LOG2E) * x2
    c_y1 = (0.25 * LOG2E) * y1
    c_y2 = (0.25 * LOG2E) * y2
    c_xy = (0.5 * LOG2E) * x1 * y1
    c_z = jnp.full((2 * EDGE, lanes), 0.25 * LOG2E * b1[0], jnp.float32) * sign
    c_zy = (0.5 * LOG2E * b1[0]) * y1 * sign
    ratio = b1[1] / b1[0]
    blue_factor = math.exp(-1.5)
    fade = -1.5 / samples

    def block(step, state):
        zb = jnp.where(flipped, zblocks - 1 - step, step)
        a = [
            jnp.broadcast_to(coef_ref[k, pl.ds(zb, 1), :], (2 * EDGE, lanes)) for k in range(slots)
        ]
        even = a[0] * c_dc + a[2] * c_x1 + a[4] * c_y2 + a[6] * c_x2
        odd = a[1] * c_y1 + a[5] * c_xy
        g_even = a[3] * c_z
        g_odd = a[7] * c_zy
        halves = []
        for h in range(2):
            depth, before, red, green, blue = state[h]
            base = even + odd if h == 0 else even - odd
            g = g_even + g_odd if h == 0 else g_even - g_odd
            near = g * ratio
            for f in (base + g, base + near, base - near, base - g):
                v = jnp.exp2(f)
                one_u = 1.0 + v * v
                depth = depth + jnp.log2(one_u)
                after = jnp.exp2(fade * depth)
                weight = before - after
                before = after
                red = red + weight / one_u
                green = green + weight * jnp.exp2(f * (f * (-1.0 / LOG2E)))
                blue = blue + weight / (1.0 + blue_factor * v)
            halves.append((depth, before, red, green, blue))
        return tuple(halves)

    zero = jnp.zeros((2 * EDGE, lanes), jnp.float32)
    one = jnp.ones((2 * EDGE, lanes), jnp.float32)
    start = (zero, one, zero, zero, zero)
    state = lax.fori_loop(0, zblocks, block, (start, start), unroll=4)

    width = band * EDGE
    pick = lax.broadcasted_iota(jnp.int32, (2 * EDGE, width), 1)
    y_out = pick % EDGE
    place = pick // EDGE
    place = place % 2 * (lanes // 2) + place // 2
    outs = []
    for _, before, red, green, blue in state:
        opacity = 1.0 - before
        outs.append((opacity - red, green, blue, opacity))
    for ch in range(4):
        for b in range(strip):
            index = place + b * (band // 2)
            low = jnp.take_along_axis(outs[0][ch], index, axis=1)
            high = jnp.take_along_axis(outs[1][ch], index, axis=1)
            both = jnp.where(y_out < 2, low, high)
            first, second = both[:EDGE], both[EDGE:]
            use_first = (y_out[:EDGE] == 0) | (y_out[:EDGE] == 3)
            out_ref[ch, pl.ds(b * EDGE, EDGE), :] = jnp.where(use_first, first, second)


def per_device(coefficients, keep_count, view_flip):
    tiles = lax.axis_size("tile")
    depths = lax.axis_size("depth")
    slots, _, _, columns, rows = coefficients.shape
    strip = columns // tiles
    band = rows // depths
    zblocks = tiles * depths
    vmem = pl.BlockSpec(memory_space=pltpu.VMEM)
    params = pltpu.CompilerParams(vmem_limit_bytes=8 * 1024 * 1024)
    lanes = strip * band
    inputs = (coefficients.reshape(slots, columns, rows), keep_count.reshape(columns, rows))
    outgoing = pl.pallas_call(
        lambda *refs: pack_kernel(*refs, tiles=tiles, depths=depths),
        out_shape=pltpu.VMEM((zblocks, 5, 1, lanes), jnp.float32),
        in_specs=[pl.BlockSpec(memory_space=pltpu.HBM)] * 2,
        out_specs=vmem,
        scratch_shapes=[
            pltpu.VMEM((slots, columns, rows), jnp.float32),
            pltpu.VMEM((columns, rows), jnp.int32),
            pltpu.SemaphoreType.DMA((2,)),
        ],
        compiler_params=params,
        name="pack",
    )(*(pltpu.with_memory_space_constraint(x, pltpu.HBM) for x in inputs))
    arrived = lax.all_to_all(outgoing, ("depth", "tile"), split_axis=0, concat_axis=0, tiled=True)
    return pl.pallas_call(
        lambda *refs: render_kernel(*refs, strip=strip, band=band, samples=EDGE * zblocks),
        out_shape=jax.ShapeDtypeStruct((4, strip * EDGE, band * EDGE), jnp.float32),
        in_specs=[pl.BlockSpec(memory_space=pltpu.SMEM), vmem],
        out_specs=vmem,
        scratch_shapes=[pltpu.VMEM((slots, zblocks, lanes), jnp.float32)],
        compiler_params=params,
        name="render",
    )(view_flip, arrived)


def solution(mesh):
    placed = (P(None, "depth", "tile", None, None), P("depth", "tile", None, None), P("tile"))
    return jax.shard_map(
        per_device, mesh=mesh, in_specs=placed, out_specs=P(None, "tile", "depth"), check_vma=False
    )
```

```python
import math

import jax
import jax.numpy as jnp
from jax import lax
from jax.experimental import pallas as pl
from jax.experimental.pallas import tpu as pltpu
from jax.sharding import PartitionSpec as P

LOG2E = math.log2(math.e)
EDGE = 4


def cosine(frequency, position):
    factor = 0.5 if frequency == 0 else math.sqrt(0.5)
    return factor * math.cos(math.pi * (2 * position + 1) * frequency / 8.0)


def swap_halves(values):
    half = values.shape[1] // 2
    if values.shape[1] % 128 == 0:
        return pltpu.roll(values, half, 1)
    return jnp.concatenate([values[:, half:], values[:, :half]], axis=1)


def pack_kernel(coef_hbm, keep_hbm, out_ref, coef_ref, keep_ref, rows_ref, arrival, *, tiles, depths):
    _, columns, rows = coef_ref.shape
    strip = columns // tiles
    band = rows // depths
    moves = ((coef_hbm, coef_ref), (keep_hbm, keep_ref))
    fetches = [pltpu.make_async_copy(a, b, arrival.at[i]) for i, (a, b) in enumerate(moves)]
    for fetch in fetches:
        fetch.start()
    for fetch in fetches:
        fetch.wait()
    lane = lax.broadcasted_iota(jnp.int32, (tiles, rows), 1)
    even = lane % 2 == 0

    def take(values, index):
        return jnp.take_along_axis(values, index, axis=1)

    other = lane + 1 - 2 * (lane % 2)
    packed = []
    for b in range(strip):
        mine = pl.ds(b, tiles, stride=strip)
        keep = keep_ref[mine, :]
        slot = [coef_ref[k, mine, :] for k in range(8)]
        result = [slot[0]]
        for q in (1, 2, 3, 4):
            result.append(jnp.where(keep > q, slot[q], take(slot[8 - q], other)))
        result[4] = jnp.where(even, result[4], (9 - keep).astype(jnp.float32))
        packed.append(result)
    half = strip * band // 2
    parity = lane // half % 2
    column = lane // (band // 2) % strip
    source = lane % (band // 2) * 2 + parity
    chips = tiles // 2
    core = lax.axis_index("tile") % 2
    for d in range(depths):
        for q in range(5):
            gathered = [take(packed[b][q], source + d * band) for b in range(strip)]
            merged = gathered[0]
            for b in range(1, strip):
                merged = jnp.where(column == b, gathered[b], merged)
            rows_ref[d, q] = merged[:, : 2 * half]
    for d in range(depths):
        for q in range(5):
            for other in range(2):
                chosen = rows_ref[d, q, pl.ds(core ^ other, chips, stride=2), :]
                out_ref[pl.ds(d * chips, chips), other, q, 0, :] = chosen


def cores_kernel(both_ref, own_ref, other_ref):
    own_ref[...] = both_ref[:, 0]
    other_ref[...] = both_ref[:, 1]


def unpack(packed_ref, coef_ref, start):
    zblocks, _, _, lanes = packed_ref.shape
    first = lax.broadcasted_iota(jnp.int32, (zblocks, lanes), 1) < lanes // 2
    row = [packed_ref[:, q, 0, :] for q in range(5)]
    turned = [None] + [swap_halves(row[q]) for q in (1, 2, 3, 4)]
    keep = jnp.where(first, turned[4], 9.0 - row[4])
    slot = [row[0]] + [jnp.where(keep > q, row[q], 0.0) for q in (1, 2, 3)]
    slot.append(jnp.where(keep > 4, jnp.where(first, row[4], turned[4]), 0.0))
    slot += [jnp.where(keep > k, turned[8 - k], 0.0) for k in (5, 6, 7)]
    for k in range(8):
        coef_ref[k, pl.ds(start, zblocks), :] = slot[k]


def render_kernel(flip_ref, own_ref, other_ref, out_ref, coef_ref, *, strip, band, samples):
    unpack(own_ref, coef_ref, 0)
    unpack(other_ref, coef_ref, other_ref.shape[0])
    core = lax.axis_index("tile") % 2
    slots, zblocks, lanes = coef_ref.shape
    flipped = flip_ref[0] > 0
    sign = jnp.where(flipped, jnp.float32(-1.0), jnp.float32(1.0))
    b1 = [cosine(1, i) for i in range(EDGE)]
    row = lax.broadcasted_iota(jnp.int32, (2 * EDGE, lanes), 0)
    x = row % EDGE
    y = row // EDGE

    def table(position, values):
        result = jnp.full((2 * EDGE, lanes), values[0], jnp.float32)
        for i in range(1, len(values)):
            result = jnp.where(position == i, jnp.float32(values[i]), result)
        return result

    x1 = table(x, b1)
    x2 = table(x, [cosine(2, i) for i in range(EDGE)])
    y1 = table(y, b1[:2])
    y2 = table(y, [cosine(2, i) for i in range(2)])
    c_dc = 0.125 * LOG2E
    c_x1 = (0.25 * LOG2E) * x1
    c_x2 = (0.25 * LOG2E) * x2
    c_y1 = (0.25 * LOG2E) * y1
    c_y2 = (0.25 * LOG2E) * y2
    c_xy = (0.5 * LOG2E) * x1 * y1
    c_z = jnp.full((2 * EDGE, lanes), 0.25 * LOG2E * b1[0], jnp.float32) * sign
    c_zy = (0.5 * LOG2E * b1[0]) * y1 * sign
    ratio = b1[1] / b1[0]
    blue_factor = math.exp(-1.5)
    fade = -1.5 / samples

    def block(step, state):
        source = jnp.where(flipped, zblocks - 1 - step, step)
        zb = (source % 2 ^ core) * (zblocks // 2) + source // 2
        a = [
            jnp.broadcast_to(coef_ref[k, pl.ds(zb, 1), :], (2 * EDGE, lanes)) for k in range(slots)
        ]
        even = a[0] * c_dc + a[2] * c_x1 + a[4] * c_y2 + a[6] * c_x2
        odd = a[1] * c_y1 + a[5] * c_xy
        g_even = a[3] * c_z
        g_odd = a[7] * c_zy
        halves = []
        for h in range(2):
            depth, before, red, green, blue = state[h]
            base = even + odd if h == 0 else even - odd
            g = g_even + g_odd if h == 0 else g_even - g_odd
            near = g * ratio
            for f in (base + g, base + near, base - near, base - g):
                v = jnp.exp2(f)
                one_u = 1.0 + v * v
                depth = depth + jnp.log2(one_u)
                after = jnp.exp2(fade * depth)
                weight = before - after
                before = after
                red = red + weight / one_u
                green = green + weight * jnp.exp2(f * (f * (-1.0 / LOG2E)))
                blue = blue + weight / (1.0 + blue_factor * v)
            halves.append((depth, before, red, green, blue))
        return tuple(halves)

    zero = jnp.zeros((2 * EDGE, lanes), jnp.float32)
    one = jnp.ones((2 * EDGE, lanes), jnp.float32)
    start = (zero, one, zero, zero, zero)
    state = lax.fori_loop(0, zblocks, block, (start, start), unroll=4)

    width = band * EDGE
    pick = lax.broadcasted_iota(jnp.int32, (2 * EDGE, width), 1)
    y_out = pick % EDGE
    place = pick // EDGE
    place = place % 2 * (lanes // 2) + place // 2
    outs = []
    for _, before, red, green, blue in state:
        opacity = 1.0 - before
        outs.append((opacity - red, green, blue, opacity))
    for ch in range(4):
        for b in range(strip):
            index = place + b * (band // 2)
            low = jnp.take_along_axis(outs[0][ch], index, axis=1)
            high = jnp.take_along_axis(outs[1][ch], index, axis=1)
            both = jnp.where(y_out < 2, low, high)
            first, second = both[:EDGE], both[EDGE:]
            use_first = (y_out[:EDGE] == 0) | (y_out[:EDGE] == 3)
            out_ref[ch, pl.ds(b * EDGE, EDGE), :] = jnp.where(use_first, first, second)


def per_device(coefficients, keep_count, view_flip):
    tiles = lax.axis_size("tile")
    depths = lax.axis_size("depth")
    slots, _, _, columns, rows = coefficients.shape
    strip = columns // tiles
    band = rows // depths
    zblocks = tiles * depths
    vmem = pl.BlockSpec(memory_space=pltpu.VMEM)
    params = pltpu.CompilerParams(vmem_limit_bytes=8 * 1024 * 1024)
    lanes = strip * band
    chips = zblocks // 2
    same_core = [[2 * chip + core for chip in range(chips)] for core in range(2)]
    inputs = (coefficients.reshape(slots, columns, rows), keep_count.reshape(columns, rows))
    outgoing = pl.pallas_call(
        lambda *refs: pack_kernel(*refs, tiles=tiles, depths=depths),
        out_shape=jax.ShapeDtypeStruct((chips, 2, 5, 1, lanes), jnp.float32),
        in_specs=[pl.BlockSpec(memory_space=pltpu.HBM)] * 2,
        out_specs=vmem,
        scratch_shapes=[
            pltpu.VMEM((slots, columns, rows), jnp.float32),
            pltpu.VMEM((columns, rows), jnp.int32),
            pltpu.VMEM((depths, 5, tiles, lanes), jnp.float32),
            pltpu.SemaphoreType.DMA((2,)),
        ],
        compiler_params=params,
        name="pack",
    )(*(pltpu.with_memory_space_constraint(x, pltpu.HBM) for x in inputs))
    arrived = lax.all_to_all(
        outgoing, ("depth", "tile"), split_axis=0, concat_axis=0, tiled=True, axis_index_groups=same_core
    )
    own, other = pl.pallas_call(
        cores_kernel,
        out_shape=[jax.ShapeDtypeStruct((chips, 5, 1, lanes), jnp.float32)] * 2,
        in_specs=[vmem],
        out_specs=[vmem, vmem],
        compiler_params=params,
        name="cores",
    )(arrived)
    other = lax.ppermute(other, "tile", [(t, t ^ 1) for t in range(tiles)])
    return pl.pallas_call(
        lambda *refs: render_kernel(*refs, strip=strip, band=band, samples=EDGE * zblocks),
        out_shape=jax.ShapeDtypeStruct((4, strip * EDGE, band * EDGE), jnp.float32),
        in_specs=[pl.BlockSpec(memory_space=pltpu.SMEM), vmem, vmem],
        out_specs=vmem,
        scratch_shapes=[pltpu.VMEM((slots, zblocks, lanes), jnp.float32)],
        compiler_params=params,
        name="render",
    )(view_flip, own, other)


def solution(mesh):
    placed = (P(None, "depth", "tile", None, None), P("depth", "tile", None, None), P("tile"))
    return jax.shard_map(
        per_device, mesh=mesh, in_specs=placed, out_specs=P(None, "tile", "depth"), check_vma=False
    )
```

```python
import math

import jax
import jax.numpy as jnp
from jax import lax
from jax.experimental import pallas as pl
from jax.experimental.pallas import tpu as pltpu
from jax.sharding import PartitionSpec as P

LOG2E = math.log2(math.e)
EDGE = 4


def cosine(frequency, position):
    factor = 0.5 if frequency == 0 else math.sqrt(0.5)
    return factor * math.cos(math.pi * (2 * position + 1) * frequency / 8.0)


def swap_halves(values):
    half = values.shape[1] // 2
    if values.shape[1] % 128 == 0:
        return pltpu.roll(values, half, 1)
    return jnp.concatenate([values[:, half:], values[:, :half]], axis=1)


def pack_kernel(
    flip_ref, coef_hbm, keep_hbm, out_ref, sign_ref, coef_ref, keep_ref, arrival, *, tiles, depths
):
    _, columns, rows = coef_ref.shape
    strip = columns // tiles
    band = rows // depths
    moves = ((coef_hbm, coef_ref), (keep_hbm, keep_ref))
    fetches = [pltpu.make_async_copy(a, b, arrival.at[i]) for i, (a, b) in enumerate(moves)]
    for fetch in fetches:
        fetch.start()
    for fetch in fetches:
        fetch.wait()
    lane = lax.broadcasted_iota(jnp.int32, (tiles, rows), 1)
    even = lane % 2 == 0

    def take(values, index):
        return jnp.take_along_axis(values, index, axis=1)

    other = lane + 1 - 2 * (lane % 2)
    packed = []
    for b in range(strip):
        mine = pl.ds(b, tiles, stride=strip)
        keep = keep_ref[mine, :]
        slot = [coef_ref[k, mine, :] for k in range(8)]
        result = [slot[0]]
        for q in (1, 2, 3, 4):
            result.append(jnp.where(keep > q, slot[q], take(slot[8 - q], other)))
        result[4] = jnp.where(even, result[4], (9 - keep).astype(jnp.float32))
        packed.append(result)
    sign_ref[...] = jnp.full(sign_ref.shape, 1 - 2 * flip_ref[0], jnp.int32).astype(jnp.float32)
    half = strip * band // 2
    parity = lane // half % 2
    column = lane // (band // 2) % strip
    source = lane % (band // 2) * 2 + parity
    for d in range(depths):
        for q in range(5):
            gathered = [take(packed[b][q], source + d * band) for b in range(strip)]
            merged = gathered[0]
            for b in range(1, strip):
                merged = jnp.where(column == b, gathered[b], merged)
            out_ref[:, d, q, 0, :] = merged[:, : 2 * half]


def unpack(packed_ref, coef_ref):
    tiles, depths, _, _, lanes = packed_ref.shape
    zblocks = tiles * depths
    first = lax.broadcasted_iota(jnp.int32, (zblocks, lanes), 1) < lanes // 2
    row = [packed_ref[:, :, q, 0, :].reshape(zblocks, lanes) for q in range(5)]
    turned = [None] + [swap_halves(row[q]) for q in (1, 2, 3, 4)]
    keep = jnp.where(first, turned[4], 9.0 - row[4])
    slot = [row[0]] + [jnp.where(keep > q, row[q], 0.0) for q in (1, 2, 3)]
    slot.append(jnp.where(keep > 4, jnp.where(first, row[4], turned[4]), 0.0))
    slot += [jnp.where(keep > k, turned[8 - k], 0.0) for k in (5, 6, 7)]
    for k in range(8):
        coef_ref[k] = slot[k]


def render_kernel(sign_ref, packed_ref, out_ref, coef_ref, *, strip, band, samples):
    unpack(packed_ref, coef_ref)
    slots, zblocks, lanes = coef_ref.shape
    tiles, depths = packed_ref.shape[:2]
    sign = sign_ref[...]
    flipped = jnp.max(sign) < 0.0
    b1 = [cosine(1, i) for i in range(EDGE)]
    row = lax.broadcasted_iota(jnp.int32, (2 * EDGE, lanes), 0)
    x = row % EDGE
    y = row // EDGE

    def table(position, values):
        result = jnp.full((2 * EDGE, lanes), values[0], jnp.float32)
        for i in range(1, len(values)):
            result = jnp.where(position == i, jnp.float32(values[i]), result)
        return result

    x1 = table(x, b1)
    x2 = table(x, [cosine(2, i) for i in range(EDGE)])
    y1 = table(y, b1[:2])
    y2 = table(y, [cosine(2, i) for i in range(2)])
    c_dc = 0.125 * LOG2E
    c_x1 = (0.25 * LOG2E) * x1
    c_x2 = (0.25 * LOG2E) * x2
    c_y1 = (0.25 * LOG2E) * y1
    c_y2 = (0.25 * LOG2E) * y2
    c_xy = (0.5 * LOG2E) * x1 * y1
    c_z = jnp.full((2 * EDGE, lanes), 0.25 * LOG2E * b1[0], jnp.float32) * sign
    c_zy = (0.5 * LOG2E * b1[0]) * y1 * sign
    ratio = b1[1] / b1[0]
    blue_factor = math.exp(-1.5)
    fade = -1.5 / samples

    def block(step, state):
        source = jnp.where(flipped, zblocks - 1 - step, step)
        zb = source % tiles * depths + source // tiles
        a = [
            jnp.broadcast_to(coef_ref[k, pl.ds(zb, 1), :], (2 * EDGE, lanes)) for k in range(slots)
        ]
        even = a[0] * c_dc + a[2] * c_x1 + a[4] * c_y2 + a[6] * c_x2
        odd = a[1] * c_y1 + a[5] * c_xy
        g_even = a[3] * c_z
        g_odd = a[7] * c_zy
        halves = []
        for h in range(2):
            depth, before, red, green, blue = state[h]
            base = even + odd if h == 0 else even - odd
            g = g_even + g_odd if h == 0 else g_even - g_odd
            near = g * ratio
            for f in (base + g, base + near, base - near, base - g):
                v = jnp.exp2(f)
                one_u = 1.0 + v * v
                depth = depth + jnp.log2(one_u)
                after = jnp.exp2(fade * depth)
                weight = before - after
                before = after
                red = red + weight / one_u
                green = green + weight * jnp.exp2(f * (f * (-1.0 / LOG2E)))
                blue = blue + weight / (1.0 + blue_factor * v)
            halves.append((depth, before, red, green, blue))
        return tuple(halves)

    zero = jnp.zeros((2 * EDGE, lanes), jnp.float32)
    one = jnp.ones((2 * EDGE, lanes), jnp.float32)
    start = (zero, one, zero, zero, zero)
    state = lax.fori_loop(0, zblocks, block, (start, start), unroll=4)

    width = band * EDGE
    pick = lax.broadcasted_iota(jnp.int32, (2 * EDGE, width), 1)
    y_out = pick % EDGE
    place = pick // EDGE
    place = place % 2 * (lanes // 2) + place // 2
    outs = []
    for _, before, red, green, blue in state:
        opacity = 1.0 - before
        outs.append((opacity - red, green, blue, opacity))
    for ch in range(4):
        for b in range(strip):
            index = place + b * (band // 2)
            low = jnp.take_along_axis(outs[0][ch], index, axis=1)
            high = jnp.take_along_axis(outs[1][ch], index, axis=1)
            both = jnp.where(y_out < 2, low, high)
            first, second = both[:EDGE], both[EDGE:]
            use_first = (y_out[:EDGE] == 0) | (y_out[:EDGE] == 3)
            out_ref[ch, pl.ds(b * EDGE, EDGE), :] = jnp.where(use_first, first, second)


def per_device(coefficients, keep_count, view_flip):
    tiles = lax.axis_size("tile")
    depths = lax.axis_size("depth")
    slots, _, _, columns, rows = coefficients.shape
    strip = columns // tiles
    band = rows // depths
    zblocks = tiles * depths
    vmem = pl.BlockSpec(memory_space=pltpu.VMEM)
    params = pltpu.CompilerParams(vmem_limit_bytes=8 * 1024 * 1024)
    lanes = strip * band
    inputs = (coefficients.reshape(slots, columns, rows), keep_count.reshape(columns, rows))
    outgoing, sign = pl.pallas_call(
        lambda *refs: pack_kernel(*refs, tiles=tiles, depths=depths),
        out_shape=[
            jax.ShapeDtypeStruct((tiles, depths, 5, 1, lanes), jnp.float32),
            jax.ShapeDtypeStruct((2 * EDGE, lanes), jnp.float32),
        ],
        in_specs=[pl.BlockSpec(memory_space=pltpu.SMEM)] + [pl.BlockSpec(memory_space=pltpu.HBM)] * 2,
        out_specs=[vmem, vmem],
        scratch_shapes=[
            pltpu.VMEM((slots, columns, rows), jnp.float32),
            pltpu.VMEM((columns, rows), jnp.int32),
            pltpu.SemaphoreType.DMA((2,)),
        ],
        compiler_params=params,
        name="pack",
    )(view_flip, *(pltpu.with_memory_space_constraint(x, pltpu.HBM) for x in inputs))
    sent = outgoing.reshape(zblocks, 5, 1, lanes)
    arrived = lax.all_to_all(sent, ("tile", "depth"), split_axis=0, concat_axis=0, tiled=True)
    return pl.pallas_call(
        lambda *refs: render_kernel(*refs, strip=strip, band=band, samples=EDGE * zblocks),
        out_shape=jax.ShapeDtypeStruct((4, strip * EDGE, band * EDGE), jnp.float32),
        in_specs=[vmem, vmem],
        out_specs=vmem,
        scratch_shapes=[pltpu.VMEM((slots, zblocks, lanes), jnp.float32)],
        compiler_params=params,
        name="render",
    )(sign, arrived.reshape(outgoing.shape))


def solution(mesh):
    placed = (P(None, "depth", "tile", None, None), P("depth", "tile", None, None), P("tile"))
    return jax.shard_map(
        per_device, mesh=mesh, in_specs=placed, out_specs=P(None, "tile", "depth"), check_vma=False
    )
```

```python
import functools
import math

import jax
import jax.numpy as jnp
from jax import lax
from jax.experimental import pallas as pl
from jax.experimental.pallas import tpu as pltpu
from jax.sharding import PartitionSpec as P

LOG2E = math.log2(math.e)
EDGE = 4


def cosine(frequency, position):
    factor = 0.5 if frequency == 0 else math.sqrt(0.5)
    return factor * math.cos(math.pi * (2 * position + 1) * frequency / 8.0)


def swap_halves(values):
    half = values.shape[1] // 2
    if values.shape[1] % 128 == 0:
        return pltpu.roll(values, half, 1)
    return jnp.concatenate([values[:, half:], values[:, :half]], axis=1)


def pack_kernel(
    coef_hbm, keep_hbm, stay_ref, send_ref, coef_ref, keep_ref, rows_ref, arrival, *, tiles, depths, bit
):
    _, columns, rows = coef_ref.shape
    strip = columns // tiles
    band = rows // depths
    moves = ((coef_hbm, coef_ref), (keep_hbm, keep_ref))
    fetches = [pltpu.make_async_copy(a, b, arrival.at[i]) for i, (a, b) in enumerate(moves)]
    for fetch in fetches:
        fetch.start()
    for fetch in fetches:
        fetch.wait()
    lane = lax.broadcasted_iota(jnp.int32, (tiles, rows), 1)
    even = lane % 2 == 0

    def take(values, index):
        return jnp.take_along_axis(values, index, axis=1)

    other = lane + 1 - 2 * (lane % 2)
    packed = []
    for b in range(strip):
        mine = pl.ds(b, tiles, stride=strip)
        keep = keep_ref[mine, :]
        slot = [coef_ref[k, mine, :] for k in range(8)]
        result = [slot[0]]
        for q in (1, 2, 3, 4):
            result.append(jnp.where(keep > q, slot[q], take(slot[8 - q], other)))
        result[4] = jnp.where(even, result[4], (9 - keep).astype(jnp.float32))
        packed.append(result)
    half = strip * band // 2
    parity = lane // half % 2
    column = lane // (band // 2) % strip
    source = lane % (band // 2) * 2 + parity
    tile = lax.axis_index("tile")
    depth = lax.axis_index("depth")
    for m in range(depths):
        d = depth ^ m
        for q in range(5):
            gathered = [take(packed[b][q], source + d * band) for b in range(strip)]
            merged = gathered[0]
            for b in range(1, strip):
                merged = jnp.where(column == b, gathered[b], merged)
            rows_ref[m, :, q, :] = merged[:, : 2 * half]


    for block in range(tiles * depths):
        target, place = locate(block, bit, (stay_ref, send_ref))
        rows = rows_ref[block % depths, tile ^ (block // depths)]
        for q in range(5):
            target[place, q] = rows[q : q + 1]


def locate(block, bit, refs):
    return refs[block // bit % 2], block // (2 * bit) * bit + block % bit


def regroup_kernel(stay_ref, arrived_ref, next_stay_ref, next_send_ref, *, bit, next_bit):
    run = min(bit, next_bit)
    for block in range(0, 2 * stay_ref.shape[0], run):
        source, start = locate(block, bit, (stay_ref, arrived_ref))
        target, place = locate(block, next_bit, (next_stay_ref, next_send_ref))
        target[pl.ds(place, run)] = source[pl.ds(start, run)]


def unpack(packed_ref, coef_ref, start):
    zblocks, _, _, lanes = packed_ref.shape
    first = lax.broadcasted_iota(jnp.int32, (zblocks, lanes), 1) < lanes // 2
    row = [packed_ref[:, q, 0, :] for q in range(5)]
    turned = [None] + [swap_halves(row[q]) for q in (1, 2, 3, 4)]
    keep = jnp.where(first, turned[4], 9.0 - row[4])
    slot = [row[0]] + [jnp.where(keep > q, row[q], 0.0) for q in (1, 2, 3)]
    slot.append(jnp.where(keep > 4, jnp.where(first, row[4], turned[4]), 0.0))
    slot += [jnp.where(keep > k, turned[8 - k], 0.0) for k in (5, 6, 7)]
    for k in range(8):
        coef_ref[k, pl.ds(start, zblocks), :] = slot[k]


def render_kernel(flip_ref, stay_ref, arrived_ref, out_ref, coef_ref, *, strip, band, samples, tiles, bit):
    unpack(stay_ref, coef_ref, 0)
    unpack(arrived_ref, coef_ref, stay_ref.shape[0])
    slots, zblocks, lanes = coef_ref.shape
    depths = zblocks // tiles
    tile = lax.axis_index("tile")
    depth_index = lax.axis_index("depth")
    flipped = flip_ref[0] > 0
    sign = jnp.where(flipped, jnp.float32(-1.0), jnp.float32(1.0))
    b1 = [cosine(1, i) for i in range(EDGE)]
    row = lax.broadcasted_iota(jnp.int32, (2 * EDGE, lanes), 0)
    x = row % EDGE
    y = row // EDGE

    def table(position, values):
        result = jnp.full((2 * EDGE, lanes), values[0], jnp.float32)
        for i in range(1, len(values)):
            result = jnp.where(position == i, jnp.float32(values[i]), result)
        return result

    x1 = table(x, b1)
    x2 = table(x, [cosine(2, i) for i in range(EDGE)])
    y1 = table(y, b1[:2])
    y2 = table(y, [cosine(2, i) for i in range(2)])
    c_dc = 0.125 * LOG2E
    c_x1 = (0.25 * LOG2E) * x1
    c_x2 = (0.25 * LOG2E) * x2
    c_y1 = (0.25 * LOG2E) * y1
    c_y2 = (0.25 * LOG2E) * y2
    c_xy = (0.5 * LOG2E) * x1 * y1
    c_z = jnp.full((2 * EDGE, lanes), 0.25 * LOG2E * b1[0], jnp.float32) * sign
    c_zy = (0.5 * LOG2E * b1[0]) * y1 * sign
    ratio = b1[1] / b1[0]
    blue_factor = math.exp(-1.5)
    fade = -1.5 / samples

    def block(step, state):
        source = jnp.where(flipped, zblocks - 1 - step, step)
        number = (source % tiles ^ tile) * depths + (source // tiles ^ depth_index)
        zb = number // bit % 2 * (zblocks // 2) + number // (2 * bit) * bit + number % bit
        a = [
            jnp.broadcast_to(coef_ref[k, pl.ds(zb, 1), :], (2 * EDGE, lanes)) for k in range(slots)
        ]
        even = a[0] * c_dc + a[2] * c_x1 + a[4] * c_y2 + a[6] * c_x2
        odd = a[1] * c_y1 + a[5] * c_xy
        g_even = a[3] * c_z
        g_odd = a[7] * c_zy
        halves = []
        for h in range(2):
            depth, before, red, green, blue = state[h]
            base = even + odd if h == 0 else even - odd
            g = g_even + g_odd if h == 0 else g_even - g_odd
            near = g * ratio
            for f in (base + g, base + near, base - near, base - g):
                v = jnp.exp2(f)
                one_u = 1.0 + v * v
                depth = depth + jnp.log2(one_u)
                after = jnp.exp2(fade * depth)
                weight = before - after
                before = after
                red = red + weight / one_u
                green = green + weight * jnp.exp2(f * (f * (-1.0 / LOG2E)))
                blue = blue + weight / (1.0 + blue_factor * v)
            halves.append((depth, before, red, green, blue))
        return tuple(halves)

    zero = jnp.zeros((2 * EDGE, lanes), jnp.float32)
    one = jnp.ones((2 * EDGE, lanes), jnp.float32)
    start = (zero, one, zero, zero, zero)
    state = lax.fori_loop(0, zblocks, block, (start, start), unroll=4)

    width = band * EDGE
    pick = lax.broadcasted_iota(jnp.int32, (2 * EDGE, width), 1)
    y_out = pick % EDGE
    place = pick // EDGE
    place = place % 2 * (lanes // 2) + place // 2
    outs = []
    for _, before, red, green, blue in state:
        opacity = 1.0 - before
        outs.append((opacity - red, green, blue, opacity))
    for ch in range(4):
        for b in range(strip):
            index = place + b * (band // 2)
            low = jnp.take_along_axis(outs[0][ch], index, axis=1)
            high = jnp.take_along_axis(outs[1][ch], index, axis=1)
            both = jnp.where(y_out < 2, low, high)
            first, second = both[:EDGE], both[EDGE:]
            use_first = (y_out[:EDGE] == 0) | (y_out[:EDGE] == 3)
            out_ref[ch, pl.ds(b * EDGE, EDGE), :] = jnp.where(use_first, first, second)


def per_device(coefficients, keep_count, view_flip):
    tiles = lax.axis_size("tile")
    depths = lax.axis_size("depth")
    slots, _, _, columns, rows = coefficients.shape
    strip = columns // tiles
    band = rows // depths
    zblocks = tiles * depths
    vmem = pl.BlockSpec(memory_space=pltpu.VMEM)
    params = pltpu.CompilerParams(vmem_limit_bytes=8 * 1024 * 1024)
    lanes = strip * band
    inputs = (coefficients.reshape(slots, columns, rows), keep_count.reshape(columns, rows))
    half = jax.ShapeDtypeStruct((zblocks // 2, 5, 1, lanes), jnp.float32)
    stages = [("tile", 1 << i, depths << i) for i in range(tiles.bit_length() - 1)]
    stages += [("depth", 1 << i, 1 << i) for i in range(depths.bit_length() - 1)]
    bit = stages[0][2]
    stay, send = pl.pallas_call(
        functools.partial(pack_kernel, tiles=tiles, depths=depths, bit=bit),
        out_shape=[half, half],
        in_specs=[pl.BlockSpec(memory_space=pltpu.HBM)] * 2,
        out_specs=[vmem, vmem],
        scratch_shapes=[
            pltpu.VMEM((slots, columns, rows), jnp.float32),
            pltpu.VMEM((columns, rows), jnp.int32),
            pltpu.VMEM((depths, tiles, 8, lanes), jnp.float32),
            pltpu.SemaphoreType.DMA((2,)),
        ],
        compiler_params=params,
        name="pack",
    )(*(pltpu.with_memory_space_constraint(x, pltpu.HBM) for x in inputs))
    for axis, change, next_bit in stages:
        if next_bit != bit:
            stay, send = pl.pallas_call(
                functools.partial(regroup_kernel, bit=bit, next_bit=next_bit),
                out_shape=[half, half],
                in_specs=[vmem, vmem],
                out_specs=[vmem, vmem],
                compiler_params=params,
                name="regroup",
            )(stay, send)
            bit = next_bit
        send = lax.ppermute(send, axis, [(i, i ^ change) for i in range(lax.axis_size(axis))])
    return pl.pallas_call(
        functools.partial(
            render_kernel, strip=strip, band=band, samples=EDGE * zblocks, tiles=tiles, bit=bit
        ),
        out_shape=jax.ShapeDtypeStruct((4, strip * EDGE, band * EDGE), jnp.float32),
        in_specs=[pl.BlockSpec(memory_space=pltpu.SMEM), vmem, vmem],
        out_specs=vmem,
        scratch_shapes=[pltpu.VMEM((slots, zblocks, lanes), jnp.float32)],
        compiler_params=params,
        name="render",
    )(view_flip, stay, send)


def solution(mesh):
    placed = (P(None, "depth", "tile", None, None), P("depth", "tile", None, None), P("tile"))
    return jax.shard_map(
        per_device, mesh=mesh, in_specs=placed, out_specs=P(None, "tile", "depth"), check_vma=False
    )
```

```python
import functools
import math

import jax
import jax.numpy as jnp
from jax import lax
from jax.experimental import pallas as pl
from jax.experimental.pallas import tpu as pltpu
from jax.sharding import PartitionSpec as P

LOG2E = math.log2(math.e)
EDGE = 4


def cosine(frequency, position):
    factor = 0.5 if frequency == 0 else math.sqrt(0.5)
    return factor * math.cos(math.pi * (2 * position + 1) * frequency / 8.0)


def swap_halves(values):
    half = values.shape[1] // 2
    if values.shape[1] % 128 == 0:
        return pltpu.roll(values, half, 1)
    return jnp.concatenate([values[:, half:], values[:, :half]], axis=1)


def pack_kernel(
    coef_hbm, keep_hbm, stay_ref, send_ref, coef_ref, keep_ref, rows_ref, arrival, *, tiles, depths, bit
):
    _, columns, rows = coef_ref.shape
    strip = columns // tiles
    band = rows // depths
    moves = ((coef_hbm, coef_ref), (keep_hbm, keep_ref))
    fetches = [pltpu.make_async_copy(a, b, arrival.at[i]) for i, (a, b) in enumerate(moves)]
    for fetch in fetches:
        fetch.start()
    for fetch in fetches:
        fetch.wait()
    lane = lax.broadcasted_iota(jnp.int32, (tiles, rows), 1)
    even = lane % 2 == 0

    def take(values, index):
        return jnp.take_along_axis(values, index, axis=1)

    other = lane + 1 - 2 * (lane % 2)
    packed = []
    for b in range(strip):
        mine = pl.ds(b, tiles, stride=strip)
        keep = keep_ref[mine, :]
        slot = [coef_ref[k, mine, :] for k in range(8)]
        result = [slot[0]]
        for q in (1, 2, 3, 4):
            result.append(jnp.where(keep > q, slot[q], take(slot[8 - q], other)))
        result[4] = jnp.where(even, result[4], (9 - keep).astype(jnp.float32))
        packed.append(result)
    half = strip * band // 2
    parity = lane // half % 2
    column = lane // (band // 2) % strip
    source = lane % (band // 2) * 2 + parity
    tile = lax.axis_index("tile")
    depth = lax.axis_index("depth")
    for m in range(depths):
        d = depth ^ m
        for q in range(5):
            gathered = [take(packed[b][q], source + d * band) for b in range(strip)]
            merged = gathered[0]
            for b in range(1, strip):
                merged = jnp.where(column == b, gathered[b], merged)
            rows_ref[m, q] = merged[:, : 2 * half]


    for block in range(tiles * depths):
        target, place = locate(block, bit, (stay_ref, send_ref))
        target[:, pl.ds(place, 1), :] = rows_ref[block % depths, :, pl.ds(tile ^ (block // depths), 1), :]


def locate(block, bit, refs):
    return refs[block // bit % 2], block // (2 * bit) * bit + block % bit


def regroup_kernel(stay_ref, arrived_ref, next_stay_ref, next_send_ref, *, bit, next_bit):
    run = min(bit, next_bit)
    for block in range(0, 2 * stay_ref.shape[1], run):
        source, start = locate(block, bit, (stay_ref, arrived_ref))
        target, place = locate(block, next_bit, (next_stay_ref, next_send_ref))
        target[:, pl.ds(place, run), :] = source[:, pl.ds(start, run), :]


def unpack(packed_ref, coef_ref, start):
    _, zblocks, lanes = packed_ref.shape
    first = lax.broadcasted_iota(jnp.int32, (zblocks, lanes), 1) < lanes // 2
    row = [packed_ref[q] for q in range(5)]
    turned = [None] + [swap_halves(row[q]) for q in (1, 2, 3, 4)]
    keep = jnp.where(first, turned[4], 9.0 - row[4])
    slot = [row[0]] + [jnp.where(keep > q, row[q], 0.0) for q in (1, 2, 3)]
    slot.append(jnp.where(keep > 4, jnp.where(first, row[4], turned[4]), 0.0))
    slot += [jnp.where(keep > k, turned[8 - k], 0.0) for k in (5, 6, 7)]
    for k in range(8):
        coef_ref[k, pl.ds(start, zblocks), :] = slot[k]


def render_kernel(flip_ref, stay_ref, arrived_ref, out_ref, coef_ref, *, strip, band, samples, tiles, bit):
    unpack(stay_ref, coef_ref, 0)
    unpack(arrived_ref, coef_ref, stay_ref.shape[1])
    slots, zblocks, lanes = coef_ref.shape
    depths = zblocks // tiles
    tile = lax.axis_index("tile")
    depth_index = lax.axis_index("depth")
    flipped = flip_ref[0] > 0
    sign = jnp.where(flipped, jnp.float32(-1.0), jnp.float32(1.0))
    b1 = [cosine(1, i) for i in range(EDGE)]
    row = lax.broadcasted_iota(jnp.int32, (2 * EDGE, lanes), 0)
    x = row % EDGE
    y = row // EDGE

    def table(position, values):
        result = jnp.full((2 * EDGE, lanes), values[0], jnp.float32)
        for i in range(1, len(values)):
            result = jnp.where(position == i, jnp.float32(values[i]), result)
        return result

    x1 = table(x, b1)
    x2 = table(x, [cosine(2, i) for i in range(EDGE)])
    y1 = table(y, b1[:2])
    y2 = table(y, [cosine(2, i) for i in range(2)])
    c_dc = 0.125 * LOG2E
    c_x1 = (0.25 * LOG2E) * x1
    c_x2 = (0.25 * LOG2E) * x2
    c_y1 = (0.25 * LOG2E) * y1
    c_y2 = (0.25 * LOG2E) * y2
    c_xy = (0.5 * LOG2E) * x1 * y1
    c_z = jnp.full((2 * EDGE, lanes), 0.25 * LOG2E * b1[0], jnp.float32) * sign
    c_zy = (0.5 * LOG2E * b1[0]) * y1 * sign
    ratio = b1[1] / b1[0]
    blue_factor = math.exp(-1.5)
    fade = -1.5 / samples

    def block(step, state):
        source = jnp.where(flipped, zblocks - 1 - step, step)
        number = (source % tiles ^ tile) * depths + (source // tiles ^ depth_index)
        zb = number // bit % 2 * (zblocks // 2) + number // (2 * bit) * bit + number % bit
        a = [
            jnp.broadcast_to(coef_ref[k, pl.ds(zb, 1), :], (2 * EDGE, lanes)) for k in range(slots)
        ]
        even = a[0] * c_dc + a[2] * c_x1 + a[4] * c_y2 + a[6] * c_x2
        odd = a[1] * c_y1 + a[5] * c_xy
        g_even = a[3] * c_z
        g_odd = a[7] * c_zy
        halves = []
        for h in range(2):
            depth, before, red, green, blue = state[h]
            base = even + odd if h == 0 else even - odd
            g = g_even + g_odd if h == 0 else g_even - g_odd
            near = g * ratio
            for f in (base + g, base + near, base - near, base - g):
                v = jnp.exp2(f)
                one_u = 1.0 + v * v
                depth = depth + jnp.log2(one_u)
                after = jnp.exp2(fade * depth)
                weight = before - after
                before = after
                red = red + weight / one_u
                green = green + weight * jnp.exp2(f * (f * (-1.0 / LOG2E)))
                blue = blue + weight / (1.0 + blue_factor * v)
            halves.append((depth, before, red, green, blue))
        return tuple(halves)

    zero = jnp.zeros((2 * EDGE, lanes), jnp.float32)
    one = jnp.ones((2 * EDGE, lanes), jnp.float32)
    start = (zero, one, zero, zero, zero)
    state = lax.fori_loop(0, zblocks, block, (start, start), unroll=4)

    width = band * EDGE
    pick = lax.broadcasted_iota(jnp.int32, (2 * EDGE, width), 1)
    y_out = pick % EDGE
    place = pick // EDGE
    place = place % 2 * (lanes // 2) + place // 2
    outs = []
    for _, before, red, green, blue in state:
        opacity = 1.0 - before
        outs.append((opacity - red, green, blue, opacity))
    for ch in range(4):
        for b in range(strip):
            index = place + b * (band // 2)
            low = jnp.take_along_axis(outs[0][ch], index, axis=1)
            high = jnp.take_along_axis(outs[1][ch], index, axis=1)
            both = jnp.where(y_out < 2, low, high)
            first, second = both[:EDGE], both[EDGE:]
            use_first = (y_out[:EDGE] == 0) | (y_out[:EDGE] == 3)
            out_ref[ch, pl.ds(b * EDGE, EDGE), :] = jnp.where(use_first, first, second)


def per_device(coefficients, keep_count, view_flip):
    tiles = lax.axis_size("tile")
    depths = lax.axis_size("depth")
    slots, _, _, columns, rows = coefficients.shape
    strip = columns // tiles
    band = rows // depths
    zblocks = tiles * depths
    vmem = pl.BlockSpec(memory_space=pltpu.VMEM)
    params = pltpu.CompilerParams(vmem_limit_bytes=8 * 1024 * 1024)
    lanes = strip * band
    inputs = (coefficients.reshape(slots, columns, rows), keep_count.reshape(columns, rows))
    half = jax.ShapeDtypeStruct((5, zblocks // 2, lanes), jnp.float32)
    stages = [("tile", 1 << i, depths << i) for i in range(tiles.bit_length() - 1)]
    stages += [("depth", 1 << i, 1 << i) for i in range(depths.bit_length() - 1)]
    bit = stages[0][2]
    stay, send = pl.pallas_call(
        functools.partial(pack_kernel, tiles=tiles, depths=depths, bit=bit),
        out_shape=[half, half],
        in_specs=[pl.BlockSpec(memory_space=pltpu.HBM)] * 2,
        out_specs=[vmem, vmem],
        scratch_shapes=[
            pltpu.VMEM((slots, columns, rows), jnp.float32),
            pltpu.VMEM((columns, rows), jnp.int32),
            pltpu.VMEM((depths, 5, tiles, lanes), jnp.float32),
            pltpu.SemaphoreType.DMA((2,)),
        ],
        compiler_params=params,
        name="pack",
    )(*(pltpu.with_memory_space_constraint(x, pltpu.HBM) for x in inputs))
    for axis, change, next_bit in stages:
        if next_bit != bit:
            stay, send = pl.pallas_call(
                functools.partial(regroup_kernel, bit=bit, next_bit=next_bit),
                out_shape=[half, half],
                in_specs=[vmem, vmem],
                out_specs=[vmem, vmem],
                compiler_params=params,
                name="regroup",
            )(stay, send)
            bit = next_bit
        send = lax.ppermute(send, axis, [(i, i ^ change) for i in range(lax.axis_size(axis))])
    return pl.pallas_call(
        functools.partial(
            render_kernel, strip=strip, band=band, samples=EDGE * zblocks, tiles=tiles, bit=bit
        ),
        out_shape=jax.ShapeDtypeStruct((4, strip * EDGE, band * EDGE), jnp.float32),
        in_specs=[pl.BlockSpec(memory_space=pltpu.SMEM), vmem, vmem],
        out_specs=vmem,
        scratch_shapes=[pltpu.VMEM((slots, zblocks, lanes), jnp.float32)],
        compiler_params=params,
        name="render",
    )(view_flip, stay, send)


def solution(mesh):
    placed = (P(None, "depth", "tile", None, None), P("depth", "tile", None, None), P("tile"))
    return jax.shard_map(
        per_device, mesh=mesh, in_specs=placed, out_specs=P(None, "tile", "depth"), check_vma=False
    )
```

```python
import math

import jax
import jax.numpy as jnp
from jax import lax
from jax.experimental import pallas as pl
from jax.experimental.pallas import tpu as pltpu
from jax.sharding import PartitionSpec as P

LOG2E = math.log2(math.e)
EDGE = 4


def cosine(frequency, position):
    factor = 0.5 if frequency == 0 else math.sqrt(0.5)
    return factor * math.cos(math.pi * (2 * position + 1) * frequency / 8.0)


def swap_halves(values):
    half = values.shape[1] // 2
    if values.shape[1] % 128 == 0:
        return pltpu.roll(values, half, 1)
    return jnp.concatenate([values[:, half:], values[:, :half]], axis=1)


def pack_kernel(
    flip_ref, coef_hbm, keep_hbm, out_ref, sign_ref, coef_ref, keep_ref, rows_ref, arrival, *, tiles, depths
):
    _, columns, rows = coef_ref.shape
    strip = columns // tiles
    band = rows // depths
    moves = ((coef_hbm, coef_ref), (keep_hbm, keep_ref))
    fetches = [pltpu.make_async_copy(a, b, arrival.at[i]) for i, (a, b) in enumerate(moves)]
    for fetch in fetches:
        fetch.start()
    for fetch in fetches:
        fetch.wait()
    lane = lax.broadcasted_iota(jnp.int32, (tiles, rows), 1)
    even = lane % 2 == 0

    def take(values, index):
        return jnp.take_along_axis(values, index, axis=1)

    other = lane + 1 - 2 * (lane % 2)
    packed = []
    for b in range(strip):
        mine = pl.ds(b, tiles, stride=strip)
        keep = keep_ref[mine, :]
        slot = [coef_ref[k, mine, :] for k in range(8)]
        result = [slot[0]]
        for q in (1, 2, 3, 4):
            result.append(jnp.where(keep > q, slot[q], take(slot[8 - q], other)))
        result[4] = jnp.where(even, result[4], (9 - keep).astype(jnp.float32))
        packed.append(result)
    sign_ref[...] = jnp.full(sign_ref.shape, 1 - 2 * flip_ref[0], jnp.int32).astype(jnp.float32)
    half = strip * band // 2
    parity = lane // half % 2
    column = lane // (band // 2) % strip
    source = lane % (band // 2) * 2 + parity
    for d in range(depths):
        for q in range(5):
            gathered = [take(packed[b][q], source + d * band) for b in range(strip)]
            merged = gathered[0]
            for b in range(1, strip):
                merged = jnp.where(column == b, gathered[b], merged)
            rows_ref[d, q] = merged[:, : 2 * half]


    for d in range(depths):
        for t in range(tiles):
            out_ref[depths - 1 - d, tiles - 1 - t, :, 0, :] = rows_ref[d, :, t, :]


def unpack(packed_ref, coef_ref):
    depths, tiles, _, _, lanes = packed_ref.shape
    zblocks = tiles * depths
    first = lax.broadcasted_iota(jnp.int32, (zblocks, lanes), 1) < lanes // 2
    row = [packed_ref[:, :, q, 0, :].reshape(zblocks, lanes) for q in range(5)]
    turned = [None] + [swap_halves(row[q]) for q in (1, 2, 3, 4)]
    keep = jnp.where(first, turned[4], 9.0 - row[4])
    slot = [row[0]] + [jnp.where(keep > q, row[q], 0.0) for q in (1, 2, 3)]
    slot.append(jnp.where(keep > 4, jnp.where(first, row[4], turned[4]), 0.0))
    slot += [jnp.where(keep > k, turned[8 - k], 0.0) for k in (5, 6, 7)]
    for k in range(8):
        coef_ref[k] = slot[k]


def render_kernel(sign_ref, packed_ref, out_ref, coef_ref, *, strip, band, samples):
    unpack(packed_ref, coef_ref)
    slots, zblocks, lanes = coef_ref.shape
    sign = sign_ref[...]
    flipped = jnp.max(sign) < 0.0
    b1 = [cosine(1, i) for i in range(EDGE)]
    row = lax.broadcasted_iota(jnp.int32, (2 * EDGE, lanes), 0)
    x = row % EDGE
    y = row // EDGE

    def table(position, values):
        result = jnp.full((2 * EDGE, lanes), values[0], jnp.float32)
        for i in range(1, len(values)):
            result = jnp.where(position == i, jnp.float32(values[i]), result)
        return result

    x1 = table(x, b1)
    x2 = table(x, [cosine(2, i) for i in range(EDGE)])
    y1 = table(y, b1[:2])
    y2 = table(y, [cosine(2, i) for i in range(2)])
    c_dc = 0.125 * LOG2E
    c_x1 = (0.25 * LOG2E) * x1
    c_x2 = (0.25 * LOG2E) * x2
    c_y1 = (0.25 * LOG2E) * y1
    c_y2 = (0.25 * LOG2E) * y2
    c_xy = (0.5 * LOG2E) * x1 * y1
    c_z = jnp.full((2 * EDGE, lanes), 0.25 * LOG2E * b1[0], jnp.float32) * sign
    c_zy = (0.5 * LOG2E * b1[0]) * y1 * sign
    ratio = b1[1] / b1[0]
    blue_factor = math.exp(-1.5)
    fade = -1.5 / samples

    def block(step, state):
        source = jnp.where(flipped, zblocks - 1 - step, step)
        zb = zblocks - 1 - source
        a = [
            jnp.broadcast_to(coef_ref[k, pl.ds(zb, 1), :], (2 * EDGE, lanes)) for k in range(slots)
        ]
        even = a[0] * c_dc + a[2] * c_x1 + a[4] * c_y2 + a[6] * c_x2
        odd = a[1] * c_y1 + a[5] * c_xy
        g_even = a[3] * c_z
        g_odd = a[7] * c_zy
        halves = []
        for h in range(2):
            depth, before, red, green, blue = state[h]
            base = even + odd if h == 0 else even - odd
            g = g_even + g_odd if h == 0 else g_even - g_odd
            near = g * ratio
            for f in (base + g, base + near, base - near, base - g):
                v = jnp.exp2(f)
                one_u = 1.0 + v * v
                depth = depth + jnp.log2(one_u)
                after = jnp.exp2(fade * depth)
                weight = before - after
                before = after
                red = red + weight / one_u
                green = green + weight * jnp.exp2(f * (f * (-1.0 / LOG2E)))
                blue = blue + weight / (1.0 + blue_factor * v)
            halves.append((depth, before, red, green, blue))
        return tuple(halves)

    zero = jnp.zeros((2 * EDGE, lanes), jnp.float32)
    one = jnp.ones((2 * EDGE, lanes), jnp.float32)
    start = (zero, one, zero, zero, zero)
    state = lax.fori_loop(0, zblocks, block, (start, start), unroll=8)

    width = band * EDGE
    pick = lax.broadcasted_iota(jnp.int32, (2 * EDGE, width), 1)
    y_out = pick % EDGE
    place = pick // EDGE
    place = place % 2 * (lanes // 2) + place // 2
    outs = []
    for _, before, red, green, blue in state:
        opacity = 1.0 - before
        outs.append((opacity - red, green, blue, opacity))
    for ch in range(4):
        for b in range(strip):
            index = place + b * (band // 2)
            low = jnp.take_along_axis(outs[0][ch], index, axis=1)
            high = jnp.take_along_axis(outs[1][ch], index, axis=1)
            both = jnp.where(y_out < 2, low, high)
            first, second = both[:EDGE], both[EDGE:]
            use_first = (y_out[:EDGE] == 0) | (y_out[:EDGE] == 3)
            out_ref[ch, pl.ds(b * EDGE, EDGE), :] = jnp.where(use_first, first, second)


def per_device(coefficients, keep_count, view_flip):
    tiles = lax.axis_size("tile")
    depths = lax.axis_size("depth")
    slots, _, _, columns, rows = coefficients.shape
    strip = columns // tiles
    band = rows // depths
    zblocks = tiles * depths
    vmem = pl.BlockSpec(memory_space=pltpu.VMEM)
    params = pltpu.CompilerParams(vmem_limit_bytes=8 * 1024 * 1024)
    lanes = strip * band
    inputs = (coefficients.reshape(slots, columns, rows), keep_count.reshape(columns, rows))
    outgoing, sign = pl.pallas_call(
        lambda *refs: pack_kernel(*refs, tiles=tiles, depths=depths),
        out_shape=[
            jax.ShapeDtypeStruct((depths, tiles, 5, 1, lanes), jnp.float32),
            jax.ShapeDtypeStruct((2 * EDGE, lanes), jnp.float32),
        ],
        in_specs=[pl.BlockSpec(memory_space=pltpu.SMEM)] + [pl.BlockSpec(memory_space=pltpu.HBM)] * 2,
        out_specs=[vmem, vmem],
        scratch_shapes=[
            pltpu.VMEM((slots, columns, rows), jnp.float32),
            pltpu.VMEM((columns, rows), jnp.int32),
            pltpu.VMEM((depths, 5, tiles, lanes), jnp.float32),
            pltpu.SemaphoreType.DMA((2,)),
        ],
        compiler_params=params,
        name="pack",
    )(view_flip, *(pltpu.with_memory_space_constraint(x, pltpu.HBM) for x in inputs))
    sent = outgoing.reshape(zblocks, 5, 1, lanes)
    falling = [list(range(zblocks - 1, -1, -1))]
    arrived = lax.all_to_all(
        sent, ("depth", "tile"), split_axis=0, concat_axis=0, tiled=True, axis_index_groups=falling
    )
    return pl.pallas_call(
        lambda *refs: render_kernel(*refs, strip=strip, band=band, samples=EDGE * zblocks),
        out_shape=jax.ShapeDtypeStruct((4, strip * EDGE, band * EDGE), jnp.float32),
        in_specs=[vmem, vmem],
        out_specs=vmem,
        scratch_shapes=[pltpu.VMEM((slots, zblocks, lanes), jnp.float32)],
        compiler_params=params,
        name="render",
    )(sign, arrived.reshape(outgoing.shape))


def solution(mesh):
    placed = (P(None, "depth", "tile", None, None), P("depth", "tile", None, None), P("tile"))
    return jax.shard_map(
        per_device, mesh=mesh, in_specs=placed, out_specs=P(None, "tile", "depth"), check_vma=False
    )
```

```python
import math

import jax
import jax.numpy as jnp
from jax import lax
from jax.experimental import pallas as pl
from jax.experimental.pallas import tpu as pltpu
from jax.sharding import PartitionSpec as P

LOG2E = math.log2(math.e)
EDGE = 4


def cosine(frequency, position):
    factor = 0.5 if frequency == 0 else math.sqrt(0.5)
    return factor * math.cos(math.pi * (2 * position + 1) * frequency / 8.0)


def swap_halves(values):
    half = values.shape[1] // 2
    if values.shape[1] % 128 == 0:
        return pltpu.roll(values, half, 1)
    return jnp.concatenate([values[:, half:], values[:, :half]], axis=1)


def pack_kernel(
    flip_ref, coef_hbm, keep_hbm, out_ref, sign_ref, coef_ref, keep_ref, rows_ref, arrival, *, tiles, depths
):
    _, columns, rows = coef_ref.shape
    strip = columns // tiles
    band = rows // depths
    moves = [(keep_hbm, keep_ref)] + [(coef_hbm.at[k], coef_ref.at[k]) for k in range(8)]
    fetches = [pltpu.make_async_copy(a, b, arrival.at[i]) for i, (a, b) in enumerate(moves)]
    for fetch in fetches:
        fetch.start()
    for fetch in fetches:
        fetch.wait()
    lane = lax.broadcasted_iota(jnp.int32, (tiles, rows), 1)
    even = lane % 2 == 0

    def take(values, index):
        return jnp.take_along_axis(values, index, axis=1)

    other = lane + 1 - 2 * (lane % 2)
    packed = []
    for b in range(strip):
        mine = pl.ds(b, tiles, stride=strip)
        keep = keep_ref[mine, :]
        slot = [coef_ref[k, mine, :] for k in range(8)]
        result = [slot[0]]
        for q in (1, 2, 3, 4):
            result.append(jnp.where(keep > q, slot[q], take(slot[8 - q], other)))
        result[4] = jnp.where(even, result[4], (9 - keep).astype(jnp.float32))
        packed.append(result)
    sign_ref[...] = jnp.full(sign_ref.shape, 1 - 2 * flip_ref[0], jnp.int32).astype(jnp.float32)
    half = strip * band // 2
    parity = lane // half % 2
    column = lane // (band // 2) % strip
    source = lane % (band // 2) * 2 + parity
    for d in range(depths):
        for q in range(5):
            gathered = [take(packed[b][q], source + d * band) for b in range(strip)]
            merged = gathered[0]
            for b in range(1, strip):
                merged = jnp.where(column == b, gathered[b], merged)
            rows_ref[d, q] = merged[:, : 2 * half]


    for d in range(depths):
        for t in range(tiles):
            out_ref[depths - 1 - d, tiles - 1 - t, :, 0, :] = rows_ref[d, :, t, :]


def unpack(packed_ref, coef_ref):
    depths, tiles, _, _, lanes = packed_ref.shape
    zblocks = tiles * depths
    first = lax.broadcasted_iota(jnp.int32, (zblocks, lanes), 1) < lanes // 2
    row = [packed_ref[:, :, q, 0, :].reshape(zblocks, lanes) for q in range(5)]
    turned = [None] + [swap_halves(row[q]) for q in (1, 2, 3, 4)]
    keep = jnp.where(first, turned[4], 9.0 - row[4])
    slot = [row[0]] + [jnp.where(keep > q, row[q], 0.0) for q in (1, 2, 3)]
    slot.append(jnp.where(keep > 4, jnp.where(first, row[4], turned[4]), 0.0))
    slot += [jnp.where(keep > k, turned[8 - k], 0.0) for k in (5, 6, 7)]
    for k in range(8):
        coef_ref[k] = slot[k]


def render_kernel(sign_ref, packed_ref, out_ref, coef_ref, *, strip, band, samples):
    unpack(packed_ref, coef_ref)
    slots, zblocks, lanes = coef_ref.shape
    sign = sign_ref[...]
    flipped = jnp.max(sign) < 0.0
    b1 = [cosine(1, i) for i in range(EDGE)]
    row = lax.broadcasted_iota(jnp.int32, (2 * EDGE, lanes), 0)
    x = row % EDGE
    y = row // EDGE

    def table(position, values):
        result = jnp.full((2 * EDGE, lanes), values[0], jnp.float32)
        for i in range(1, len(values)):
            result = jnp.where(position == i, jnp.float32(values[i]), result)
        return result

    x1 = table(x, b1)
    x2 = table(x, [cosine(2, i) for i in range(EDGE)])
    y1 = table(y, b1[:2])
    y2 = table(y, [cosine(2, i) for i in range(2)])
    c_dc = 0.125 * LOG2E
    c_x1 = (0.25 * LOG2E) * x1
    c_x2 = (0.25 * LOG2E) * x2
    c_y1 = (0.25 * LOG2E) * y1
    c_y2 = (0.25 * LOG2E) * y2
    c_xy = (0.5 * LOG2E) * x1 * y1
    c_z = jnp.full((2 * EDGE, lanes), 0.25 * LOG2E * b1[0], jnp.float32) * sign
    c_zy = (0.5 * LOG2E * b1[0]) * y1 * sign
    ratio = b1[1] / b1[0]
    blue_one = 2.0**-20
    blue_factor = blue_one * math.exp(-1.5)
    fade = -1.5 / samples

    def block(step, state):
        source = jnp.where(flipped, zblocks - 1 - step, step)
        zb = zblocks - 1 - source
        a = [
            jnp.broadcast_to(coef_ref[k, pl.ds(zb, 1), :], (2 * EDGE, lanes)) for k in range(slots)
        ]
        even = a[0] * c_dc + a[2] * c_x1 + a[4] * c_y2 + a[6] * c_x2
        odd = a[1] * c_y1 + a[5] * c_xy
        g_even = a[3] * c_z
        g_odd = a[7] * c_zy
        halves = []
        for h in range(2):
            depth, before, red, green, blue = state[h]
            base = even + odd if h == 0 else even - odd
            g = g_even + g_odd if h == 0 else g_even - g_odd
            near = g * ratio
            for f in (base + g, base + near, base - near, base - g):
                v = jnp.exp2(f)
                one_u = 1.0 + v * v
                depth = depth + jnp.log2(one_u)
                after = jnp.exp2(fade * depth)
                weight = before - after
                before = after
                blue_u = blue_one + blue_factor * v
                shared = weight / (one_u * blue_u)
                red = red + shared * blue_u
                green = green + weight * jnp.exp2(f * (f * (-1.0 / LOG2E)))
                blue = blue + shared * one_u
            halves.append((depth, before, red, green, blue))
        return tuple(halves)

    zero = jnp.zeros((2 * EDGE, lanes), jnp.float32)
    one = jnp.ones((2 * EDGE, lanes), jnp.float32)
    start = (zero, one, zero, zero, zero)
    state = lax.fori_loop(0, zblocks, block, (start, start), unroll=16)

    width = band * EDGE
    pick = lax.broadcasted_iota(jnp.int32, (2 * EDGE, width), 1)
    y_out = pick % EDGE
    place = pick // EDGE
    place = place % 2 * (lanes // 2) + place // 2
    outs = []
    for _, before, red, green, blue in state:
        opacity = 1.0 - before
        outs.append((opacity - red, green, blue * blue_one, opacity))
    for ch in range(4):
        for b in range(strip):
            index = place + b * (band // 2)
            low = jnp.take_along_axis(outs[0][ch], index, axis=1)
            high = jnp.take_along_axis(outs[1][ch], index, axis=1)
            both = jnp.where(y_out < 2, low, high)
            first, second = both[:EDGE], both[EDGE:]
            use_first = (y_out[:EDGE] == 0) | (y_out[:EDGE] == 3)
            out_ref[ch, pl.ds(b * EDGE, EDGE), :] = jnp.where(use_first, first, second)


def per_device(coefficients, keep_count, view_flip):
    tiles = lax.axis_size("tile")
    depths = lax.axis_size("depth")
    slots, _, _, columns, rows = coefficients.shape
    strip = columns // tiles
    band = rows // depths
    zblocks = tiles * depths
    vmem = pl.BlockSpec(memory_space=pltpu.VMEM)
    params = pltpu.CompilerParams(vmem_limit_bytes=8 * 1024 * 1024)
    lanes = strip * band
    inputs = (coefficients.reshape(slots, columns, rows), keep_count.reshape(columns, rows))
    outgoing, sign = pl.pallas_call(
        lambda *refs: pack_kernel(*refs, tiles=tiles, depths=depths),
        out_shape=[
            jax.ShapeDtypeStruct((depths, tiles, 5, 1, lanes), jnp.float32),
            jax.ShapeDtypeStruct((2 * EDGE, lanes), jnp.float32),
        ],
        in_specs=[pl.BlockSpec(memory_space=pltpu.SMEM)] + [pl.BlockSpec(memory_space=pltpu.HBM)] * 2,
        out_specs=[vmem, vmem],
        scratch_shapes=[
            pltpu.VMEM((slots, columns, rows), jnp.float32),
            pltpu.VMEM((columns, rows), jnp.int32),
            pltpu.VMEM((depths, 5, tiles, lanes), jnp.float32),
            pltpu.SemaphoreType.DMA((1 + slots,)),
        ],
        compiler_params=params,
        name="pack",
    )(view_flip, *(pltpu.with_memory_space_constraint(x, pltpu.HBM) for x in inputs))
    sent = outgoing.reshape(zblocks, 5, 1, lanes)
    falling = [list(range(zblocks - 1, -1, -1))]
    arrived = lax.all_to_all(
        sent, ("depth", "tile"), split_axis=0, concat_axis=0, tiled=True, axis_index_groups=falling
    )
    return pl.pallas_call(
        lambda *refs: render_kernel(*refs, strip=strip, band=band, samples=EDGE * zblocks),
        out_shape=jax.ShapeDtypeStruct((4, strip * EDGE, band * EDGE), jnp.float32),
        in_specs=[vmem, vmem],
        out_specs=vmem,
        scratch_shapes=[pltpu.VMEM((slots, zblocks, lanes), jnp.float32)],
        compiler_params=params,
        name="render",
    )(sign, arrived.reshape(outgoing.shape))


def solution(mesh):
    placed = (P(None, "depth", "tile", None, None), P("depth", "tile", None, None), P("tile"))
    return jax.shard_map(
        per_device, mesh=mesh, in_specs=placed, out_specs=P(None, "tile", "depth"), check_vma=False
    )
```

```python
import math

import jax
import jax.numpy as jnp
from jax import lax
from jax.experimental import pallas as pl
from jax.experimental.pallas import tpu as pltpu
from jax.sharding import PartitionSpec as P

LOG2E = math.log2(math.e)
EDGE = 4


def cosine(frequency, position):
    factor = 0.5 if frequency == 0 else math.sqrt(0.5)
    return factor * math.cos(math.pi * (2 * position + 1) * frequency / 8.0)


def swap_halves(values):
    half = values.shape[1] // 2
    if values.shape[1] % 128 == 0:
        return pltpu.roll(values, half, 1)
    return jnp.concatenate([values[:, half:], values[:, :half]], axis=1)


def pack_kernel(
    flip_ref, coef_hbm, keep_hbm, out_ref, sign_ref, coef_ref, keep_ref, rows_ref, arrival, *, tiles, depths
):
    _, columns, rows = coef_ref.shape
    strip = columns // tiles
    band = rows // depths
    moves = [(keep_hbm, keep_ref)] + [(coef_hbm.at[k], coef_ref.at[k]) for k in range(8)]
    fetches = [pltpu.make_async_copy(a, b, arrival.at[i]) for i, (a, b) in enumerate(moves)]
    for fetch in fetches:
        fetch.start()
    for fetch in fetches:
        fetch.wait()
    lane = lax.broadcasted_iota(jnp.int32, (tiles, rows), 1)
    even = lane % 2 == 0

    def take(values, index):
        return jnp.take_along_axis(values, index, axis=1)

    other = lane + 1 - 2 * (lane % 2)
    packed = []
    for b in range(strip):
        mine = pl.ds(b, tiles, stride=strip)
        keep = keep_ref[mine, :]
        slot = [coef_ref[k, mine, :] for k in range(8)]
        result = [slot[0]]
        for q in (1, 2, 3, 4):
            result.append(jnp.where(keep > q, slot[q], take(slot[8 - q], other)))
        result[4] = jnp.where(even, result[4], (9 - keep).astype(jnp.float32))
        packed.append(result)
    sign_ref[...] = jnp.full(sign_ref.shape, 1 - 2 * flip_ref[0], jnp.int32).astype(jnp.float32)
    half = strip * band // 2
    parity = lane // half % 2
    column = lane // (band // 2) % strip
    source = lane % (band // 2) * 2 + parity
    for d in range(depths):
        for q in range(5):
            gathered = [take(packed[b][q], source + d * band) for b in range(strip)]
            merged = gathered[0]
            for b in range(1, strip):
                merged = jnp.where(column == b, gathered[b], merged)
            rows_ref[d, q] = merged[:, : 2 * half]


    for d in range(depths):
        for t in range(tiles):
            out_ref[depths - 1 - d, tiles - 1 - t, :, 0, :] = rows_ref[d, :, t, :]


def unpack(packed_ref, coef_ref):
    depths, tiles, _, _, lanes = packed_ref.shape
    zblocks = tiles * depths
    first = lax.broadcasted_iota(jnp.int32, (zblocks, lanes), 1) < lanes // 2
    row = [packed_ref[:, :, q, 0, :].reshape(zblocks, lanes) for q in range(5)]
    turned = [None] + [swap_halves(row[q]) for q in (1, 2, 3, 4)]
    keep = jnp.where(first, turned[4], 9.0 - row[4])
    slot = [row[0]] + [jnp.where(keep > q, row[q], 0.0) for q in (1, 2, 3)]
    slot.append(jnp.where(keep > 4, jnp.where(first, row[4], turned[4]), 0.0))
    slot += [jnp.where(keep > k, turned[8 - k], 0.0) for k in (5, 6, 7)]
    for k in range(8):
        coef_ref[k] = slot[k]


def render_kernel(sign_ref, packed_ref, out_ref, coef_ref, *, strip, band, samples):
    unpack(packed_ref, coef_ref)
    slots, zblocks, lanes = coef_ref.shape
    sign = sign_ref[...]
    flipped = jnp.max(sign) < 0.0
    b1 = [cosine(1, i) for i in range(EDGE)]
    row = lax.broadcasted_iota(jnp.int32, (2 * EDGE, lanes), 0)
    x = row % EDGE
    y = row // EDGE

    def table(position, values):
        result = jnp.full((2 * EDGE, lanes), values[0], jnp.float32)
        for i in range(1, len(values)):
            result = jnp.where(position == i, jnp.float32(values[i]), result)
        return result

    x1 = table(x, b1)
    x2 = table(x, [cosine(2, i) for i in range(EDGE)])
    y1 = table(y, b1[:2])
    y2 = table(y, [cosine(2, i) for i in range(2)])
    c_dc = 0.125 * LOG2E
    c_x1 = (0.25 * LOG2E) * x1
    c_x2 = (0.25 * LOG2E) * x2
    c_y1 = (0.25 * LOG2E) * y1
    c_y2 = (0.25 * LOG2E) * y2
    c_xy = (0.5 * LOG2E) * x1 * y1
    c_z = jnp.full((2 * EDGE, lanes), 0.25 * LOG2E * b1[0], jnp.float32) * sign
    c_zy = (0.5 * LOG2E * b1[0]) * y1 * sign
    ratio = b1[1] / b1[0]
    blue_one = 2.0**-20
    blue_factor = blue_one * math.exp(-1.5)
    fade = -1.5 / samples

    def block(step, state):
        source = jnp.where(flipped, zblocks - 1 - step, step)
        zb = zblocks - 1 - source
        a = [
            coef_ref[k, pl.ds(zb, 2 * EDGE, stride=0), :] for k in range(slots)
        ]
        even = a[0] * c_dc + a[2] * c_x1 + a[4] * c_y2 + a[6] * c_x2
        odd = a[1] * c_y1 + a[5] * c_xy
        g_even = a[3] * c_z
        g_odd = a[7] * c_zy
        halves = []
        for h in range(2):
            depth, before, red, green, blue = state[h]
            base = even + odd if h == 0 else even - odd
            g = g_even + g_odd if h == 0 else g_even - g_odd
            near = g * ratio
            for f in (base + g, base + near, base - near, base - g):
                v = jnp.exp2(f)
                one_u = 1.0 + v * v
                depth = depth + jnp.log2(one_u)
                after = jnp.exp2(fade * depth)
                weight = before - after
                before = after
                blue_u = blue_one + blue_factor * v
                shared = weight / (one_u * blue_u)
                red = red + shared * blue_u
                green = green + weight * jnp.exp2(f * (f * (-1.0 / LOG2E)))
                blue = blue + shared * one_u
            halves.append((depth, before, red, green, blue))
        return tuple(halves)

    zero = jnp.zeros((2 * EDGE, lanes), jnp.float32)
    one = jnp.ones((2 * EDGE, lanes), jnp.float32)
    start = (zero, one, zero, zero, zero)
    state = lax.fori_loop(0, zblocks, block, (start, start), unroll=16)

    width = band * EDGE
    pick = lax.broadcasted_iota(jnp.int32, (2 * EDGE, width), 1)
    y_out = pick % EDGE
    place = pick // EDGE
    place = place % 2 * (lanes // 2) + place // 2
    outs = []
    for _, before, red, green, blue in state:
        opacity = 1.0 - before
        outs.append((opacity - red, green, blue * blue_one, opacity))
    for ch in range(4):
        for b in range(strip):
            index = place + b * (band // 2)
            low = jnp.take_along_axis(outs[0][ch], index, axis=1)
            high = jnp.take_along_axis(outs[1][ch], index, axis=1)
            both = jnp.where(y_out < 2, low, high)
            first, second = both[:EDGE], both[EDGE:]
            use_first = (y_out[:EDGE] == 0) | (y_out[:EDGE] == 3)
            out_ref[ch, pl.ds(b * EDGE, EDGE), :] = jnp.where(use_first, first, second)


def per_device(coefficients, keep_count, view_flip):
    tiles = lax.axis_size("tile")
    depths = lax.axis_size("depth")
    slots, _, _, columns, rows = coefficients.shape
    strip = columns // tiles
    band = rows // depths
    zblocks = tiles * depths
    vmem = pl.BlockSpec(memory_space=pltpu.VMEM)
    params = pltpu.CompilerParams(vmem_limit_bytes=8 * 1024 * 1024)
    lanes = strip * band
    inputs = (coefficients.reshape(slots, columns, rows), keep_count.reshape(columns, rows))
    outgoing, sign = pl.pallas_call(
        lambda *refs: pack_kernel(*refs, tiles=tiles, depths=depths),
        out_shape=[
            jax.ShapeDtypeStruct((depths, tiles, 5, 1, lanes), jnp.float32),
            jax.ShapeDtypeStruct((2 * EDGE, lanes), jnp.float32),
        ],
        in_specs=[pl.BlockSpec(memory_space=pltpu.SMEM)] + [pl.BlockSpec(memory_space=pltpu.HBM)] * 2,
        out_specs=[vmem, vmem],
        scratch_shapes=[
            pltpu.VMEM((slots, columns, rows), jnp.float32),
            pltpu.VMEM((columns, rows), jnp.int32),
            pltpu.VMEM((depths, 5, tiles, lanes), jnp.float32),
            pltpu.SemaphoreType.DMA((1 + slots,)),
        ],
        compiler_params=params,
        name="pack",
    )(view_flip, *(pltpu.with_memory_space_constraint(x, pltpu.HBM) for x in inputs))
    sent = outgoing.reshape(zblocks, 5, 1, lanes)
    falling = [list(range(zblocks - 1, -1, -1))]
    arrived = lax.all_to_all(
        sent, ("depth", "tile"), split_axis=0, concat_axis=0, tiled=True, axis_index_groups=falling
    )
    return pl.pallas_call(
        lambda *refs: render_kernel(*refs, strip=strip, band=band, samples=EDGE * zblocks),
        out_shape=jax.ShapeDtypeStruct((4, strip * EDGE, band * EDGE), jnp.float32),
        in_specs=[vmem, vmem],
        out_specs=vmem,
        scratch_shapes=[pltpu.VMEM((slots, zblocks, lanes), jnp.float32)],
        compiler_params=params,
        name="render",
    )(sign, arrived.reshape(outgoing.shape))


def solution(mesh):
    placed = (P(None, "depth", "tile", None, None), P("depth", "tile", None, None), P("tile"))
    return jax.shard_map(
        per_device, mesh=mesh, in_specs=placed, out_specs=P(None, "tile", "depth"), check_vma=False
    )
```

```python
import math

import jax
import jax.numpy as jnp
from jax import lax
from jax.experimental import pallas as pl
from jax.experimental.pallas import tpu as pltpu
from jax.sharding import PartitionSpec as P

LOG2E = math.log2(math.e)
EDGE = 4


def cosine(frequency, position):
    factor = 0.5 if frequency == 0 else math.sqrt(0.5)
    return factor * math.cos(math.pi * (2 * position + 1) * frequency / 8.0)


def swap_halves(values):
    half = values.shape[1] // 2
    if values.shape[1] % 128 == 0:
        return pltpu.roll(values, half, 1)
    return jnp.concatenate([values[:, half:], values[:, :half]], axis=1)


def pack_kernel(
    flip_ref, coef_hbm, keep_hbm, out_ref, sign_ref, coef_ref, keep_ref, arrival, *, tiles, depths
):
    _, columns, rows = coef_ref.shape
    strip = columns // tiles
    band = rows // depths
    fetch_keep = pltpu.make_async_copy(keep_hbm, keep_ref, arrival.at[8])
    fetches = [pltpu.make_async_copy(coef_hbm.at[k], coef_ref.at[k], arrival.at[k]) for k in range(8)]
    fetch_keep.start()
    for k in (1, 7, 2, 6, 3, 5, 4, 0):
        fetches[k].start()
    fetch_keep.wait()
    lane = lax.broadcasted_iota(jnp.int32, (tiles, rows), 1)
    even = lane % 2 == 0

    def take(values, index):
        return jnp.take_along_axis(values, index, axis=1)

    other = lane + 1 - 2 * (lane % 2)
    sign_ref[...] = jnp.full(sign_ref.shape, 1 - 2 * flip_ref[0], jnp.int32).astype(jnp.float32)
    half = strip * band // 2
    parity = lane // half % 2
    column = lane // (band // 2) % strip
    source = lane % (band // 2) * 2 + parity
    mine = [pl.ds(b, tiles, stride=strip) for b in range(strip)]
    keep = [keep_ref[rows_b, :] for rows_b in mine]
    for q in (1, 2, 3, 4, 0):
        for k in (q, 8 - q) if q % 4 else (q,):
            fetches[k].wait()
        packed = [coef_ref[q, rows_b, :] for rows_b in mine]
        if q > 0:
            turned = [take(coef_ref[8 - q, rows_b, :], other) for rows_b in mine]
            packed = [jnp.where(keep[b] > q, packed[b], turned[b]) for b in range(strip)]
        if q == 4:
            packed = [jnp.where(even, packed[b], (9 - keep[b]).astype(jnp.float32)) for b in range(strip)]
        for d in range(depths):
            gathered = [take(packed[b], source + d * band) for b in range(strip)]
            merged = gathered[0]
            for b in range(1, strip):
                merged = jnp.where(column == b, gathered[b], merged)
            start = (depths - 1 - d) * tiles * 5 + q
            out_ref[pl.ds(start, tiles, stride=5), :] = merged[:, : 2 * half]


def unpack(packed_ref, coef_ref):
    zblocks, lanes = packed_ref.shape[0] // 5, packed_ref.shape[1]
    first = lax.broadcasted_iota(jnp.int32, (zblocks, lanes), 1) < lanes // 2
    row = [packed_ref[pl.ds(q, zblocks, stride=5), :] for q in range(5)]
    turned = [None] + [swap_halves(row[q]) for q in (1, 2, 3, 4)]
    keep = jnp.where(first, turned[4], 9.0 - row[4])
    slot = [row[0]] + [jnp.where(keep > q, row[q], 0.0) for q in (1, 2, 3)]
    slot.append(jnp.where(keep > 4, jnp.where(first, row[4], turned[4]), 0.0))
    slot += [jnp.where(keep > k, turned[8 - k], 0.0) for k in (5, 6, 7)]
    for k in range(8):
        coef_ref[k] = slot[k]


def render_kernel(sign_ref, packed_ref, out_ref, coef_ref, *, strip, band, samples, tiles, depths):
    unpack(packed_ref, coef_ref)
    slots, zblocks, lanes = coef_ref.shape
    sign = sign_ref[...]
    flipped = jnp.max(sign) < 0.0
    b1 = [cosine(1, i) for i in range(EDGE)]
    row = lax.broadcasted_iota(jnp.int32, (2 * EDGE, lanes), 0)
    x = row % EDGE
    y = row // EDGE

    def table(position, values):
        result = jnp.full((2 * EDGE, lanes), values[0], jnp.float32)
        for i in range(1, len(values)):
            result = jnp.where(position == i, jnp.float32(values[i]), result)
        return result

    x1 = table(x, b1)
    x2 = table(x, [cosine(2, i) for i in range(EDGE)])
    y1 = table(y, b1[:2])
    y2 = table(y, [cosine(2, i) for i in range(2)])
    c_dc = 0.125 * LOG2E
    c_x1 = (0.25 * LOG2E) * x1
    c_x2 = (0.25 * LOG2E) * x2
    c_y1 = (0.25 * LOG2E) * y1
    c_y2 = (0.25 * LOG2E) * y2
    c_xy = (0.5 * LOG2E) * x1 * y1
    c_z = jnp.full((2 * EDGE, lanes), 0.25 * LOG2E * b1[0], jnp.float32) * sign
    c_zy = (0.5 * LOG2E * b1[0]) * y1 * sign
    ratio = b1[1] / b1[0]
    blue_one = 2.0**-20
    blue_factor = blue_one * math.exp(-1.5)
    fade = -1.5 / samples

    def block(step, state):
        source = jnp.where(flipped, zblocks - 1 - step, step)
        zb = (depths - 1 - source // tiles) * tiles + source % tiles
        a = [
            jnp.broadcast_to(coef_ref[k, pl.ds(zb, 1), :], (2 * EDGE, lanes)) for k in range(slots)
        ]
        even = a[0] * c_dc + a[2] * c_x1 + a[4] * c_y2 + a[6] * c_x2
        odd = a[1] * c_y1 + a[5] * c_xy
        g_even = a[3] * c_z
        g_odd = a[7] * c_zy
        halves = []
        for h in range(2):
            depth, before, red, green, blue = state[h]
            base = even + odd if h == 0 else even - odd
            g = g_even + g_odd if h == 0 else g_even - g_odd
            near = g * ratio
            for f in (base + g, base + near, base - near, base - g):
                v = jnp.exp2(f)
                one_u = 1.0 + v * v
                depth = depth + jnp.log2(one_u)
                after = jnp.exp2(fade * depth)
                weight = before - after
                before = after
                blue_u = blue_one + blue_factor * v
                shared = weight / (one_u * blue_u)
                red = red + shared * blue_u
                green = green + weight * jnp.exp2(f * (f * (-1.0 / LOG2E)))
                blue = blue + shared * one_u
            halves.append((depth, before, red, green, blue))
        return tuple(halves)

    zero = jnp.zeros((2 * EDGE, lanes), jnp.float32)
    one = jnp.ones((2 * EDGE, lanes), jnp.float32)
    start = (zero, one, zero, zero, zero)
    state = lax.fori_loop(0, zblocks, block, (start, start), unroll=16)

    width = band * EDGE
    pick = lax.broadcasted_iota(jnp.int32, (2 * EDGE, width), 1)
    y_out = pick % EDGE
    place = pick // EDGE
    place = place % 2 * (lanes // 2) + place // 2
    outs = []
    for _, before, red, green, blue in state:
        opacity = 1.0 - before
        outs.append((opacity - red, green, blue * blue_one, opacity))
    for ch in range(4):
        for b in range(strip):
            index = place + b * (band // 2)
            low = jnp.take_along_axis(outs[0][ch], index, axis=1)
            high = jnp.take_along_axis(outs[1][ch], index, axis=1)
            both = jnp.where(y_out < 2, low, high)
            first, second = both[:EDGE], both[EDGE:]
            use_first = (y_out[:EDGE] == 0) | (y_out[:EDGE] == 3)
            out_ref[ch, pl.ds(b * EDGE, EDGE), :] = jnp.where(use_first, first, second)


def per_device(coefficients, keep_count, view_flip):
    tiles = lax.axis_size("tile")
    depths = lax.axis_size("depth")
    slots, _, _, columns, rows = coefficients.shape
    strip = columns // tiles
    band = rows // depths
    zblocks = tiles * depths
    vmem = pl.BlockSpec(memory_space=pltpu.VMEM)
    params = pltpu.CompilerParams(vmem_limit_bytes=8 * 1024 * 1024)
    lanes = strip * band
    inputs = (coefficients.reshape(slots, columns, rows), keep_count.reshape(columns, rows))
    outgoing, sign = pl.pallas_call(
        lambda *refs: pack_kernel(*refs, tiles=tiles, depths=depths),
        out_shape=[
            jax.ShapeDtypeStruct((zblocks * 5, lanes), jnp.float32),
            jax.ShapeDtypeStruct((2 * EDGE, lanes), jnp.float32),
        ],
        in_specs=[pl.BlockSpec(memory_space=pltpu.SMEM)] + [pl.BlockSpec(memory_space=pltpu.HBM)] * 2,
        out_specs=[vmem, vmem],
        scratch_shapes=[
            pltpu.VMEM((slots, columns, rows), jnp.float32),
            pltpu.VMEM((columns, rows), jnp.int32),
            pltpu.SemaphoreType.DMA((1 + slots,)),
        ],
        compiler_params=params,
        name="pack",
    )(view_flip, *(pltpu.with_memory_space_constraint(x, pltpu.HBM) for x in inputs))
    sent = outgoing.reshape(zblocks, 5, 1, lanes)
    falling = [[d * tiles + t for d in reversed(range(depths)) for t in range(tiles)]]
    arrived = lax.all_to_all(
        sent, ("depth", "tile"), split_axis=0, concat_axis=0, tiled=True, axis_index_groups=falling
    )
    return pl.pallas_call(
        lambda *refs: render_kernel(
            *refs, strip=strip, band=band, samples=EDGE * zblocks, tiles=tiles, depths=depths
        ),
        out_shape=jax.ShapeDtypeStruct((4, strip * EDGE, band * EDGE), jnp.float32),
        in_specs=[vmem, vmem],
        out_specs=vmem,
        scratch_shapes=[pltpu.VMEM((slots, zblocks, lanes), jnp.float32)],
        compiler_params=params,
        name="render",
    )(sign, arrived.reshape(outgoing.shape))


def solution(mesh):
    placed = (P(None, "depth", "tile", None, None), P("depth", "tile", None, None), P("tile"))
    return jax.shard_map(
        per_device, mesh=mesh, in_specs=placed, out_specs=P(None, "tile", "depth"), check_vma=False
    )
```

```python
import math

import jax
import jax.numpy as jnp
from jax import lax
from jax.experimental import pallas as pl
from jax.experimental.pallas import tpu as pltpu
from jax.sharding import PartitionSpec as P

LOG2E = math.log2(math.e)
EDGE = 4


def cosine(frequency, position):
    factor = 0.5 if frequency == 0 else math.sqrt(0.5)
    return factor * math.cos(math.pi * (2 * position + 1) * frequency / 8.0)


def swap_halves(values):
    half = values.shape[1] // 2
    if values.shape[1] % 128 == 0:
        return pltpu.roll(values, half, 1)
    return jnp.concatenate([values[:, half:], values[:, :half]], axis=1)


def listed_at(t, d, tiles, depths):
    return (tiles - 1 - t) * depths + depths - 1 - d


def pack_kernel(
    flip_ref, coef_hbm, keep_hbm, out_ref, sign_ref, coef_ref, keep_ref, rows_ref, arrival, *, tiles, depths
):
    _, columns, rows = coef_ref.shape
    strip = columns // tiles
    band = rows // depths
    fetch_keep = pltpu.make_async_copy(keep_hbm, keep_ref, arrival.at[8])
    fetches = [pltpu.make_async_copy(coef_hbm.at[k], coef_ref.at[k], arrival.at[k]) for k in range(8)]
    fetches.append(fetch_keep)
    for fetch in fetches:
        fetch.start()
    for fetch in fetches:
        fetch.wait()
    lane = lax.broadcasted_iota(jnp.int32, (tiles, rows), 1)
    even = lane % 2 == 0

    def take(values, index):
        return jnp.take_along_axis(values, index, axis=1)

    other = lane + 1 - 2 * (lane % 2)
    sign_ref[...] = jnp.full(sign_ref.shape, 1 - 2 * flip_ref[0], jnp.int32).astype(jnp.float32)
    half = strip * band // 2
    parity = lane // half % 2
    column = lane // (band // 2) % strip
    source = lane % (band // 2) * 2 + parity
    mine = [pl.ds(b, tiles, stride=strip) for b in range(strip)]
    keep = [keep_ref[rows_b, :] for rows_b in mine]
    for q in (1, 2, 3, 4, 0):
        packed = [coef_ref[q, rows_b, :] for rows_b in mine]
        if q > 0:
            turned = [take(coef_ref[8 - q, rows_b, :], other) for rows_b in mine]
            packed = [jnp.where(keep[b] > q, packed[b], turned[b]) for b in range(strip)]
        if q == 4:
            packed = [jnp.where(even, packed[b], (9 - keep[b]).astype(jnp.float32)) for b in range(strip)]
        for d in range(depths):
            gathered = [take(packed[b], source + d * band) for b in range(strip)]
            merged = gathered[0]
            for b in range(1, strip):
                merged = jnp.where(column == b, gathered[b], merged)
            rows_ref[d, q] = merged[:, : 2 * half]
    for d in range(depths):
        for t in range(tiles):
            out_ref[pl.ds(listed_at(t, d, tiles, depths) * 5, 5), :] = rows_ref[d, :, t, :]


def unpack(packed_ref, coef_ref):
    zblocks, lanes = packed_ref.shape[0] // 5, packed_ref.shape[1]
    first = lax.broadcasted_iota(jnp.int32, (zblocks, lanes), 1) < lanes // 2
    row = [packed_ref[pl.ds(q, zblocks, stride=5), :] for q in range(5)]
    turned = [None] + [swap_halves(row[q]) for q in (1, 2, 3, 4)]
    keep = jnp.where(first, turned[4], 9.0 - row[4])
    slot = [row[0]] + [jnp.where(keep > q, row[q], 0.0) for q in (1, 2, 3)]
    slot.append(jnp.where(keep > 4, jnp.where(first, row[4], turned[4]), 0.0))
    slot += [jnp.where(keep > k, turned[8 - k], 0.0) for k in (5, 6, 7)]
    for k in range(8):
        coef_ref[k] = slot[k]


def render_kernel(sign_ref, packed_ref, out_ref, coef_ref, *, strip, band, samples, tiles, depths):
    unpack(packed_ref, coef_ref)
    slots, zblocks, lanes = coef_ref.shape
    sign = sign_ref[...]
    flipped = jnp.max(sign) < 0.0
    b1 = [cosine(1, i) for i in range(EDGE)]
    row = lax.broadcasted_iota(jnp.int32, (2 * EDGE, lanes), 0)
    x = row % EDGE
    y = row // EDGE

    def table(position, values):
        result = jnp.full((2 * EDGE, lanes), values[0], jnp.float32)
        for i in range(1, len(values)):
            result = jnp.where(position == i, jnp.float32(values[i]), result)
        return result

    x1 = table(x, b1)
    x2 = table(x, [cosine(2, i) for i in range(EDGE)])
    y1 = table(y, b1[:2])
    y2 = table(y, [cosine(2, i) for i in range(2)])
    c_dc = 0.125 * LOG2E
    c_x1 = (0.25 * LOG2E) * x1
    c_x2 = (0.25 * LOG2E) * x2
    c_y1 = (0.25 * LOG2E) * y1
    c_y2 = (0.25 * LOG2E) * y2
    c_xy = (0.5 * LOG2E) * x1 * y1
    c_z = jnp.full((2 * EDGE, lanes), 0.25 * LOG2E * b1[0], jnp.float32) * sign
    c_zy = (0.5 * LOG2E * b1[0]) * y1 * sign
    ratio = b1[1] / b1[0]
    blue_one = 2.0**-20
    blue_factor = blue_one * math.exp(-1.5)
    fade = -1.5 / samples

    def block(step, state):
        source = jnp.where(flipped, zblocks - 1 - step, step)
        zb = listed_at(source % tiles, source // tiles, tiles, depths)
        a = [
            jnp.broadcast_to(coef_ref[k, pl.ds(zb, 1), :], (2 * EDGE, lanes)) for k in range(slots)
        ]
        even = a[0] * c_dc + a[2] * c_x1 + a[4] * c_y2 + a[6] * c_x2
        odd = a[1] * c_y1 + a[5] * c_xy
        g_even = a[3] * c_z
        g_odd = a[7] * c_zy
        halves = []
        for h in range(2):
            depth, before, red, green, blue = state[h]
            base = even + odd if h == 0 else even - odd
            g = g_even + g_odd if h == 0 else g_even - g_odd
            near = g * ratio
            for f in (base + g, base + near, base - near, base - g):
                v = jnp.exp2(f)
                one_u = 1.0 + v * v
                depth = depth + jnp.log2(one_u)
                after = jnp.exp2(fade * depth)
                weight = before - after
                before = after
                blue_u = blue_one + blue_factor * v
                shared = weight / (one_u * blue_u)
                red = red + shared * blue_u
                green = green + weight * jnp.exp2(f * (f * (-1.0 / LOG2E)))
                blue = blue + shared * one_u
            halves.append((depth, before, red, green, blue))
        return tuple(halves)

    zero = jnp.zeros((2 * EDGE, lanes), jnp.float32)
    one = jnp.ones((2 * EDGE, lanes), jnp.float32)
    start = (zero, one, zero, zero, zero)
    state = lax.fori_loop(0, zblocks, block, (start, start), unroll=16)

    width = band * EDGE
    pick = lax.broadcasted_iota(jnp.int32, (2 * EDGE, width), 1)
    y_out = pick % EDGE
    place = pick // EDGE
    place = place % 2 * (lanes // 2) + place // 2
    outs = []
    for _, before, red, green, blue in state:
        opacity = 1.0 - before
        outs.append((opacity - red, green, blue * blue_one, opacity))
    for ch in range(4):
        for b in range(strip):
            index = place + b * (band // 2)
            low = jnp.take_along_axis(outs[0][ch], index, axis=1)
            high = jnp.take_along_axis(outs[1][ch], index, axis=1)
            both = jnp.where(y_out < 2, low, high)
            first, second = both[:EDGE], both[EDGE:]
            use_first = (y_out[:EDGE] == 0) | (y_out[:EDGE] == 3)
            out_ref[ch, pl.ds(b * EDGE, EDGE), :] = jnp.where(use_first, first, second)


def per_device(coefficients, keep_count, view_flip):
    tiles = lax.axis_size("tile")
    depths = lax.axis_size("depth")
    slots, _, _, columns, rows = coefficients.shape
    strip = columns // tiles
    band = rows // depths
    zblocks = tiles * depths
    vmem = pl.BlockSpec(memory_space=pltpu.VMEM)
    params = pltpu.CompilerParams(vmem_limit_bytes=8 * 1024 * 1024)
    lanes = strip * band
    inputs = (coefficients.reshape(slots, columns, rows), keep_count.reshape(columns, rows))
    outgoing, sign = pl.pallas_call(
        lambda *refs: pack_kernel(*refs, tiles=tiles, depths=depths),
        out_shape=[
            jax.ShapeDtypeStruct((zblocks * 5, lanes), jnp.float32),
            jax.ShapeDtypeStruct((2 * EDGE, lanes), jnp.float32),
        ],
        in_specs=[pl.BlockSpec(memory_space=pltpu.SMEM)] + [pl.BlockSpec(memory_space=pltpu.HBM)] * 2,
        out_specs=[vmem, vmem],
        scratch_shapes=[
            pltpu.VMEM((slots, columns, rows), jnp.float32),
            pltpu.VMEM((columns, rows), jnp.int32),
            pltpu.VMEM((depths, 5, tiles, lanes), jnp.float32),
            pltpu.SemaphoreType.DMA((1 + slots,)),
        ],
        compiler_params=params,
        name="pack",
    )(view_flip, *(pltpu.with_memory_space_constraint(x, pltpu.HBM) for x in inputs))
    sent = outgoing.reshape(zblocks, 5, 1, lanes)
    devices = [(t, d) for d in range(depths) for t in range(tiles)]
    listed = sorted(range(zblocks), key=lambda i: listed_at(*devices[i], tiles, depths))
    arrived = lax.all_to_all(
        sent, ("depth", "tile"), split_axis=0, concat_axis=0, tiled=True, axis_index_groups=[listed]
    )
    return pl.pallas_call(
        lambda *refs: render_kernel(
            *refs, strip=strip, band=band, samples=EDGE * zblocks, tiles=tiles, depths=depths
        ),
        out_shape=jax.ShapeDtypeStruct((4, strip * EDGE, band * EDGE), jnp.float32),
        in_specs=[vmem, vmem],
        out_specs=vmem,
        scratch_shapes=[pltpu.VMEM((slots, zblocks, lanes), jnp.float32)],
        compiler_params=params,
        name="render",
    )(sign, arrived.reshape(outgoing.shape))


def solution(mesh):
    placed = (P(None, "depth", "tile", None, None), P("depth", "tile", None, None), P("tile"))
    return jax.shard_map(
        per_device, mesh=mesh, in_specs=placed, out_specs=P(None, "tile", "depth"), check_vma=False
    )
```

```python
import math

import jax
import jax.numpy as jnp
from jax import lax
from jax.experimental import pallas as pl
from jax.experimental.pallas import tpu as pltpu
from jax.sharding import PartitionSpec as P

LOG2E = math.log2(math.e)
EDGE = 4


def cosine(frequency, position):
    factor = 0.5 if frequency == 0 else math.sqrt(0.5)
    return factor * math.cos(math.pi * (2 * position + 1) * frequency / 8.0)


def swap_halves(values):
    half = values.shape[1] // 2
    if values.shape[1] % 128 == 0:
        return pltpu.roll(values, half, 1)
    return jnp.concatenate([values[:, half:], values[:, :half]], axis=1)


def listed_at(t, d, tiles, depths):
    turned, size = 0, 1
    while 2 * size <= depths:
        turned = turned + d // size % 2 * (depths // (2 * size))
        size *= 2
    if size != depths:
        turned = d
    return tiles * depths - 1 - turned * tiles - t


def pack_kernel(
    flip_ref, coef_hbm, keep_hbm, out_ref, sign_ref, coef_ref, keep_ref, rows_ref, arrival, *, tiles, depths
):
    _, columns, rows = coef_ref.shape
    strip = columns // tiles
    band = rows // depths
    moves = ((coef_hbm, coef_ref), (keep_hbm, keep_ref))
    fetches = [pltpu.make_async_copy(a, b, arrival.at[i]) for i, (a, b) in enumerate(moves)]
    for fetch in fetches:
        fetch.start()
    for fetch in fetches:
        fetch.wait()
    lane = lax.broadcasted_iota(jnp.int32, (tiles, rows), 1)
    even = lane % 2 == 0

    def take(values, index):
        return jnp.take_along_axis(values, index, axis=1)

    other = lane + 1 - 2 * (lane % 2)
    packed = []
    for b in range(strip):
        mine = pl.ds(b, tiles, stride=strip)
        keep = keep_ref[mine, :]
        slot = [coef_ref[k, mine, :] for k in range(8)]
        result = [slot[0]]
        for q in (1, 2, 3, 4):
            result.append(jnp.where(keep > q, slot[q], take(slot[8 - q], other)))
        result[4] = jnp.where(even, result[4], (9 - keep).astype(jnp.float32))
        packed.append(result)
    sign_ref[...] = jnp.full(sign_ref.shape, 1 - 2 * flip_ref[0], jnp.int32).astype(jnp.float32)
    half = strip * band // 2
    parity = lane // half % 2
    column = lane // (band // 2) % strip
    source = lane % (band // 2) * 2 + parity
    for d in range(depths):
        for q in range(5):
            gathered = [take(packed[b][q], source + d * band) for b in range(strip)]
            merged = gathered[0]
            for b in range(1, strip):
                merged = jnp.where(column == b, gathered[b], merged)
            rows_ref[d, q] = merged[:, : 2 * half]


    for d in range(depths):
        for t in range(tiles):
            out_ref[listed_at(t, d, tiles, depths), :, 0, :] = rows_ref[d, :, t, :]


def unpack(packed_ref, coef_ref):
    zblocks, _, _, lanes = packed_ref.shape
    first = lax.broadcasted_iota(jnp.int32, (zblocks, lanes), 1) < lanes // 2
    row = [packed_ref[:, q, 0, :] for q in range(5)]
    turned = [None] + [swap_halves(row[q]) for q in (1, 2, 3, 4)]
    keep = jnp.where(first, turned[4], 9.0 - row[4])
    slot = [row[0]] + [jnp.where(keep > q, row[q], 0.0) for q in (1, 2, 3)]
    slot.append(jnp.where(keep > 4, jnp.where(first, row[4], turned[4]), 0.0))
    slot += [jnp.where(keep > k, turned[8 - k], 0.0) for k in (5, 6, 7)]
    for k in range(8):
        coef_ref[k] = slot[k]


def render_kernel(sign_ref, packed_ref, out_ref, coef_ref, *, strip, band, samples, tiles, depths):
    unpack(packed_ref, coef_ref)
    slots, zblocks, lanes = coef_ref.shape
    sign = sign_ref[...]
    flipped = jnp.max(sign) < 0.0
    b1 = [cosine(1, i) for i in range(EDGE)]
    row = lax.broadcasted_iota(jnp.int32, (2 * EDGE, lanes), 0)
    x = row % EDGE
    y = row // EDGE

    def table(position, values):
        result = jnp.full((2 * EDGE, lanes), values[0], jnp.float32)
        for i in range(1, len(values)):
            result = jnp.where(position == i, jnp.float32(values[i]), result)
        return result

    x1 = table(x, b1)
    x2 = table(x, [cosine(2, i) for i in range(EDGE)])
    y1 = table(y, b1[:2])
    y2 = table(y, [cosine(2, i) for i in range(2)])
    c_dc = 0.125 * LOG2E
    c_x1 = (0.25 * LOG2E) * x1
    c_x2 = (0.25 * LOG2E) * x2
    c_y1 = (0.25 * LOG2E) * y1
    c_y2 = (0.25 * LOG2E) * y2
    c_xy = (0.5 * LOG2E) * x1 * y1
    c_z = jnp.full((2 * EDGE, lanes), 0.25 * LOG2E * b1[0], jnp.float32) * sign
    c_zy = (0.5 * LOG2E * b1[0]) * y1 * sign
    ratio = b1[1] / b1[0]
    blue_one = 2.0**-20
    blue_factor = blue_one * math.exp(-1.5)
    fade = -1.5 / samples

    def block(step, state):
        source = jnp.where(flipped, zblocks - 1 - step, step)
        zb = listed_at(source % tiles, source // tiles, tiles, depths)
        a = [
            jnp.broadcast_to(coef_ref[k, pl.ds(zb, 1), :], (2 * EDGE, lanes)) for k in range(slots)
        ]
        even = a[0] * c_dc + a[2] * c_x1 + a[4] * c_y2 + a[6] * c_x2
        odd = a[1] * c_y1 + a[5] * c_xy
        g_even = a[3] * c_z
        g_odd = a[7] * c_zy
        halves = []
        for h in range(2):
            depth, before, red, green, blue = state[h]
            base = even + odd if h == 0 else even - odd
            g = g_even + g_odd if h == 0 else g_even - g_odd
            near = g * ratio
            for f in (base + g, base + near, base - near, base - g):
                v = jnp.exp2(f)
                one_u = 1.0 + v * v
                depth = depth + jnp.log2(one_u)
                after = jnp.exp2(fade * depth)
                weight = before - after
                before = after
                blue_u = blue_one + blue_factor * v
                shared = weight / (one_u * blue_u)
                red = red + shared * blue_u
                green = green + weight * jnp.exp2(f * (f * (-1.0 / LOG2E)))
                blue = blue + shared * one_u
            halves.append((depth, before, red, green, blue))
        return tuple(halves)

    zero = jnp.zeros((2 * EDGE, lanes), jnp.float32)
    one = jnp.ones((2 * EDGE, lanes), jnp.float32)
    start = (zero, one, zero, zero, zero)
    state = lax.fori_loop(0, zblocks, block, (start, start), unroll=16)

    width = band * EDGE
    pick = lax.broadcasted_iota(jnp.int32, (2 * EDGE, width), 1)
    y_out = pick % EDGE
    place = pick // EDGE
    place = place % 2 * (lanes // 2) + place // 2
    outs = []
    for _, before, red, green, blue in state:
        opacity = 1.0 - before
        outs.append((opacity - red, green, blue * blue_one, opacity))
    for ch in range(4):
        for b in range(strip):
            index = place + b * (band // 2)
            low = jnp.take_along_axis(outs[0][ch], index, axis=1)
            high = jnp.take_along_axis(outs[1][ch], index, axis=1)
            both = jnp.where(y_out < 2, low, high)
            first, second = both[:EDGE], both[EDGE:]
            use_first = (y_out[:EDGE] == 0) | (y_out[:EDGE] == 3)
            out_ref[ch, pl.ds(b * EDGE, EDGE), :] = jnp.where(use_first, first, second)


def per_device(coefficients, keep_count, view_flip):
    tiles = lax.axis_size("tile")
    depths = lax.axis_size("depth")
    slots, _, _, columns, rows = coefficients.shape
    strip = columns // tiles
    band = rows // depths
    zblocks = tiles * depths
    vmem = pl.BlockSpec(memory_space=pltpu.VMEM)
    params = pltpu.CompilerParams(vmem_limit_bytes=8 * 1024 * 1024)
    lanes = strip * band
    inputs = (coefficients.reshape(slots, columns, rows), keep_count.reshape(columns, rows))
    outgoing, sign = pl.pallas_call(
        lambda *refs: pack_kernel(*refs, tiles=tiles, depths=depths),
        out_shape=[
            jax.ShapeDtypeStruct((zblocks, 5, 1, lanes), jnp.float32),
            jax.ShapeDtypeStruct((2 * EDGE, lanes), jnp.float32),
        ],
        in_specs=[pl.BlockSpec(memory_space=pltpu.SMEM)] + [pl.BlockSpec(memory_space=pltpu.HBM)] * 2,
        out_specs=[vmem, vmem],
        scratch_shapes=[
            pltpu.VMEM((slots, columns, rows), jnp.float32),
            pltpu.VMEM((columns, rows), jnp.int32),
            pltpu.VMEM((depths, 5, tiles, lanes), jnp.float32),
            pltpu.SemaphoreType.DMA((2,)),
        ],
        compiler_params=params,
        name="pack",
    )(view_flip, *(pltpu.with_memory_space_constraint(x, pltpu.HBM) for x in inputs))
    devices = [(t, d) for d in range(depths) for t in range(tiles)]
    listed = sorted(range(zblocks), key=lambda i: listed_at(*devices[i], tiles, depths))
    arrived = lax.all_to_all(
        outgoing, ("depth", "tile"), split_axis=0, concat_axis=0, tiled=True, axis_index_groups=[listed]
    )
    return pl.pallas_call(
        lambda *refs: render_kernel(
            *refs, strip=strip, band=band, samples=EDGE * zblocks, tiles=tiles, depths=depths
        ),
        out_shape=jax.ShapeDtypeStruct((4, strip * EDGE, band * EDGE), jnp.float32),
        in_specs=[vmem, vmem],
        out_specs=vmem,
        scratch_shapes=[pltpu.VMEM((slots, zblocks, lanes), jnp.float32)],
        compiler_params=params,
        name="render",
    )(sign, arrived)


def solution(mesh):
    placed = (P(None, "depth", "tile", None, None), P("depth", "tile", None, None), P("tile"))
    return jax.shard_map(
        per_device, mesh=mesh, in_specs=placed, out_specs=P(None, "tile", "depth"), check_vma=False
    )
```

```python
import math

import jax
import jax.numpy as jnp
from jax import lax
from jax.experimental import pallas as pl
from jax.experimental.pallas import tpu as pltpu
from jax.sharding import PartitionSpec as P

LOG2E = math.log2(math.e)
EDGE = 4


def cosine(frequency, position):
    factor = 0.5 if frequency == 0 else math.sqrt(0.5)
    return factor * math.cos(math.pi * (2 * position + 1) * frequency / 8.0)


def swap_halves(values):
    half = values.shape[1] // 2
    if values.shape[1] % 128 == 0:
        return pltpu.roll(values, half, 1)
    return jnp.concatenate([values[:, half:], values[:, :half]], axis=1)


def listed_at(t, d, tiles, depths):
    turned, size = 0, 1
    while 2 * size <= depths:
        turned = turned + d // size % 2 * (depths // (2 * size))
        size *= 2
    if size != depths:
        turned = d
    return tiles * depths - 1 - turned * tiles - t


def pack_kernel(
    flip_ref, coef_hbm, keep_hbm, out_ref, sign_ref, coef_ref, keep_ref, rows_ref, arrival, *, tiles, depths
):
    _, columns, rows = coef_ref.shape
    strip = columns // tiles
    band = rows // depths
    moves = ((coef_hbm, coef_ref), (keep_hbm, keep_ref))
    fetches = [pltpu.make_async_copy(a, b, arrival.at[i]) for i, (a, b) in enumerate(moves)]
    for fetch in fetches:
        fetch.start()
    for fetch in fetches:
        fetch.wait()
    lane = lax.broadcasted_iota(jnp.int32, (tiles, rows), 1)
    even = lane % 2 == 0

    def take(values, index):
        return jnp.take_along_axis(values, index, axis=1)

    other = lane + 1 - 2 * (lane % 2)
    packed = []
    for b in range(strip):
        mine = pl.ds(b, tiles, stride=strip)
        keep = keep_ref[mine, :]
        slot = [coef_ref[k, mine, :] for k in range(8)]
        result = [slot[0]]
        for q in (1, 2, 3, 4):
            result.append(jnp.where(keep > q, slot[q], take(slot[8 - q], other)))
        result[4] = jnp.where(even, result[4], (9 - keep).astype(jnp.float32))
        packed.append(result)
    sign_ref[...] = jnp.full(sign_ref.shape, 1 - 2 * flip_ref[0], jnp.int32).astype(jnp.float32)
    half = strip * band // 2
    parity = lane // half % 2
    column = lane // (band // 2) % strip
    source = lane % (band // 2) * 2 + parity
    for d in range(depths):
        for q in range(5):
            gathered = [take(packed[b][q], source + d * band) for b in range(strip)]
            merged = gathered[0]
            for b in range(1, strip):
                merged = jnp.where(column == b, gathered[b], merged)
            rows_ref[d, q] = merged[:, : 2 * half]


    for d in range(depths):
        for t in range(tiles):
            out_ref[listed_at(t, d, tiles, depths), :, 0, :] = rows_ref[d, :, t, :]


def unpack(packed_ref, coef_ref):
    zblocks, _, _, lanes = packed_ref.shape
    first = lax.broadcasted_iota(jnp.int32, (zblocks, lanes), 1) < lanes // 2
    row = [packed_ref[:, q, 0, :] for q in range(5)]
    turned = [None] + [swap_halves(row[q]) for q in (1, 2, 3, 4)]
    keep = jnp.where(first, turned[4], 9.0 - row[4])
    slot = [row[0]] + [jnp.where(keep > q, row[q], 0.0) for q in (1, 2, 3)]
    slot.append(jnp.where(keep > 4, jnp.where(first, row[4], turned[4]), 0.0))
    slot += [jnp.where(keep > k, turned[8 - k], 0.0) for k in (5, 6, 7)]
    for k in range(8):
        coef_ref[k] = slot[k]


def render_kernel(sign_ref, packed_ref, out_ref, coef_ref, *, strip, band, samples, tiles, depths):
    unpack(packed_ref, coef_ref)
    slots, zblocks, lanes = coef_ref.shape
    sign = sign_ref[...]
    flipped = jnp.max(sign) < 0.0
    b1 = [cosine(1, i) for i in range(EDGE)]
    row = lax.broadcasted_iota(jnp.int32, (2 * EDGE, lanes), 0)
    x = row % EDGE
    y = row // EDGE

    def table(position, values):
        result = jnp.full((2 * EDGE, lanes), values[0], jnp.float32)
        for i in range(1, len(values)):
            result = jnp.where(position == i, jnp.float32(values[i]), result)
        return result

    x1 = table(x, b1)
    x2 = table(x, [cosine(2, i) for i in range(EDGE)])
    y1 = table(y, b1[:2])
    y2 = table(y, [cosine(2, i) for i in range(2)])
    c_dc = 0.125 * LOG2E
    c_x1 = (0.25 * LOG2E) * x1
    c_x2 = (0.25 * LOG2E) * x2
    c_y1 = (0.25 * LOG2E) * y1
    c_y2 = (0.25 * LOG2E) * y2
    c_xy = (0.5 * LOG2E) * x1 * y1
    c_z = jnp.full((2 * EDGE, lanes), 0.25 * LOG2E * b1[0], jnp.float32) * sign
    c_zy = (0.5 * LOG2E * b1[0]) * y1 * sign
    ratio = b1[1] / b1[0]
    blue_one = 2.0**-20
    blue_factor = blue_one * math.exp(-1.5)
    fade = -1.5 / samples

    def block(step, state):
        source = jnp.where(flipped, zblocks - 1 - step, step)
        zb = listed_at(source % tiles, source // tiles, tiles, depths)
        a = [
            jnp.broadcast_to(coef_ref[k, pl.ds(zb, 1), :], (2 * EDGE, lanes)) for k in range(slots)
        ]
        even = a[0] * c_dc + a[2] * c_x1 + a[4] * c_y2 + a[6] * c_x2
        odd = a[1] * c_y1 + a[5] * c_xy
        g_even = a[3] * c_z
        g_odd = a[7] * c_zy
        halves = []
        for h in range(2):
            depth, before, red, green, blue = state[h]
            base = even + odd if h == 0 else even - odd
            g = g_even + g_odd if h == 0 else g_even - g_odd
            near = g * ratio
            for f in (base + g, base + near, base - near, base - g):
                v = jnp.exp2(f)
                one_u = 1.0 + v * v
                depth = depth + jnp.log2(one_u)
                after = jnp.exp2(fade * depth)
                weight = before - after
                before = after
                blue_u = blue_one + blue_factor * v
                shared = weight / (one_u * blue_u)
                red = red + shared * blue_u
                green = green + weight * jnp.exp2(f * (f * (-1.0 / LOG2E)))
                blue = blue + shared * one_u
            halves.append((depth, before, red, green, blue))
        return tuple(halves)

    zero = jnp.zeros((2 * EDGE, lanes), jnp.float32)
    one = jnp.ones((2 * EDGE, lanes), jnp.float32)
    start = (zero, one, zero, zero, zero)
    state = lax.fori_loop(0, zblocks, block, (start, start), unroll=32)

    width = band * EDGE
    pick = lax.broadcasted_iota(jnp.int32, (2 * EDGE, width), 1)
    y_out = pick % EDGE
    place = pick // EDGE
    place = place % 2 * (lanes // 2) + place // 2
    outs = []
    for _, before, red, green, blue in state:
        opacity = 1.0 - before
        outs.append((opacity - red, green, blue * blue_one, opacity))
    for ch in range(4):
        for b in range(strip):
            index = place + b * (band // 2)
            low = jnp.take_along_axis(outs[0][ch], index, axis=1)
            high = jnp.take_along_axis(outs[1][ch], index, axis=1)
            both = jnp.where(y_out < 2, low, high)
            first, second = both[:EDGE], both[EDGE:]
            use_first = (y_out[:EDGE] == 0) | (y_out[:EDGE] == 3)
            out_ref[ch, pl.ds(b * EDGE, EDGE), :] = jnp.where(use_first, first, second)


def per_device(coefficients, keep_count, view_flip):
    tiles = lax.axis_size("tile")
    depths = lax.axis_size("depth")
    slots, _, _, columns, rows = coefficients.shape
    strip = columns // tiles
    band = rows // depths
    zblocks = tiles * depths
    vmem = pl.BlockSpec(memory_space=pltpu.VMEM)
    params = pltpu.CompilerParams(vmem_limit_bytes=8 * 1024 * 1024)
    lanes = strip * band
    inputs = (coefficients.reshape(slots, columns, rows), keep_count.reshape(columns, rows))
    outgoing, sign = pl.pallas_call(
        lambda *refs: pack_kernel(*refs, tiles=tiles, depths=depths),
        out_shape=[
            jax.ShapeDtypeStruct((zblocks, 5, 1, lanes), jnp.float32),
            jax.ShapeDtypeStruct((2 * EDGE, lanes), jnp.float32),
        ],
        in_specs=[pl.BlockSpec(memory_space=pltpu.SMEM)] + [pl.BlockSpec(memory_space=pltpu.HBM)] * 2,
        out_specs=[vmem, vmem],
        scratch_shapes=[
            pltpu.VMEM((slots, columns, rows), jnp.float32),
            pltpu.VMEM((columns, rows), jnp.int32),
            pltpu.VMEM((depths, 5, tiles, lanes), jnp.float32),
            pltpu.SemaphoreType.DMA((2,)),
        ],
        compiler_params=params,
        name="pack",
    )(view_flip, *(pltpu.with_memory_space_constraint(x, pltpu.HBM) for x in inputs))
    devices = [(t, d) for d in range(depths) for t in range(tiles)]
    listed = sorted(range(zblocks), key=lambda i: listed_at(*devices[i], tiles, depths))
    arrived = lax.all_to_all(
        outgoing, ("depth", "tile"), split_axis=0, concat_axis=0, tiled=True, axis_index_groups=[listed]
    )
    return pl.pallas_call(
        lambda *refs: render_kernel(
            *refs, strip=strip, band=band, samples=EDGE * zblocks, tiles=tiles, depths=depths
        ),
        out_shape=jax.ShapeDtypeStruct((4, strip * EDGE, band * EDGE), jnp.float32),
        in_specs=[vmem, vmem],
        out_specs=vmem,
        scratch_shapes=[pltpu.VMEM((slots, zblocks, lanes), jnp.float32)],
        compiler_params=params,
        name="render",
    )(sign, arrived)


def solution(mesh):
    placed = (P(None, "depth", "tile", None, None), P("depth", "tile", None, None), P("tile"))
    return jax.shard_map(
        per_device, mesh=mesh, in_specs=placed, out_specs=P(None, "tile", "depth"), check_vma=False
    )
```

```python
import math

import jax
import jax.numpy as jnp
from jax import lax
from jax.experimental import pallas as pl
from jax.experimental.pallas import tpu as pltpu
from jax.sharding import PartitionSpec as P

LOG2E = math.log2(math.e)
EDGE = 4


def cosine(frequency, position):
    factor = 0.5 if frequency == 0 else math.sqrt(0.5)
    return factor * math.cos(math.pi * (2 * position + 1) * frequency / 8.0)


def swap_halves(values):
    half = values.shape[1] // 2
    if values.shape[1] % 128 == 0:
        return pltpu.roll(values, half, 1)
    return jnp.concatenate([values[:, half:], values[:, :half]], axis=1)


def listed_at(t, d, tiles, depths):
    turned, size = 0, 1
    while 2 * size <= depths:
        turned = turned + d // size % 2 * (depths // (2 * size))
        size *= 2
    if size != depths:
        turned = d
    return tiles * depths - 1 - turned * tiles - t


def pack_kernel(
    flip_ref, coef_hbm, keep_hbm, out_ref, sign_ref, coef_ref, keep_ref, rows_ref, arrival, *, tiles, depths
):
    _, columns, rows = coef_ref.shape
    strip = columns // tiles
    band = rows // depths
    moves = ((coef_hbm, coef_ref), (keep_hbm, keep_ref))
    fetches = [pltpu.make_async_copy(a, b, arrival.at[i]) for i, (a, b) in enumerate(moves)]
    for fetch in fetches:
        fetch.start()
    for fetch in fetches:
        fetch.wait()
    lane = lax.broadcasted_iota(jnp.int32, (tiles, rows), 1)
    even = lane % 2 == 0

    def take(values, index):
        return jnp.take_along_axis(values, index, axis=1)

    other = lane + 1 - 2 * (lane % 2)
    packed = []
    for b in range(strip):
        mine = pl.ds(b, tiles, stride=strip)
        keep = keep_ref[mine, :]
        slot = [coef_ref[k, mine, :] for k in range(8)]
        result = [slot[0]]
        for q in (1, 2, 3, 4):
            result.append(jnp.where(keep > q, slot[q], take(slot[8 - q], other)))
        result[4] = jnp.where(even, result[4], (9 - keep).astype(jnp.float32))
        packed.append(result)
    sign_ref[...] = jnp.full(sign_ref.shape, 1 - 2 * flip_ref[0], jnp.int32).astype(jnp.float32)
    half = strip * band // 2
    parity = lane // half % 2
    column = lane // (band // 2) % strip
    source = lane % (band // 2) * 2 + parity
    for d in range(depths):
        for q in range(5):
            gathered = [take(packed[b][q], source + d * band) for b in range(strip)]
            merged = gathered[0]
            for b in range(1, strip):
                merged = jnp.where(column == b, gathered[b], merged)
            rows_ref[d, q] = merged[:, : 2 * half]


    for d in range(depths):
        for t in range(tiles):
            out_ref[listed_at(t, d, tiles, depths), :, 0, :] = rows_ref[d, :, t, :]


def unpack(packed_ref, coef_ref):
    zblocks, lanes = packed_ref.shape[0] // 5, packed_ref.shape[1]
    first = lax.broadcasted_iota(jnp.int32, (zblocks, lanes), 1) < lanes // 2
    row = [packed_ref[pl.ds(q, zblocks, stride=5), :] for q in range(5)]
    turned = [None] + [swap_halves(row[q]) for q in (1, 2, 3, 4)]
    keep = jnp.where(first, turned[4], 9.0 - row[4])
    slot = [row[0]] + [jnp.where(keep > q, row[q], 0.0) for q in (1, 2, 3)]
    slot.append(jnp.where(keep > 4, jnp.where(first, row[4], turned[4]), 0.0))
    slot += [jnp.where(keep > k, turned[8 - k], 0.0) for k in (5, 6, 7)]
    for k in range(8):
        coef_ref[k] = slot[k]


def render_kernel(sign_ref, packed_ref, out_ref, coef_ref, sampled_ref, *, strip, band, samples, tiles, depths):
    unpack(packed_ref, coef_ref)
    slots, zblocks, lanes = coef_ref.shape
    sign = sign_ref[...]
    flipped = jnp.max(sign) < 0.0
    b1 = [cosine(1, i) for i in range(EDGE)]
    row = lax.broadcasted_iota(jnp.int32, (2 * EDGE, lanes), 0)
    x = row % EDGE
    y = row // EDGE

    def table(position, values):
        result = jnp.full((2 * EDGE, lanes), values[0], jnp.float32)
        for i in range(1, len(values)):
            result = jnp.where(position == i, jnp.float32(values[i]), result)
        return result

    x1 = table(x, b1)
    x2 = table(x, [cosine(2, i) for i in range(EDGE)])
    y1 = table(y, b1[:2])
    y2 = table(y, [cosine(2, i) for i in range(2)])
    c_dc = 0.125 * LOG2E
    c_x1 = (0.25 * LOG2E) * x1
    c_x2 = (0.25 * LOG2E) * x2
    c_y1 = (0.25 * LOG2E) * y1
    c_y2 = (0.25 * LOG2E) * y2
    c_xy = (0.5 * LOG2E) * x1 * y1
    c_z = jnp.full((2 * EDGE, lanes), 0.25 * LOG2E * b1[0], jnp.float32) * sign
    c_zy = (0.5 * LOG2E * b1[0]) * y1 * sign
    ratio = b1[1] / b1[0]
    blue_one = 2.0**-20
    blue_factor = blue_one * math.exp(-1.5)
    fade = -1.5 / samples

    def factors(step):
        source = jnp.where(flipped, zblocks - 1 - step, step)
        zb = listed_at(source % tiles, source // tiles, tiles, depths)
        a = [
            jnp.broadcast_to(coef_ref[k, pl.ds(zb, 1), :], (2 * EDGE, lanes)) for k in range(slots)
        ]
        even = a[0] * c_dc + a[2] * c_x1 + a[4] * c_y2 + a[6] * c_x2
        odd = a[1] * c_y1 + a[5] * c_xy
        g_even = a[3] * c_z
        g_odd = a[7] * c_zy
        result = []
        for h in range(2):
            base = even + odd if h == 0 else even - odd
            g = g_even + g_odd if h == 0 else g_even - g_odd
            near = g * ratio
            for f in (base + g, base + near, base - near, base - g):
                v = jnp.exp2(f)
                one_u = 1.0 + v * v
                blue_u = blue_one + blue_factor * v
                both = 1.0 / (one_u * blue_u)
                green = jnp.exp2(f * (f * (-1.0 / LOG2E)))
                result.append((jnp.log2(one_u), both * blue_u, green, both * one_u))
        return result

    blocks = 2 if zblocks % 2 == 0 else 1
    sampled_ref[...] = jnp.zeros_like(sampled_ref)

    def trip(number, state):
        state = [list(part) for part in state]
        for b in range(blocks):
            for h in range(2):
                depth, before, red, green, blue = state[h]
                for z in range(EDGE):
                    i = (b * 2 + h) * EDGE + z
                    depth = depth + sampled_ref[0, i]
                    after = jnp.exp2(fade * depth)
                    weight = before - after
                    before = after
                    red = red + weight * sampled_ref[1, i]
                    green = green + weight * sampled_ref[2, i]
                    blue = blue + weight * sampled_ref[3, i]
                state[h] = (depth, before, red, green, blue)
        for b in range(blocks):
            step = jnp.minimum(number * blocks + b, zblocks - 1)
            for i, sample in enumerate(factors(step)):
                for kind in range(4):
                    sampled_ref[kind, b * 2 * EDGE + i] = sample[kind]
        return tuple(tuple(part) for part in state)

    zero = jnp.zeros((2 * EDGE, lanes), jnp.float32)
    one = jnp.ones((2 * EDGE, lanes), jnp.float32)
    start = (zero, one, zero, zero, zero)
    state = lax.fori_loop(0, zblocks // blocks + 1, trip, (start, start))

    width = band * EDGE
    pick = lax.broadcasted_iota(jnp.int32, (2 * EDGE, width), 1)
    y_out = pick % EDGE
    place = pick // EDGE
    place = place % 2 * (lanes // 2) + place // 2
    outs = []
    for _, before, red, green, blue in state:
        opacity = 1.0 - before
        outs.append((opacity - red, green, blue * blue_one, opacity))
    for ch in range(4):
        for b in range(strip):
            index = place + b * (band // 2)
            low = jnp.take_along_axis(outs[0][ch], index, axis=1)
            high = jnp.take_along_axis(outs[1][ch], index, axis=1)
            both = jnp.where(y_out < 2, low, high)
            first, second = both[:EDGE], both[EDGE:]
            use_first = (y_out[:EDGE] == 0) | (y_out[:EDGE] == 3)
            out_ref[ch, pl.ds(b * EDGE, EDGE), :] = jnp.where(use_first, first, second)


def per_device(coefficients, keep_count, view_flip):
    tiles = lax.axis_size("tile")
    depths = lax.axis_size("depth")
    slots, _, _, columns, rows = coefficients.shape
    strip = columns // tiles
    band = rows // depths
    zblocks = tiles * depths
    vmem = pl.BlockSpec(memory_space=pltpu.VMEM)
    params = pltpu.CompilerParams(vmem_limit_bytes=8 * 1024 * 1024)
    lanes = strip * band
    inputs = (coefficients.reshape(slots, columns, rows), keep_count.reshape(columns, rows))
    outgoing, sign = pl.pallas_call(
        lambda *refs: pack_kernel(*refs, tiles=tiles, depths=depths),
        out_shape=[
            jax.ShapeDtypeStruct((zblocks, 5, 1, lanes), jnp.float32),
            jax.ShapeDtypeStruct((2 * EDGE, lanes), jnp.float32),
        ],
        in_specs=[pl.BlockSpec(memory_space=pltpu.SMEM)] + [pl.BlockSpec(memory_space=pltpu.HBM)] * 2,
        out_specs=[vmem, vmem],
        scratch_shapes=[
            pltpu.VMEM((slots, columns, rows), jnp.float32),
            pltpu.VMEM((columns, rows), jnp.int32),
            pltpu.VMEM((depths, 5, tiles, lanes), jnp.float32),
            pltpu.SemaphoreType.DMA((2,)),
        ],
        compiler_params=params,
        name="pack",
    )(view_flip, *(pltpu.with_memory_space_constraint(x, pltpu.HBM) for x in inputs))
    devices = [(t, d) for d in range(depths) for t in range(tiles)]
    listed = sorted(range(zblocks), key=lambda i: listed_at(*devices[i], tiles, depths))
    arrived = lax.all_to_all(
        outgoing, ("depth", "tile"), split_axis=0, concat_axis=0, tiled=True, axis_index_groups=[listed]
    )
    return pl.pallas_call(
        lambda *refs: render_kernel(
            *refs, strip=strip, band=band, samples=EDGE * zblocks, tiles=tiles, depths=depths
        ),
        out_shape=jax.ShapeDtypeStruct((4, strip * EDGE, band * EDGE), jnp.float32),
        in_specs=[vmem, vmem],
        out_specs=vmem,
        scratch_shapes=[
            pltpu.VMEM((slots, zblocks, lanes), jnp.float32),
            pltpu.VMEM((4, 4 * EDGE, 2 * EDGE, lanes), jnp.float32),
        ],
        compiler_params=params,
        name="render",
    )(sign, arrived.reshape(zblocks * 5, lanes))


def solution(mesh):
    placed = (P(None, "depth", "tile", None, None), P("depth", "tile", None, None), P("tile"))
    return jax.shard_map(
        per_device, mesh=mesh, in_specs=placed, out_specs=P(None, "tile", "depth"), check_vma=False
    )
```

```python
import math

import jax
import jax.numpy as jnp
from jax import lax
from jax.experimental import pallas as pl
from jax.experimental.pallas import tpu as pltpu
from jax.sharding import PartitionSpec as P

LOG2E = math.log2(math.e)
EDGE = 4


def cosine(frequency, position):
    factor = 0.5 if frequency == 0 else math.sqrt(0.5)
    return factor * math.cos(math.pi * (2 * position + 1) * frequency / 8.0)


def swap_halves(values):
    half = values.shape[1] // 2
    if values.shape[1] % 128 == 0:
        return pltpu.roll(values, half, 1)
    return jnp.concatenate([values[:, half:], values[:, :half]], axis=1)


def listed_at(t, d, tiles, depths):
    turned, size = 0, 1
    while 2 * size <= depths:
        turned = turned + d // size % 2 * (depths // (2 * size))
        size *= 2
    if size != depths:
        turned = d
    return tiles * depths - 1 - turned * tiles - t


def pack_kernel(
    flip_ref, coef_hbm, keep_hbm, out_ref, sign_ref, coef_ref, keep_ref, rows_ref, arrival, *, tiles, depths
):
    _, columns, rows = coef_ref.shape
    strip = columns // tiles
    band = rows // depths
    moves = ((coef_hbm, coef_ref), (keep_hbm, keep_ref))
    fetches = [pltpu.make_async_copy(a, b, arrival.at[i]) for i, (a, b) in enumerate(moves)]
    for fetch in fetches:
        fetch.start()
    for fetch in fetches:
        fetch.wait()
    lane = lax.broadcasted_iota(jnp.int32, (tiles, rows), 1)
    even = lane % 2 == 0

    def take(values, index):
        return jnp.take_along_axis(values, index, axis=1)

    other = lane + 1 - 2 * (lane % 2)
    packed = []
    for b in range(strip):
        mine = pl.ds(b, tiles, stride=strip)
        keep = keep_ref[mine, :]
        slot = [coef_ref[k, mine, :] for k in range(8)]
        result = [slot[0]]
        for q in (1, 2, 3, 4):
            result.append(jnp.where(keep > q, slot[q], take(slot[8 - q], other)))
        result[4] = jnp.where(even, result[4], (9 - keep).astype(jnp.float32))
        packed.append(result)
    sign_ref[...] = jnp.full(sign_ref.shape, 1 - 2 * flip_ref[0], jnp.int32).astype(jnp.float32)
    half = strip * band // 2
    parity = lane // half % 2
    column = lane // (band // 2) % strip
    source = lane % (band // 2) * 2 + parity
    for d in range(depths):
        for q in range(5):
            gathered = [take(packed[b][q], source + d * band) for b in range(strip)]
            merged = gathered[0]
            for b in range(1, strip):
                merged = jnp.where(column == b, gathered[b], merged)
            rows_ref[d, q] = merged[:, : 2 * half]


    for d in range(depths):
        for t in range(tiles):
            out_ref[listed_at(t, d, tiles, depths), :, 0, :] = rows_ref[d, :, t, :]


def unpack(packed_ref, coef_ref):
    zblocks, lanes = packed_ref.shape[0] // 5, packed_ref.shape[1]
    first = lax.broadcasted_iota(jnp.int32, (zblocks, lanes), 1) < lanes // 2
    row = [packed_ref[pl.ds(q, zblocks, stride=5), :] for q in range(5)]
    turned = [None] + [swap_halves(row[q]) for q in (1, 2, 3, 4)]
    keep = jnp.where(first, turned[4], 9.0 - row[4])
    slot = [row[0]] + [jnp.where(keep > q, row[q], 0.0) for q in (1, 2, 3)]
    slot.append(jnp.where(keep > 4, jnp.where(first, row[4], turned[4]), 0.0))
    slot += [jnp.where(keep > k, turned[8 - k], 0.0) for k in (5, 6, 7)]
    for k in range(8):
        coef_ref[k] = slot[k]


def render_kernel(sign_ref, packed_ref, out_ref, coef_ref, *, strip, band, samples, tiles, depths):
    unpack(packed_ref, coef_ref)
    slots, zblocks, lanes = coef_ref.shape
    sign = sign_ref[...]
    flipped = jnp.max(sign) < 0.0
    b1 = [cosine(1, i) for i in range(EDGE)]
    row = lax.broadcasted_iota(jnp.int32, (2 * EDGE, lanes), 0)
    x = row % EDGE
    y = row // EDGE

    def table(position, values):
        result = jnp.full((2 * EDGE, lanes), values[0], jnp.float32)
        for i in range(1, len(values)):
            result = jnp.where(position == i, jnp.float32(values[i]), result)
        return result

    x1 = table(x, b1)
    x2 = table(x, [cosine(2, i) for i in range(EDGE)])
    y1 = table(y, b1[:2])
    y2 = table(y, [cosine(2, i) for i in range(2)])
    c_dc = 0.125 * LOG2E
    c_x1 = (0.25 * LOG2E) * x1
    c_x2 = (0.25 * LOG2E) * x2
    c_y1 = (0.25 * LOG2E) * y1
    c_y2 = (0.25 * LOG2E) * y2
    c_xy = (0.5 * LOG2E) * x1 * y1
    c_z = jnp.full((2 * EDGE, lanes), 0.25 * LOG2E * b1[0], jnp.float32) * sign
    c_zy = (0.5 * LOG2E * b1[0]) * y1 * sign
    ratio = b1[1] / b1[0]
    blue_one = 2.0**-20
    blue_factor = blue_one * math.exp(-1.5)
    fade = -1.5 / samples

    def block(step, state):
        source = jnp.where(flipped, zblocks - 1 - step, step)
        zb = listed_at(source % tiles, source // tiles, tiles, depths)
        a = [
            jnp.broadcast_to(coef_ref[k, pl.ds(zb, 1), :], (2 * EDGE, lanes)) for k in range(slots)
        ]
        even = a[0] * c_dc + a[2] * c_x1 + a[4] * c_y2 + a[6] * c_x2
        odd = a[1] * c_y1 + a[5] * c_xy
        g_even = a[3] * c_z
        g_odd = a[7] * c_zy
        halves = []
        for h in range(2):
            depth, before, red, green, blue = state[h]
            base = even + odd if h == 0 else even - odd
            g = g_even + g_odd if h == 0 else g_even - g_odd
            near = g * ratio
            for f in (base + g, base + near, base - near, base - g):
                v = jnp.exp2(f)
                one_u = 1.0 + v * v
                depth = depth + jnp.log2(one_u)
                after = jnp.exp2(fade * depth)
                weight = before - after
                before = after
                blue_u = blue_one + blue_factor * v
                shared = weight / (one_u * blue_u)
                red = red + shared * blue_u
                green = green + weight * jnp.exp2(f * (f * (-1.0 / LOG2E)))
                blue = blue + shared * one_u
            halves.append((depth, before, red, green, blue))
        return tuple(halves)

    zero = jnp.zeros((2 * EDGE, lanes), jnp.float32)
    one = jnp.ones((2 * EDGE, lanes), jnp.float32)
    start = (zero, one, zero, zero, zero)
    state = lax.fori_loop(0, zblocks, block, (start, start), unroll=16)

    width = band * EDGE
    pick = lax.broadcasted_iota(jnp.int32, (2 * EDGE, width), 1)
    y_out = pick % EDGE
    place = pick // EDGE
    place = place % 2 * (lanes // 2) + place // 2
    outs = []
    for _, before, red, green, blue in state:
        opacity = 1.0 - before
        outs.append((opacity - red, green, blue * blue_one, opacity))
    for ch in range(4):
        for b in range(strip):
            index = place + b * (band // 2)
            low = jnp.take_along_axis(outs[0][ch], index, axis=1)
            high = jnp.take_along_axis(outs[1][ch], index, axis=1)
            both = jnp.where(y_out < 2, low, high)
            first, second = both[:EDGE], both[EDGE:]
            use_first = (y_out[:EDGE] == 0) | (y_out[:EDGE] == 3)
            out_ref[ch, pl.ds(b * EDGE, EDGE), :] = jnp.where(use_first, first, second)


def per_device(coefficients, keep_count, view_flip):
    tiles = lax.axis_size("tile")
    depths = lax.axis_size("depth")
    slots, _, _, columns, rows = coefficients.shape
    strip = columns // tiles
    band = rows // depths
    zblocks = tiles * depths
    vmem = pl.BlockSpec(memory_space=pltpu.VMEM)
    params = pltpu.CompilerParams(vmem_limit_bytes=8 * 1024 * 1024)
    lanes = strip * band
    inputs = (coefficients.reshape(slots, columns, rows), keep_count.reshape(columns, rows))
    outgoing, sign = pl.pallas_call(
        lambda *refs: pack_kernel(*refs, tiles=tiles, depths=depths),
        out_shape=[
            jax.ShapeDtypeStruct((zblocks, 5, 1, lanes), jnp.float32),
            jax.ShapeDtypeStruct((2 * EDGE, lanes), jnp.float32),
        ],
        in_specs=[pl.BlockSpec(memory_space=pltpu.SMEM)] + [pl.BlockSpec(memory_space=pltpu.HBM)] * 2,
        out_specs=[vmem, vmem],
        scratch_shapes=[
            pltpu.VMEM((slots, columns, rows), jnp.float32),
            pltpu.VMEM((columns, rows), jnp.int32),
            pltpu.VMEM((depths, 5, tiles, lanes), jnp.float32),
            pltpu.SemaphoreType.DMA((2,)),
        ],
        compiler_params=params,
        name="pack",
    )(view_flip, *(pltpu.with_memory_space_constraint(x, pltpu.HBM) for x in inputs))
    devices = [(t, d) for d in range(depths) for t in range(tiles)]
    listed = sorted(range(zblocks), key=lambda i: listed_at(*devices[i], tiles, depths))
    chunks = outgoing.reshape(zblocks, 1, 5 * lanes)
    arrived = lax.all_to_all(
        chunks, ("depth", "tile"), split_axis=0, concat_axis=0, tiled=True, axis_index_groups=[listed]
    )
    return pl.pallas_call(
        lambda *refs: render_kernel(
            *refs, strip=strip, band=band, samples=EDGE * zblocks, tiles=tiles, depths=depths
        ),
        out_shape=jax.ShapeDtypeStruct((4, strip * EDGE, band * EDGE), jnp.float32),
        in_specs=[vmem, vmem],
        out_specs=vmem,
        scratch_shapes=[pltpu.VMEM((slots, zblocks, lanes), jnp.float32)],
        compiler_params=params,
        name="render",
    )(sign, arrived.reshape(zblocks * 5, lanes))


def solution(mesh):
    placed = (P(None, "depth", "tile", None, None), P("depth", "tile", None, None), P("tile"))
    return jax.shard_map(
        per_device, mesh=mesh, in_specs=placed, out_specs=P(None, "tile", "depth"), check_vma=False
    )
```

```python
import math

import jax
import jax.numpy as jnp
from jax import lax
from jax.experimental import pallas as pl
from jax.experimental.pallas import tpu as pltpu
from jax.sharding import PartitionSpec as P

LOG2E = math.log2(math.e)
EDGE = 4


def cosine(frequency, position):
    factor = 0.5 if frequency == 0 else math.sqrt(0.5)
    return factor * math.cos(math.pi * (2 * position + 1) * frequency / 8.0)


def swap_halves(values):
    half = values.shape[1] // 2
    if values.shape[1] % 128 == 0:
        return pltpu.roll(values, half, 1)
    return jnp.concatenate([values[:, half:], values[:, :half]], axis=1)


def listed_at(t, d, tiles, depths):
    turned, size = 0, 1
    while 2 * size <= depths:
        turned = turned + d // size % 2 * (depths // (2 * size))
        size *= 2
    if size != depths:
        turned = d
    return tiles * depths - 1 - turned * tiles - t


def pack_kernel(
    flip_ref, coef_hbm, keep_hbm, out_ref, sign_ref, coef_ref, keep_ref, rows_ref, arrival, *, tiles, depths
):
    _, columns, rows = coef_ref.shape
    strip = columns // tiles
    band = rows // depths
    moves = [(coef_hbm.at[pl.ds(k, 4)], coef_ref.at[pl.ds(k, 4)]) for k in (0, 4)] + [(keep_hbm, keep_ref)]
    fetches = [pltpu.make_async_copy(a, b, arrival.at[i]) for i, (a, b) in enumerate(moves)]
    for fetch in fetches:
        fetch.start()
    for fetch in fetches:
        fetch.wait()
    lane = lax.broadcasted_iota(jnp.int32, (tiles, rows), 1)
    even = lane % 2 == 0

    def take(values, index):
        return jnp.take_along_axis(values, index, axis=1)

    other = lane + 1 - 2 * (lane % 2)
    packed = []
    for b in range(strip):
        mine = pl.ds(b, tiles, stride=strip)
        keep = keep_ref[mine, :]
        slot = [coef_ref[k, mine, :] for k in range(8)]
        result = [slot[0]]
        for q in (1, 2, 3, 4):
            result.append(jnp.where(keep > q, slot[q], take(slot[8 - q], other)))
        result[4] = jnp.where(even, result[4], (9 - keep).astype(jnp.float32))
        packed.append(result)
    sign_ref[...] = jnp.full(sign_ref.shape, 1 - 2 * flip_ref[0], jnp.int32).astype(jnp.float32)
    half = strip * band // 2
    parity = lane // half % 2
    column = lane // (band // 2) % strip
    source = lane % (band // 2) * 2 + parity
    for d in range(depths):
        for q in range(5):
            gathered = [take(packed[b][q], source + d * band) for b in range(strip)]
            merged = gathered[0]
            for b in range(1, strip):
                merged = jnp.where(column == b, gathered[b], merged)
            rows_ref[d, q] = merged[:, : 2 * half]


    for d in range(depths):
        for t in range(tiles):
            out_ref[listed_at(t, d, tiles, depths), :, 0, :] = rows_ref[d, :, t, :]


def unpack(packed_ref, coef_ref):
    zblocks, lanes = packed_ref.shape[0] // 5, packed_ref.shape[1]
    first = lax.broadcasted_iota(jnp.int32, (zblocks, lanes), 1) < lanes // 2
    row = [packed_ref[pl.ds(q, zblocks, stride=5), :] for q in range(5)]
    turned = [None] + [swap_halves(row[q]) for q in (1, 2, 3, 4)]
    keep = jnp.where(first, turned[4], 9.0 - row[4])
    slot = [row[0]] + [jnp.where(keep > q, row[q], 0.0) for q in (1, 2, 3)]
    slot.append(jnp.where(keep > 4, jnp.where(first, row[4], turned[4]), 0.0))
    slot += [jnp.where(keep > k, turned[8 - k], 0.0) for k in (5, 6, 7)]
    for k in range(8):
        coef_ref[k] = slot[k]


def render_kernel(sign_ref, packed_ref, out_ref, coef_ref, *, strip, band, samples, tiles, depths):
    unpack(packed_ref, coef_ref)
    slots, zblocks, lanes = coef_ref.shape
    sign = sign_ref[...]
    flipped = jnp.max(sign) < 0.0
    b1 = [cosine(1, i) for i in range(EDGE)]
    row = lax.broadcasted_iota(jnp.int32, (2 * EDGE, lanes), 0)
    x = row % EDGE
    y = row // EDGE

    def table(position, values):
        result = jnp.full((2 * EDGE, lanes), values[0], jnp.float32)
        for i in range(1, len(values)):
            result = jnp.where(position == i, jnp.float32(values[i]), result)
        return result

    x1 = table(x, b1)
    x2 = table(x, [cosine(2, i) for i in range(EDGE)])
    y1 = table(y, b1[:2])
    y2 = table(y, [cosine(2, i) for i in range(2)])
    c_dc = 0.125 * LOG2E
    c_x1 = (0.25 * LOG2E) * x1
    c_x2 = (0.25 * LOG2E) * x2
    c_y1 = (0.25 * LOG2E) * y1
    c_y2 = (0.25 * LOG2E) * y2
    c_xy = (0.5 * LOG2E) * x1 * y1
    c_z = jnp.full((2 * EDGE, lanes), 0.25 * LOG2E * b1[0], jnp.float32) * sign
    c_zy = (0.5 * LOG2E * b1[0]) * y1 * sign
    ratio = b1[1] / b1[0]
    blue_one = 2.0**-20
    blue_factor = blue_one * math.exp(-1.5)
    fade = -1.5 / samples

    def block(step, state):
        source = jnp.where(flipped, zblocks - 1 - step, step)
        zb = listed_at(source % tiles, source // tiles, tiles, depths)
        a = [
            jnp.broadcast_to(coef_ref[k, pl.ds(zb, 1), :], (2 * EDGE, lanes)) for k in range(slots)
        ]
        even = a[0] * c_dc + a[2] * c_x1 + a[4] * c_y2 + a[6] * c_x2
        odd = a[1] * c_y1 + a[5] * c_xy
        g_even = a[3] * c_z
        g_odd = a[7] * c_zy
        halves = []
        for h in range(2):
            depth, before, red, green, blue = state[h]
            base = even + odd if h == 0 else even - odd
            g = g_even + g_odd if h == 0 else g_even - g_odd
            near = g * ratio
            for f in (base + g, base + near, base - near, base - g):
                v = jnp.exp2(f)
                one_u = 1.0 + v * v
                depth = depth + jnp.log2(one_u)
                after = jnp.exp2(fade * depth)
                weight = before - after
                before = after
                blue_u = blue_one + blue_factor * v
                shared = weight / (one_u * blue_u)
                red = red + shared * blue_u
                green = green + weight * jnp.exp2(f * (f * (-1.0 / LOG2E)))
                blue = blue + shared * one_u
            halves.append((depth, before, red, green, blue))
        return tuple(halves)

    zero = jnp.zeros((2 * EDGE, lanes), jnp.float32)
    one = jnp.ones((2 * EDGE, lanes), jnp.float32)
    start = (zero, one, zero, zero, zero)
    state = lax.fori_loop(0, zblocks, block, (start, start), unroll=8)

    width = band * EDGE
    pick = lax.broadcasted_iota(jnp.int32, (2 * EDGE, width), 1)
    y_out = pick % EDGE
    place = pick // EDGE
    place = place % 2 * (lanes // 2) + place // 2
    outs = []
    for _, before, red, green, blue in state:
        opacity = 1.0 - before
        outs.append((opacity - red, green, blue * blue_one, opacity))
    for ch in range(4):
        for b in range(strip):
            index = place + b * (band // 2)
            low = jnp.take_along_axis(outs[0][ch], index, axis=1)
            high = jnp.take_along_axis(outs[1][ch], index, axis=1)
            both = jnp.where(y_out < 2, low, high)
            first, second = both[:EDGE], both[EDGE:]
            use_first = (y_out[:EDGE] == 0) | (y_out[:EDGE] == 3)
            out_ref[ch, pl.ds(b * EDGE, EDGE), :] = jnp.where(use_first, first, second)


def per_device(coefficients, keep_count, view_flip):
    tiles = lax.axis_size("tile")
    depths = lax.axis_size("depth")
    slots, _, _, columns, rows = coefficients.shape
    strip = columns // tiles
    band = rows // depths
    zblocks = tiles * depths
    vmem = pl.BlockSpec(memory_space=pltpu.VMEM)
    params = pltpu.CompilerParams(vmem_limit_bytes=8 * 1024 * 1024)
    lanes = strip * band
    inputs = (coefficients.reshape(slots, columns, rows), keep_count.reshape(columns, rows))
    outgoing, sign = pl.pallas_call(
        lambda *refs: pack_kernel(*refs, tiles=tiles, depths=depths),
        out_shape=[
            jax.ShapeDtypeStruct((zblocks, 5, 1, lanes), jnp.float32),
            jax.ShapeDtypeStruct((2 * EDGE, lanes), jnp.float32),
        ],
        in_specs=[pl.BlockSpec(memory_space=pltpu.SMEM)] + [pl.BlockSpec(memory_space=pltpu.HBM)] * 2,
        out_specs=[vmem, vmem],
        scratch_shapes=[
            pltpu.VMEM((slots, columns, rows), jnp.float32),
            pltpu.VMEM((columns, rows), jnp.int32),
            pltpu.VMEM((depths, 5, tiles, lanes), jnp.float32),
            pltpu.SemaphoreType.DMA((3,)),
        ],
        compiler_params=params,
        name="pack",
    )(view_flip, *(pltpu.with_memory_space_constraint(x, pltpu.HBM) for x in inputs))
    devices = [(t, d) for d in range(depths) for t in range(tiles)]
    listed = sorted(range(zblocks), key=lambda i: listed_at(*devices[i], tiles, depths))
    chunks = outgoing.reshape(zblocks, 1, 5 * lanes)
    arrived = lax.all_to_all(
        chunks, ("depth", "tile"), split_axis=0, concat_axis=0, tiled=True, axis_index_groups=[listed]
    )
    return pl.pallas_call(
        lambda *refs: render_kernel(
            *refs, strip=strip, band=band, samples=EDGE * zblocks, tiles=tiles, depths=depths
        ),
        out_shape=jax.ShapeDtypeStruct((4, strip * EDGE, band * EDGE), jnp.float32),
        in_specs=[vmem, vmem],
        out_specs=vmem,
        scratch_shapes=[pltpu.VMEM((slots, zblocks, lanes), jnp.float32)],
        compiler_params=params,
        name="render",
    )(sign, arrived.reshape(zblocks * 5, lanes))


def solution(mesh):
    placed = (P(None, "depth", "tile", None, None), P("depth", "tile", None, None), P("tile"))
    return jax.shard_map(
        per_device, mesh=mesh, in_specs=placed, out_specs=P(None, "tile", "depth"), check_vma=False
    )
```

```python
import math

import jax
import jax.numpy as jnp
from jax import lax
from jax.experimental import pallas as pl
from jax.experimental.pallas import tpu as pltpu
from jax.sharding import PartitionSpec as P

LOG2E = math.log2(math.e)
EDGE = 4


def cosine(frequency, position):
    factor = 0.5 if frequency == 0 else math.sqrt(0.5)
    return factor * math.cos(math.pi * (2 * position + 1) * frequency / 8.0)


def swap_halves(values):
    half = values.shape[1] // 2
    if values.shape[1] % 128 == 0:
        return pltpu.roll(values, half, 1)
    return jnp.concatenate([values[:, half:], values[:, :half]], axis=1)


def listed_at(t, d, tiles, depths):
    turned, size = 0, 1
    while 2 * size <= depths:
        turned = turned + d // size % 2 * (depths // (2 * size))
        size *= 2
    if size != depths:
        turned = d
    return tiles * depths - 1 - turned * tiles - t


def pack_kernel(
    flip_ref, coef_hbm, keep_hbm, out_ref, sign_ref, coef_ref, keep_ref, rows_ref, arrival, *, tiles, depths
):
    _, columns, rows = coef_ref.shape
    strip = columns // tiles
    band = rows // depths
    moves = [(coef_hbm.at[pl.ds(k, 4)], coef_ref.at[pl.ds(k, 4)]) for k in (0, 4)] + [(keep_hbm, keep_ref)]
    fetches = [pltpu.make_async_copy(a, b, arrival.at[i]) for i, (a, b) in enumerate(moves)]
    for fetch in fetches:
        fetch.start()
    for fetch in fetches:
        fetch.wait()
    lane = lax.broadcasted_iota(jnp.int32, (tiles, rows), 1)
    even = lane % 2 == 0

    def take(values, index):
        return jnp.take_along_axis(values, index, axis=1)

    other = lane + 1 - 2 * (lane % 2)
    packed = []
    for b in range(strip):
        mine = pl.ds(b, tiles, stride=strip)
        keep = keep_ref[mine, :]
        slot = [coef_ref[k, mine, :] for k in range(8)]
        result = [slot[0]]
        for q in (1, 2, 3, 4):
            result.append(jnp.where(keep > q, slot[q], take(slot[8 - q], other)))
        result[4] = jnp.where(even, result[4], (9 - keep).astype(jnp.float32))
        packed.append(result)
    sign_ref[...] = jnp.full(sign_ref.shape, 1 - 2 * flip_ref[0], jnp.int32).astype(jnp.float32)
    half = strip * band // 2
    parity = lane // half % 2
    column = lane // (band // 2) % strip
    source = lane % (band // 2) * 2 + parity
    for d in range(depths):
        for q in range(5):
            gathered = [take(packed[b][q], source + d * band) for b in range(strip)]
            merged = gathered[0]
            for b in range(1, strip):
                merged = jnp.where(column == b, gathered[b], merged)
            rows_ref[d, q] = merged[:, : 2 * half]


    for d in range(depths):
        for t in range(tiles):
            out_ref[listed_at(t, d, tiles, depths), :, 0, :] = rows_ref[d, :, t, :]


def unpack(packed_ref, coef_ref, scales):
    zblocks, lanes = packed_ref.shape[0] // 5, packed_ref.shape[1]
    first = lax.broadcasted_iota(jnp.int32, (zblocks, lanes), 1) < lanes // 2
    row = [packed_ref[pl.ds(q, zblocks, stride=5), :] for q in range(5)]
    turned = [None] + [swap_halves(row[q]) for q in (1, 2, 3, 4)]
    keep = jnp.where(first, turned[4], 9.0 - row[4])
    slot = [row[0]] + [jnp.where(keep > q, row[q], 0.0) for q in (1, 2, 3)]
    slot.append(jnp.where(keep > 4, jnp.where(first, row[4], turned[4]), 0.0))
    slot += [jnp.where(keep > k, turned[8 - k], 0.0) for k in (5, 6, 7)]
    for k in range(8):
        coef_ref[k] = slot[k] * scales[k] if k in scales else slot[k]


def render_kernel(sign_ref, packed_ref, out_ref, coef_ref, *, strip, band, samples, tiles, depths):
    slots, zblocks, lanes = coef_ref.shape
    sign = sign_ref[...]
    flipped = jnp.max(sign) < 0.0
    b1 = [cosine(1, i) for i in range(EDGE)]
    c_z = 0.25 * LOG2E * b1[0]
    unpack(packed_ref, coef_ref, {0: 0.125 * LOG2E, 3: c_z * sign[:1]})
    row = lax.broadcasted_iota(jnp.int32, (2 * EDGE, lanes), 0)
    x = row % EDGE
    y = row // EDGE

    def table(position, values):
        result = jnp.full((2 * EDGE, lanes), values[0], jnp.float32)
        for i in range(1, len(values)):
            result = jnp.where(position == i, jnp.float32(values[i]), result)
        return result

    x1 = table(x, b1)
    x2 = table(x, [cosine(2, i) for i in range(EDGE)])
    y1 = table(y, b1[:2])
    y2 = table(y, [cosine(2, i) for i in range(2)])
    c_x1 = (0.25 * LOG2E) * x1
    c_x2 = (0.25 * LOG2E) * x2
    c_y1 = (0.25 * LOG2E) * y1
    c_y2 = (0.25 * LOG2E) * y2
    c_xy = (0.5 * LOG2E) * x1 * y1
    c_zy = (0.5 * LOG2E * b1[0]) * y1 * sign
    ratio = b1[1] / b1[0]
    blue_factor = math.exp(-1.5)
    fade = -1.5 / samples

    def block(step, state):
        source = jnp.where(flipped, zblocks - 1 - step, step)
        zb = listed_at(source % tiles, source // tiles, tiles, depths)
        a = [
            jnp.broadcast_to(coef_ref[k, pl.ds(zb, 1), :], (2 * EDGE, lanes)) for k in range(slots)
        ]
        even = a[0] + a[2] * c_x1 + a[4] * c_y2 + a[6] * c_x2
        odd = a[1] * c_y1 + a[5] * c_xy
        g_even = a[3]
        g_odd = a[7] * c_zy
        halves = []
        for h in range(2):
            depth, before, red, green, blue = state[h]
            base = even + odd if h == 0 else even - odd
            g = g_even + g_odd if h == 0 else g_even - g_odd
            near = g * ratio
            for f in (base + g, base + near, base - near, base - g):
                v = jnp.exp2(f)
                one_u = 1.0 + v * v
                depth = depth + jnp.log2(one_u)
                after = jnp.exp2(fade * depth)
                weight = before - after
                before = after
                red = red + weight / one_u
                green = green + weight * jnp.exp2(f * (f * (-1.0 / LOG2E)))
                blue = blue + weight / (1.0 + blue_factor * v)
            halves.append((depth, before, red, green, blue))
        return tuple(halves)

    zero = jnp.zeros((2 * EDGE, lanes), jnp.float32)
    one = jnp.ones((2 * EDGE, lanes), jnp.float32)
    start = (zero, one, zero, zero, zero)
    state = lax.fori_loop(0, zblocks, block, (start, start), unroll=16)

    width = band * EDGE
    pick = lax.broadcasted_iota(jnp.int32, (2 * EDGE, width), 1)
    y_out = pick % EDGE
    place = pick // EDGE
    place = place % 2 * (lanes // 2) + place // 2
    outs = []
    for _, before, red, green, blue in state:
        opacity = 1.0 - before
        outs.append((opacity - red, green, blue, opacity))
    for ch in range(4):
        for b in range(strip):
            index = place + b * (band // 2)
            low = jnp.take_along_axis(outs[0][ch], index, axis=1)
            high = jnp.take_along_axis(outs[1][ch], index, axis=1)
            both = jnp.where(y_out < 2, low, high)
            first, second = both[:EDGE], both[EDGE:]
            use_first = (y_out[:EDGE] == 0) | (y_out[:EDGE] == 3)
            out_ref[ch, pl.ds(b * EDGE, EDGE), :] = jnp.where(use_first, first, second)


def per_device(coefficients, keep_count, view_flip):
    tiles = lax.axis_size("tile")
    depths = lax.axis_size("depth")
    slots, _, _, columns, rows = coefficients.shape
    strip = columns // tiles
    band = rows // depths
    zblocks = tiles * depths
    vmem = pl.BlockSpec(memory_space=pltpu.VMEM)
    params = pltpu.CompilerParams(vmem_limit_bytes=8 * 1024 * 1024)
    lanes = strip * band
    inputs = (coefficients.reshape(slots, columns, rows), keep_count.reshape(columns, rows))
    outgoing, sign = pl.pallas_call(
        lambda *refs: pack_kernel(*refs, tiles=tiles, depths=depths),
        out_shape=[
            jax.ShapeDtypeStruct((zblocks, 5, 1, lanes), jnp.float32),
            jax.ShapeDtypeStruct((2 * EDGE, lanes), jnp.float32),
        ],
        in_specs=[pl.BlockSpec(memory_space=pltpu.SMEM)] + [pl.BlockSpec(memory_space=pltpu.HBM)] * 2,
        out_specs=[vmem, vmem],
        scratch_shapes=[
            pltpu.VMEM((slots, columns, rows), jnp.float32),
            pltpu.VMEM((columns, rows), jnp.int32),
            pltpu.VMEM((depths, 5, tiles, lanes), jnp.float32),
            pltpu.SemaphoreType.DMA((3,)),
        ],
        compiler_params=params,
        name="pack",
    )(view_flip, *(pltpu.with_memory_space_constraint(x, pltpu.HBM) for x in inputs))
    devices = [(t, d) for d in range(depths) for t in range(tiles)]
    listed = sorted(range(zblocks), key=lambda i: listed_at(*devices[i], tiles, depths))
    chunks = outgoing.reshape(zblocks, 1, 5 * lanes)
    arrived = lax.all_to_all(
        chunks, ("depth", "tile"), split_axis=0, concat_axis=0, tiled=True, axis_index_groups=[listed]
    )
    return pl.pallas_call(
        lambda *refs: render_kernel(
            *refs, strip=strip, band=band, samples=EDGE * zblocks, tiles=tiles, depths=depths
        ),
        out_shape=jax.ShapeDtypeStruct((4, strip * EDGE, band * EDGE), jnp.float32),
        in_specs=[vmem, vmem],
        out_specs=vmem,
        scratch_shapes=[pltpu.VMEM((slots, zblocks, lanes), jnp.float32)],
        compiler_params=params,
        name="render",
    )(sign, arrived.reshape(zblocks * 5, lanes))


def solution(mesh):
    placed = (P(None, "depth", "tile", None, None), P("depth", "tile", None, None), P("tile"))
    return jax.shard_map(
        per_device, mesh=mesh, in_specs=placed, out_specs=P(None, "tile", "depth"), check_vma=False
    )
```

```python
import math

import jax
import jax.numpy as jnp
from jax import lax
from jax.experimental import pallas as pl
from jax.experimental.pallas import tpu as pltpu
from jax.sharding import PartitionSpec as P

LOG2E = math.log2(math.e)
EDGE = 4


def cosine(frequency, position):
    factor = 0.5 if frequency == 0 else math.sqrt(0.5)
    return factor * math.cos(math.pi * (2 * position + 1) * frequency / 8.0)


def swap_halves(values):
    half = values.shape[1] // 2
    if values.shape[1] % 128 == 0:
        return pltpu.roll(values, half, 1)
    return jnp.concatenate([values[:, half:], values[:, :half]], axis=1)


def listed_at(t, d, tiles, depths):
    turned, size = 0, 1
    while 2 * size <= depths:
        turned = turned + d // size % 2 * (depths // (2 * size))
        size *= 2
    if size != depths:
        turned = d
    return tiles * depths - 1 - turned * tiles - t


def pack_kernel(
    coef_hbm, keep_hbm, out_ref, coef_ref, keep_ref, rows_ref, arrival, *, tiles, depths
):
    _, columns, rows = coef_ref.shape
    strip = columns // tiles
    band = rows // depths
    moves = ((coef_hbm, coef_ref), (keep_hbm, keep_ref))
    fetches = [pltpu.make_async_copy(a, b, arrival.at[i]) for i, (a, b) in enumerate(moves)]
    for fetch in fetches:
        fetch.start()
    for fetch in fetches:
        fetch.wait()
    lane = lax.broadcasted_iota(jnp.int32, (tiles, rows), 1)
    even = lane % 2 == 0

    def take(values, index):
        return jnp.take_along_axis(values, index, axis=1)

    other = lane + 1 - 2 * (lane % 2)
    packed = []
    for b in range(strip):
        mine = pl.ds(b, tiles, stride=strip)
        keep = keep_ref[mine, :]
        slot = [coef_ref[k, mine, :] for k in range(8)]
        result = [slot[0]]
        for q in (1, 2, 3, 4):
            result.append(jnp.where(keep > q, slot[q], take(slot[8 - q], other)))
        result[4] = jnp.where(even, result[4], (9 - keep).astype(jnp.float32))
        packed.append(result)
    half = strip * band // 2
    parity = lane // half % 2
    column = lane // (band // 2) % strip
    source = lane % (band // 2) * 2 + parity
    for d in range(depths):
        for q in range(5):
            gathered = [take(packed[b][q], source + d * band) for b in range(strip)]
            merged = gathered[0]
            for b in range(1, strip):
                merged = jnp.where(column == b, gathered[b], merged)
            rows_ref[d, q] = merged[:, : 2 * half]


    for d in range(depths):
        for t in range(tiles):
            out_ref[listed_at(t, d, tiles, depths), :, 0, :] = rows_ref[d, :, t, :]


def unpack(packed_ref, coef_ref):
    zblocks, lanes = packed_ref.shape[0] // 5, packed_ref.shape[1]
    first = lax.broadcasted_iota(jnp.int32, (zblocks, lanes), 1) < lanes // 2
    row = [packed_ref[pl.ds(q, zblocks, stride=5), :] for q in range(5)]
    turned = [None] + [swap_halves(row[q]) for q in (1, 2, 3, 4)]
    keep = jnp.where(first, turned[4], 9.0 - row[4])
    slot = [row[0]] + [jnp.where(keep > q, row[q], 0.0) for q in (1, 2, 3)]
    slot.append(jnp.where(keep > 4, jnp.where(first, row[4], turned[4]), 0.0))
    slot += [jnp.where(keep > k, turned[8 - k], 0.0) for k in (5, 6, 7)]
    for k in range(8):
        coef_ref[k] = slot[k]


def render_kernel(flip_ref, packed_ref, out_ref, coef_ref, *, strip, band, samples, tiles, depths):
    unpack(packed_ref, coef_ref)
    slots, zblocks, lanes = coef_ref.shape
    flipped = flip_ref[0] > 0
    sign = jnp.where(flipped, jnp.float32(-1.0), jnp.float32(1.0))
    b1 = [cosine(1, i) for i in range(EDGE)]
    row = lax.broadcasted_iota(jnp.int32, (2 * EDGE, lanes), 0)
    x = row % EDGE
    y = row // EDGE

    def table(position, values):
        result = jnp.full((2 * EDGE, lanes), values[0], jnp.float32)
        for i in range(1, len(values)):
            result = jnp.where(position == i, jnp.float32(values[i]), result)
        return result

    x1 = table(x, b1)
    x2 = table(x, [cosine(2, i) for i in range(EDGE)])
    y1 = table(y, b1[:2])
    y2 = table(y, [cosine(2, i) for i in range(2)])
    c_dc = 0.125 * LOG2E
    c_x1 = (0.25 * LOG2E) * x1
    c_x2 = (0.25 * LOG2E) * x2
    c_y1 = (0.25 * LOG2E) * y1
    c_y2 = (0.25 * LOG2E) * y2
    c_xy = (0.5 * LOG2E) * x1 * y1
    c_z = jnp.full((2 * EDGE, lanes), 0.25 * LOG2E * b1[0], jnp.float32) * sign
    c_zy = (0.5 * LOG2E * b1[0]) * y1 * sign
    ratio = b1[1] / b1[0]
    blue_one = 2.0**-20
    blue_factor = blue_one * math.exp(-1.5)
    fade = -1.5 / samples

    def block(step, state):
        source = jnp.where(flipped, zblocks - 1 - step, step)
        zb = listed_at(source % tiles, source // tiles, tiles, depths)
        a = [
            jnp.broadcast_to(coef_ref[k, pl.ds(zb, 1), :], (2 * EDGE, lanes)) for k in range(slots)
        ]
        even = a[0] * c_dc + a[2] * c_x1 + a[4] * c_y2 + a[6] * c_x2
        odd = a[1] * c_y1 + a[5] * c_xy
        g_even = a[3] * c_z
        g_odd = a[7] * c_zy
        halves = []
        for h in range(2):
            depth, before, red, green, blue = state[h]
            base = even + odd if h == 0 else even - odd
            g = g_even + g_odd if h == 0 else g_even - g_odd
            near = g * ratio
            for f in (base + g, base + near, base - near, base - g):
                v = jnp.exp2(f)
                one_u = 1.0 + v * v
                depth = depth + jnp.log2(one_u)
                after = jnp.exp2(fade * depth)
                weight = before - after
                before = after
                blue_u = blue_one + blue_factor * v
                shared = weight / (one_u * blue_u)
                red = red + shared * blue_u
                green = green + weight * jnp.exp2(f * (f * (-1.0 / LOG2E)))
                blue = blue + shared * one_u
            halves.append((depth, before, red, green, blue))
        return tuple(halves)

    zero = jnp.zeros((2 * EDGE, lanes), jnp.float32)
    one = jnp.ones((2 * EDGE, lanes), jnp.float32)
    start = (zero, one, zero, zero, zero)
    state = lax.fori_loop(0, zblocks, block, (start, start), unroll=16)

    width = band * EDGE
    pick = lax.broadcasted_iota(jnp.int32, (2 * EDGE, width), 1)
    y_out = pick % EDGE
    place = pick // EDGE
    place = place % 2 * (lanes // 2) + place // 2
    outs = []
    for _, before, red, green, blue in state:
        opacity = 1.0 - before
        outs.append((opacity - red, green, blue * blue_one, opacity))
    for ch in range(4):
        for b in range(strip):
            index = place + b * (band // 2)
            low = jnp.take_along_axis(outs[0][ch], index, axis=1)
            high = jnp.take_along_axis(outs[1][ch], index, axis=1)
            both = jnp.where(y_out < 2, low, high)
            first, second = both[:EDGE], both[EDGE:]
            use_first = (y_out[:EDGE] == 0) | (y_out[:EDGE] == 3)
            out_ref[ch, pl.ds(b * EDGE, EDGE), :] = jnp.where(use_first, first, second)


def per_device(coefficients, keep_count, view_flip):
    tiles = lax.axis_size("tile")
    depths = lax.axis_size("depth")
    slots, _, _, columns, rows = coefficients.shape
    strip = columns // tiles
    band = rows // depths
    zblocks = tiles * depths
    vmem = pl.BlockSpec(memory_space=pltpu.VMEM)
    params = pltpu.CompilerParams(vmem_limit_bytes=8 * 1024 * 1024)
    lanes = strip * band
    inputs = (coefficients.reshape(slots, columns, rows), keep_count.reshape(columns, rows))
    outgoing = pl.pallas_call(
        lambda *refs: pack_kernel(*refs, tiles=tiles, depths=depths),
        out_shape=jax.ShapeDtypeStruct((zblocks, 5, 1, lanes), jnp.float32),
        in_specs=[pl.BlockSpec(memory_space=pltpu.HBM)] * 2,
        out_specs=vmem,
        scratch_shapes=[
            pltpu.VMEM((slots, columns, rows), jnp.float32),
            pltpu.VMEM((columns, rows), jnp.int32),
            pltpu.VMEM((depths, 5, tiles, lanes), jnp.float32),
            pltpu.SemaphoreType.DMA((2,)),
        ],
        compiler_params=params,
        name="pack",
    )(*(pltpu.with_memory_space_constraint(x, pltpu.HBM) for x in inputs))
    devices = [(t, d) for d in range(depths) for t in range(tiles)]
    listed = sorted(range(zblocks), key=lambda i: listed_at(*devices[i], tiles, depths))
    chunks = outgoing.reshape(zblocks, 1, 5 * lanes)
    arrived = lax.all_to_all(
        chunks, ("depth", "tile"), split_axis=0, concat_axis=0, tiled=True, axis_index_groups=[listed]
    )
    return pl.pallas_call(
        lambda *refs: render_kernel(
            *refs, strip=strip, band=band, samples=EDGE * zblocks, tiles=tiles, depths=depths
        ),
        out_shape=jax.ShapeDtypeStruct((4, strip * EDGE, band * EDGE), jnp.float32),
        in_specs=[pl.BlockSpec(memory_space=pltpu.SMEM), vmem],
        out_specs=vmem,
        scratch_shapes=[pltpu.VMEM((slots, zblocks, lanes), jnp.float32)],
        compiler_params=params,
        name="render",
    )(view_flip, arrived.reshape(zblocks * 5, lanes))


def solution(mesh):
    placed = (P(None, "depth", "tile", None, None), P("depth", "tile", None, None), P("tile"))
    return jax.shard_map(
        per_device, mesh=mesh, in_specs=placed, out_specs=P(None, "tile", "depth"), check_vma=False
    )
```

```python
import math

import jax
import jax.numpy as jnp
from jax import lax
from jax.experimental import pallas as pl
from jax.experimental.pallas import tpu as pltpu
from jax.sharding import PartitionSpec as P

LOG2E = math.log2(math.e)
EDGE = 4


def cosine(frequency, position):
    factor = 0.5 if frequency == 0 else math.sqrt(0.5)
    return factor * math.cos(math.pi * (2 * position + 1) * frequency / 8.0)


def swap_halves(values):
    half = values.shape[1] // 2
    if values.shape[1] % 128 == 0:
        return pltpu.roll(values, half, 1)
    return jnp.concatenate([values[:, half:], values[:, :half]], axis=1)


def listed_at(t, d, tiles, depths):
    turned, size = 0, 1
    while 2 * size <= depths:
        turned = turned + d // size % 2 * (depths // (2 * size))
        size *= 2
    if size != depths:
        turned = d
    return tiles * depths - 1 - turned * tiles - t


def pack_kernel(
    flip_ref, coef_hbm, keep_hbm, out_ref, sign_ref, coef_ref, keep_ref, rows_ref, arrival, *, tiles, depths
):
    _, columns, rows = coef_ref.shape
    strip = columns // tiles
    band = rows // depths
    moves = ((coef_hbm, coef_ref), (keep_hbm, keep_ref))
    fetches = [pltpu.make_async_copy(a, b, arrival.at[i]) for i, (a, b) in enumerate(moves)]
    for fetch in fetches:
        fetch.start()
    for fetch in fetches:
        fetch.wait()
    lane = lax.broadcasted_iota(jnp.int32, (tiles, rows), 1)
    even = lane % 2 == 0

    def take(values, index):
        return jnp.take_along_axis(values, index, axis=1)

    other = lane + 1 - 2 * (lane % 2)
    packed = []
    for b in range(strip):
        mine = pl.ds(b, tiles, stride=strip)
        keep = keep_ref[mine, :]
        slot = [coef_ref[k, mine, :] for k in range(8)]
        result = [slot[0]]
        for q in (1, 2, 3, 4):
            result.append(jnp.where(keep > q, slot[q], take(slot[8 - q], other)))
        result[4] = jnp.where(even, result[4], (9 - keep).astype(jnp.float32))
        packed.append(result)
    sign_ref[...] = jnp.full(sign_ref.shape, 1 - 2 * flip_ref[0], jnp.int32).astype(jnp.float32)
    half = strip * band // 2
    parity = lane // half % 2
    column = lane // (band // 2) % strip
    source = lane % (band // 2) * 2 + parity
    for d in range(depths):
        for q in range(5):
            gathered = [take(packed[b][q], source + d * band) for b in range(strip)]
            merged = gathered[0]
            for b in range(1, strip):
                merged = jnp.where(column == b, gathered[b], merged)
            rows_ref[d, q] = merged[:, : 2 * half]


    for d in range(depths):
        for t in range(tiles):
            out_ref[listed_at(t, d, tiles, depths), :, 0, :] = rows_ref[d, :, t, :]


def unpack(packed_ref, coef_ref):
    zblocks, lanes = packed_ref.shape[0] // 5, packed_ref.shape[1]
    first = lax.broadcasted_iota(jnp.int32, (zblocks, lanes), 1) < lanes // 2
    row = [packed_ref[pl.ds(q, zblocks, stride=5), :] for q in range(5)]
    turned = [None] + [swap_halves(row[q]) for q in (1, 2, 3, 4)]
    keep = jnp.where(first, turned[4], 9.0 - row[4])
    slot = [row[0]] + [jnp.where(keep > q, row[q], 0.0) for q in (1, 2, 3)]
    slot.append(jnp.where(keep > 4, jnp.where(first, row[4], turned[4]), 0.0))
    slot += [jnp.where(keep > k, turned[8 - k], 0.0) for k in (5, 6, 7)]
    for k in range(8):
        coef_ref[k] = slot[k]


def render_kernel(
    flip_ref, sign_ref, packed_ref, out_hbm, coef_ref, out_ref, leaving, *, strip, band, samples, tiles, depths
):
    unpack(packed_ref, coef_ref)
    slots, zblocks, lanes = coef_ref.shape
    sign = sign_ref[...]
    flipped = flip_ref[0] > 0
    b1 = [cosine(1, i) for i in range(EDGE)]
    row = lax.broadcasted_iota(jnp.int32, (2 * EDGE, lanes), 0)
    x = row % EDGE
    y = row // EDGE

    def table(position, values):
        result = jnp.full((2 * EDGE, lanes), values[0], jnp.float32)
        for i in range(1, len(values)):
            result = jnp.where(position == i, jnp.float32(values[i]), result)
        return result

    x1 = table(x, b1)
    x2 = table(x, [cosine(2, i) for i in range(EDGE)])
    y1 = table(y, b1[:2])
    y2 = table(y, [cosine(2, i) for i in range(2)])
    c_dc = 0.125 * LOG2E
    c_x1 = (0.25 * LOG2E) * x1
    c_x2 = (0.25 * LOG2E) * x2
    c_y1 = (0.25 * LOG2E) * y1
    c_y2 = (0.25 * LOG2E) * y2
    c_xy = (0.5 * LOG2E) * x1 * y1
    c_z = jnp.full((2 * EDGE, lanes), 0.25 * LOG2E * b1[0], jnp.float32) * sign
    c_zy = (0.5 * LOG2E * b1[0]) * y1 * sign
    ratio = b1[1] / b1[0]
    blue_one = 2.0**-20
    blue_factor = blue_one * math.exp(-1.5)
    fade = -1.5 / samples

    def block(step, state):
        source = jnp.where(flipped, zblocks - 1 - step, step)
        zb = listed_at(source % tiles, source // tiles, tiles, depths)
        a = [
            jnp.broadcast_to(coef_ref[k, pl.ds(zb, 1), :], (2 * EDGE, lanes)) for k in range(slots)
        ]
        even = a[0] * c_dc + a[2] * c_x1 + a[4] * c_y2 + a[6] * c_x2
        odd = a[1] * c_y1 + a[5] * c_xy
        g_even = a[3] * c_z
        g_odd = a[7] * c_zy
        halves = []
        for h in range(2):
            depth, before, red, green, blue = state[h]
            base = even + odd if h == 0 else even - odd
            g = g_even + g_odd if h == 0 else g_even - g_odd
            near = g * ratio
            for f in (base + g, base + near, base - near, base - g):
                v = jnp.exp2(f)
                one_u = 1.0 + v * v
                depth = depth + jnp.log2(one_u)
                after = jnp.exp2(fade * depth)
                weight = before - after
                before = after
                blue_u = blue_one + blue_factor * v
                shared = weight / (one_u * blue_u)
                red = red + shared * blue_u
                green = green + weight * jnp.exp2(f * (f * (-1.0 / LOG2E)))
                blue = blue + shared * one_u
            halves.append((depth, before, red, green, blue))
        return tuple(halves)

    zero = jnp.zeros((2 * EDGE, lanes), jnp.float32)
    one = jnp.ones((2 * EDGE, lanes), jnp.float32)
    start = (zero, one, zero, zero, zero)
    state = lax.fori_loop(0, zblocks, block, (start, start), unroll=16)

    width = band * EDGE
    pick = lax.broadcasted_iota(jnp.int32, (2 * EDGE, width), 1)
    y_out = pick % EDGE
    place = pick // EDGE
    place = place % 2 * (lanes // 2) + place // 2
    outs = []
    for _, before, red, green, blue in state:
        opacity = 1.0 - before
        outs.append((opacity - red, green, blue * blue_one, opacity))
    copies = [pltpu.make_async_copy(out_ref.at[ch], out_hbm.at[ch], leaving.at[ch]) for ch in range(4)]
    for ch in range(4):
        for b in range(strip):
            index = place + b * (band // 2)
            low = jnp.take_along_axis(outs[0][ch], index, axis=1)
            high = jnp.take_along_axis(outs[1][ch], index, axis=1)
            both = jnp.where(y_out < 2, low, high)
            first, second = both[:EDGE], both[EDGE:]
            use_first = (y_out[:EDGE] == 0) | (y_out[:EDGE] == 3)
            out_ref[ch, pl.ds(b * EDGE, EDGE), :] = jnp.where(use_first, first, second)
        copies[ch].start()
    for copy in copies:
        copy.wait()


def per_device(coefficients, keep_count, view_flip):
    tiles = lax.axis_size("tile")
    depths = lax.axis_size("depth")
    slots, _, _, columns, rows = coefficients.shape
    strip = columns // tiles
    band = rows // depths
    zblocks = tiles * depths
    vmem = pl.BlockSpec(memory_space=pltpu.VMEM)
    params = pltpu.CompilerParams(vmem_limit_bytes=8 * 1024 * 1024)
    lanes = strip * band
    inputs = (coefficients.reshape(slots, columns, rows), keep_count.reshape(columns, rows))
    outgoing, sign = pl.pallas_call(
        lambda *refs: pack_kernel(*refs, tiles=tiles, depths=depths),
        out_shape=[
            jax.ShapeDtypeStruct((zblocks, 5, 1, lanes), jnp.float32),
            jax.ShapeDtypeStruct((2 * EDGE, lanes), jnp.float32),
        ],
        in_specs=[pl.BlockSpec(memory_space=pltpu.SMEM)] + [pl.BlockSpec(memory_space=pltpu.HBM)] * 2,
        out_specs=[vmem, vmem],
        scratch_shapes=[
            pltpu.VMEM((slots, columns, rows), jnp.float32),
            pltpu.VMEM((columns, rows), jnp.int32),
            pltpu.VMEM((depths, 5, tiles, lanes), jnp.float32),
            pltpu.SemaphoreType.DMA((2,)),
        ],
        compiler_params=params,
        name="pack",
    )(view_flip, *(pltpu.with_memory_space_constraint(x, pltpu.HBM) for x in inputs))
    devices = [(t, d) for d in range(depths) for t in range(tiles)]
    listed = sorted(range(zblocks), key=lambda i: listed_at(*devices[i], tiles, depths))
    chunks = outgoing.reshape(zblocks, 1, 5 * lanes)
    arrived = lax.all_to_all(
        chunks, ("depth", "tile"), split_axis=0, concat_axis=0, tiled=True, axis_index_groups=[listed]
    )
    return pl.pallas_call(
        lambda *refs: render_kernel(
            *refs, strip=strip, band=band, samples=EDGE * zblocks, tiles=tiles, depths=depths
        ),
        out_shape=jax.ShapeDtypeStruct((4, strip * EDGE, band * EDGE), jnp.float32),
        in_specs=[pl.BlockSpec(memory_space=pltpu.SMEM), vmem, vmem],
        out_specs=pl.BlockSpec(memory_space=pltpu.HBM),
        scratch_shapes=[
            pltpu.VMEM((slots, zblocks, lanes), jnp.float32),
            pltpu.VMEM((4, strip * EDGE, band * EDGE), jnp.float32),
            pltpu.SemaphoreType.DMA((4,)),
        ],
        compiler_params=params,
        name="render",
    )(view_flip, sign, arrived.reshape(zblocks * 5, lanes))


def solution(mesh):
    placed = (P(None, "depth", "tile", None, None), P("depth", "tile", None, None), P("tile"))
    return jax.shard_map(
        per_device, mesh=mesh, in_specs=placed, out_specs=P(None, "tile", "depth"), check_vma=False
    )
```

```python
import math

import jax
import jax.numpy as jnp
from jax import lax
from jax.experimental import pallas as pl
from jax.experimental.pallas import tpu as pltpu
from jax.sharding import PartitionSpec as P

LOG2E = math.log2(math.e)
EDGE = 4


def cosine(frequency, position):
    factor = 0.5 if frequency == 0 else math.sqrt(0.5)
    return factor * math.cos(math.pi * (2 * position + 1) * frequency / 8.0)


def swap_halves(values):
    half = values.shape[1] // 2
    if values.shape[1] % 128 == 0:
        return pltpu.roll(values, half, 1)
    return jnp.concatenate([values[:, half:], values[:, :half]], axis=1)


def split(values, size):
    if size & (size - 1):
        return values // size, values % size
    return values >> (size.bit_length() - 1), values & (size - 1)


def listed_at(t, d, tiles, depths):
    return tiles * depths - 1 - d * tiles - t


def pack_kernel(
    flip_ref, coef_hbm, keep_hbm, out_ref, sign_ref, coef_ref, keep_ref, rows_ref, arrival, *, tiles, depths
):
    _, columns, rows = coef_ref.shape
    strip = columns // tiles
    band = rows // depths
    moves = ((coef_hbm, coef_ref), (keep_hbm, keep_ref))
    fetches = [pltpu.make_async_copy(a, b, arrival.at[i]) for i, (a, b) in enumerate(moves)]
    for fetch in fetches:
        fetch.start()
    for fetch in fetches:
        fetch.wait()
    lane = lax.broadcasted_iota(jnp.int32, (tiles, rows), 1)
    odd = split(lane, 2)[1]
    even = odd == 0

    def take(values, index):
        return jnp.take_along_axis(values, index, axis=1)

    other = lane + 1 - 2 * odd
    packed = []
    for b in range(strip):
        mine = pl.ds(b, tiles, stride=strip)
        keep = keep_ref[mine, :]
        slot = [coef_ref[k, mine, :] for k in range(8)]
        result = [slot[0]]
        for q in (1, 2, 3, 4):
            result.append(jnp.where(keep > q, slot[q], take(slot[8 - q], other)))
        result[4] = jnp.where(even, result[4], (9 - keep).astype(jnp.float32))
        packed.append(result)
    sign_ref[...] = jnp.full(sign_ref.shape, 1 - 2 * flip_ref[0], jnp.int32).astype(jnp.float32)
    half = strip * band // 2
    chunk, within = split(lane, band // 2)
    parity, column = split(chunk, strip)
    parity = split(parity, 2)[1]
    source = within * 2 + parity
    for d in range(depths):
        for q in range(5):
            gathered = [take(packed[b][q], source + d * band) for b in range(strip)]
            merged = gathered[0]
            for b in range(1, strip):
                merged = jnp.where(column == b, gathered[b], merged)
            rows_ref[d, q] = merged[:, : 2 * half]


    for d in range(depths):
        for t in range(tiles):
            out_ref[listed_at(t, d, tiles, depths), :, 0, :] = rows_ref[d, :, t, :]


def unpack(packed_ref, coef_ref):
    zblocks, lanes = packed_ref.shape[0] // 5, packed_ref.shape[1]
    first = lax.broadcasted_iota(jnp.int32, (zblocks, lanes), 1) < lanes // 2
    row = [packed_ref[pl.ds(q, zblocks, stride=5), :] for q in range(5)]
    turned = [None] + [swap_halves(row[q]) for q in (1, 2, 3, 4)]
    keep = jnp.where(first, turned[4], 9.0 - row[4])
    slot = [row[0]] + [jnp.where(keep > q, row[q], 0.0) for q in (1, 2, 3)]
    slot.append(jnp.where(keep > 4, jnp.where(first, row[4], turned[4]), 0.0))
    slot += [jnp.where(keep > k, turned[8 - k], 0.0) for k in (5, 6, 7)]
    for k in range(8):
        coef_ref[k] = slot[k]


def render_kernel(
    flip_ref, sign_ref, packed_ref, out_hbm, coef_ref, out_ref, leaving, *, strip, band, samples
):
    unpack(packed_ref, coef_ref)
    slots, zblocks, lanes = coef_ref.shape
    sign = sign_ref[...]
    flipped = flip_ref[0] > 0
    b1 = [cosine(1, i) for i in range(EDGE)]
    row = lax.broadcasted_iota(jnp.int32, (2 * EDGE, lanes), 0)
    y, x = split(row, EDGE)

    def table(position, values):
        result = jnp.full((2 * EDGE, lanes), values[0], jnp.float32)
        for i in range(1, len(values)):
            result = jnp.where(position == i, jnp.float32(values[i]), result)
        return result

    x1 = table(x, b1)
    x2 = table(x, [cosine(2, i) for i in range(EDGE)])
    y1 = table(y, b1[:2])
    y2 = table(y, [cosine(2, i) for i in range(2)])
    c_dc = 0.125 * LOG2E
    c_x1 = (0.25 * LOG2E) * x1
    c_x2 = (0.25 * LOG2E) * x2
    c_y1 = (0.25 * LOG2E) * y1
    c_y2 = (0.25 * LOG2E) * y2
    c_xy = (0.5 * LOG2E) * x1 * y1
    c_z = jnp.full((2 * EDGE, lanes), 0.25 * LOG2E * b1[0], jnp.float32) * sign
    c_zy = (0.5 * LOG2E * b1[0]) * y1 * sign
    ratio = b1[1] / b1[0]
    blue_one = 2.0**-20
    blue_factor = blue_one * math.exp(-1.5)
    fade = -1.5 / samples

    def block(step, state):
        source = jnp.where(flipped, zblocks - 1 - step, step)
        zb = zblocks - 1 - source
        a = [
            jnp.broadcast_to(coef_ref[k, pl.ds(zb, 1), :], (2 * EDGE, lanes)) for k in range(slots)
        ]
        even = a[0] * c_dc + a[2] * c_x1 + a[4] * c_y2 + a[6] * c_x2
        odd = a[1] * c_y1 + a[5] * c_xy
        g_even = a[3] * c_z
        g_odd = a[7] * c_zy
        halves = []
        for h in range(2):
            depth, before, red, green, blue = state[h]
            base = even + odd if h == 0 else even - odd
            g = g_even + g_odd if h == 0 else g_even - g_odd
            near = g * ratio
            for f in (base + g, base + near, base - near, base - g):
                v = jnp.exp2(f)
                one_u = 1.0 + v * v
                depth = depth + jnp.log2(one_u)
                after = jnp.exp2(fade * depth)
                weight = before - after
                before = after
                blue_u = blue_one + blue_factor * v
                shared = weight / (one_u * blue_u)
                red = red + shared * blue_u
                green = green + weight * jnp.exp2(f * (f * (-1.0 / LOG2E)))
                blue = blue + shared * one_u
            halves.append((depth, before, red, green, blue))
        return tuple(halves)

    zero = jnp.zeros((2 * EDGE, lanes), jnp.float32)
    one = jnp.ones((2 * EDGE, lanes), jnp.float32)
    start = (zero, one, zero, zero, zero)
    state = lax.fori_loop(0, zblocks, block, (start, start), unroll=16)

    width = band * EDGE
    pick = lax.broadcasted_iota(jnp.int32, (2 * EDGE, width), 1)
    place, y_out = split(pick, EDGE)
    place, odd = split(place, 2)
    place = odd * (lanes // 2) + place
    outs = []
    for _, before, red, green, blue in state:
        opacity = 1.0 - before
        outs.append((opacity - red, green, blue * blue_one, opacity))
    copies = [pltpu.make_async_copy(out_ref.at[ch], out_hbm.at[ch], leaving.at[ch]) for ch in range(4)]
    for ch in range(4):
        for b in range(strip):
            index = place + b * (band // 2)
            low = jnp.take_along_axis(outs[0][ch], index, axis=1)
            high = jnp.take_along_axis(outs[1][ch], index, axis=1)
            both = jnp.where(y_out < 2, low, high)
            first, second = both[:EDGE], both[EDGE:]
            use_first = (y_out[:EDGE] == 0) | (y_out[:EDGE] == 3)
            out_ref[ch, pl.ds(b * EDGE, EDGE), :] = jnp.where(use_first, first, second)
        copies[ch].start()
    for copy in copies:
        copy.wait()


def per_device(coefficients, keep_count, view_flip):
    tiles = lax.axis_size("tile")
    depths = lax.axis_size("depth")
    slots, _, _, columns, rows = coefficients.shape
    strip = columns // tiles
    band = rows // depths
    zblocks = tiles * depths
    vmem = pl.BlockSpec(memory_space=pltpu.VMEM)
    params = pltpu.CompilerParams(vmem_limit_bytes=8 * 1024 * 1024)
    lanes = strip * band
    inputs = (coefficients.reshape(slots, columns, rows), keep_count.reshape(columns, rows))
    outgoing, sign = pl.pallas_call(
        lambda *refs: pack_kernel(*refs, tiles=tiles, depths=depths),
        out_shape=[
            jax.ShapeDtypeStruct((zblocks, 5, 1, lanes), jnp.float32),
            jax.ShapeDtypeStruct((2 * EDGE, lanes), jnp.float32),
        ],
        in_specs=[pl.BlockSpec(memory_space=pltpu.SMEM)] + [pl.BlockSpec(memory_space=pltpu.HBM)] * 2,
        out_specs=[vmem, vmem],
        scratch_shapes=[
            pltpu.VMEM((slots, columns, rows), jnp.float32),
            pltpu.VMEM((columns, rows), jnp.int32),
            pltpu.VMEM((depths, 5, tiles, lanes), jnp.float32),
            pltpu.SemaphoreType.DMA((2,)),
        ],
        compiler_params=params,
        name="pack",
    )(view_flip, *(pltpu.with_memory_space_constraint(x, pltpu.HBM) for x in inputs))
    devices = [(t, d) for d in range(depths) for t in range(tiles)]
    listed = sorted(range(zblocks), key=lambda i: listed_at(*devices[i], tiles, depths))
    chunks = outgoing.reshape(zblocks, 1, 5 * lanes)
    arrived = lax.all_to_all(
        chunks, ("depth", "tile"), split_axis=0, concat_axis=0, tiled=True, axis_index_groups=[listed]
    )
    return pl.pallas_call(
        lambda *refs: render_kernel(*refs, strip=strip, band=band, samples=EDGE * zblocks),
        out_shape=jax.ShapeDtypeStruct((4, strip * EDGE, band * EDGE), jnp.float32),
        in_specs=[pl.BlockSpec(memory_space=pltpu.SMEM), vmem, vmem],
        out_specs=pl.BlockSpec(memory_space=pltpu.HBM),
        scratch_shapes=[
            pltpu.VMEM((slots, zblocks, lanes), jnp.float32),
            pltpu.VMEM((4, strip * EDGE, band * EDGE), jnp.float32),
            pltpu.SemaphoreType.DMA((4,)),
        ],
        compiler_params=params,
        name="render",
    )(view_flip, sign, arrived.reshape(zblocks * 5, lanes))


def solution(mesh):
    placed = (P(None, "depth", "tile", None, None), P("depth", "tile", None, None), P("tile"))
    return jax.shard_map(
        per_device, mesh=mesh, in_specs=placed, out_specs=P(None, "tile", "depth"), check_vma=False
    )
```

```python
import math

import jax
import jax.numpy as jnp
from jax import lax
from jax.experimental import pallas as pl
from jax.experimental.pallas import tpu as pltpu
from jax.sharding import PartitionSpec as P

LOG2E = math.log2(math.e)
EDGE = 4


def cosine(frequency, position):
    factor = 0.5 if frequency == 0 else math.sqrt(0.5)
    return factor * math.cos(math.pi * (2 * position + 1) * frequency / 8.0)


def swap_halves(values):
    half = values.shape[1] // 2
    if values.shape[1] % 128 == 0:
        return pltpu.roll(values, half, 1)
    return jnp.concatenate([values[:, half:], values[:, :half]], axis=1)


def split(values, size):
    if size & (size - 1):
        return values // size, values % size
    return values >> (size.bit_length() - 1), values & (size - 1)


def listed_at(t, d, tiles, depths):
    return tiles * depths - 1 - d * tiles - t


def pack_kernel(
    flip_ref, coef_hbm, keep_hbm, out_ref, sign_ref, coef_ref, keep_ref, rows_ref, arrival, *, tiles, depths
):
    _, columns, rows = coef_ref.shape
    strip = columns // tiles
    band = rows // depths
    moves = [(coef_hbm.at[pl.ds(k, 4)], coef_ref.at[pl.ds(k, 4)]) for k in (0, 4)] + [(keep_hbm, keep_ref)]
    fetches = [pltpu.make_async_copy(a, b, arrival.at[i]) for i, (a, b) in enumerate(moves)]
    for fetch in fetches:
        fetch.start()
    for fetch in fetches:
        fetch.wait()
    lane = lax.broadcasted_iota(jnp.int32, (tiles, rows), 1)
    odd = split(lane, 2)[1]
    even = odd == 0

    def take(values, index):
        return jnp.take_along_axis(values, index, axis=1)

    other = lane + 1 - 2 * odd
    packed = []
    for b in range(strip):
        mine = pl.ds(b, tiles, stride=strip)
        keep = keep_ref[mine, :]
        slot = [coef_ref[k, mine, :] for k in range(8)]
        result = [slot[0]]
        for q in (1, 2, 3, 4):
            result.append(jnp.where(keep > q, slot[q], take(slot[8 - q], other)))
        result[4] = jnp.where(even, result[4], (9 - keep).astype(jnp.float32))
        packed.append(result)
    sign_ref[...] = jnp.full(sign_ref.shape, 1 - 2 * flip_ref[0], jnp.int32).astype(jnp.float32)
    half = strip * band // 2
    chunk, within = split(lane, band // 2)
    parity, column = split(chunk, strip)
    parity = split(parity, 2)[1]
    source = within * 2 + parity
    for d in range(depths):
        for q in range(5):
            gathered = [take(packed[b][q], source + d * band) for b in range(strip)]
            merged = gathered[0]
            for b in range(1, strip):
                merged = jnp.where(column == b, gathered[b], merged)
            rows_ref[d, q] = merged[:, : 2 * half]


    for d in range(depths):
        for t in range(tiles):
            out_ref[listed_at(t, d, tiles, depths), :, 0, :] = rows_ref[d, :, t, :]


def unpack(packed_ref, coef_ref, scales):
    zblocks, lanes = packed_ref.shape[0] // 5, packed_ref.shape[1]
    first = lax.broadcasted_iota(jnp.int32, (zblocks, lanes), 1) < lanes // 2
    row = [packed_ref[pl.ds(q, zblocks, stride=5), :] for q in range(5)]
    turned = [None] + [swap_halves(row[q]) for q in (1, 2, 3, 4)]
    keep = jnp.where(first, turned[4], 9.0 - row[4])
    slot = [row[0]] + [jnp.where(keep > q, row[q], 0.0) for q in (1, 2, 3)]
    slot.append(jnp.where(keep > 4, jnp.where(first, row[4], turned[4]), 0.0))
    slot += [jnp.where(keep > k, turned[8 - k], 0.0) for k in (5, 6, 7)]
    for k in range(8):
        coef_ref[k] = slot[k] * scales[k] if k in scales else slot[k]


def render_kernel(
    flip_ref, sign_ref, packed_ref, out_hbm, coef_ref, out_ref, leaving, *, strip, band, samples
):
    slots, zblocks, lanes = coef_ref.shape
    sign = sign_ref[...]
    flipped = flip_ref[0] > 0
    b1 = [cosine(1, i) for i in range(EDGE)]
    unpack(packed_ref, coef_ref, {0: 0.125 * LOG2E, 3: 0.25 * LOG2E * b1[0] * sign[:1]})
    row = lax.broadcasted_iota(jnp.int32, (2 * EDGE, lanes), 0)
    y, x = split(row, EDGE)

    def table(position, values):
        result = jnp.full((2 * EDGE, lanes), values[0], jnp.float32)
        for i in range(1, len(values)):
            result = jnp.where(position == i, jnp.float32(values[i]), result)
        return result

    x1 = table(x, b1)
    x2 = table(x, [cosine(2, i) for i in range(EDGE)])
    y1 = table(y, b1[:2])
    y2 = table(y, [cosine(2, i) for i in range(2)])
    c_x1 = (0.25 * LOG2E) * x1
    c_x2 = (0.25 * LOG2E) * x2
    c_y1 = (0.25 * LOG2E) * y1
    c_y2 = (0.25 * LOG2E) * y2
    c_xy = (0.5 * LOG2E) * x1 * y1
    c_zy = (0.5 * LOG2E * b1[0]) * y1 * sign
    ratio = b1[1] / b1[0]
    blue_factor = math.exp(-1.5)
    fade = -1.5 / samples

    def block(step, state):
        source = jnp.where(flipped, zblocks - 1 - step, step)
        zb = zblocks - 1 - source
        a = [
            jnp.broadcast_to(coef_ref[k, pl.ds(zb, 1), :], (2 * EDGE, lanes)) for k in range(slots)
        ]
        even = a[0] + a[2] * c_x1 + a[4] * c_y2 + a[6] * c_x2
        odd = a[1] * c_y1 + a[5] * c_xy
        g_even = a[3]
        g_odd = a[7] * c_zy
        halves = []
        for h in range(2):
            depth, before, red, green, blue = state[h]
            base = even + odd if h == 0 else even - odd
            g = g_even + g_odd if h == 0 else g_even - g_odd
            near = g * ratio
            for f in (base + g, base + near, base - near, base - g):
                v = jnp.exp2(f)
                one_u = 1.0 + v * v
                depth = depth + jnp.log2(one_u)
                after = jnp.exp2(fade * depth)
                weight = before - after
                before = after
                red = red + weight / one_u
                green = green + weight * jnp.exp2(f * (f * (-1.0 / LOG2E)))
                blue = blue + weight / (1.0 + blue_factor * v)
            halves.append((depth, before, red, green, blue))
        return tuple(halves)

    zero = jnp.zeros((2 * EDGE, lanes), jnp.float32)
    one = jnp.ones((2 * EDGE, lanes), jnp.float32)
    start = (zero, one, zero, zero, zero)
    state = lax.fori_loop(0, zblocks, block, (start, start), unroll=16)

    width = band * EDGE
    pick = lax.broadcasted_iota(jnp.int32, (2 * EDGE, width), 1)
    place, y_out = split(pick, EDGE)
    place, odd = split(place, 2)
    place = odd * (lanes // 2) + place
    outs = []
    for _, before, red, green, blue in state:
        opacity = 1.0 - before
        outs.append((opacity - red, green, blue, opacity))
    copies = [pltpu.make_async_copy(out_ref.at[ch], out_hbm.at[ch], leaving.at[ch]) for ch in range(4)]
    for ch in range(4):
        for b in range(strip):
            index = place + b * (band // 2)
            low = jnp.take_along_axis(outs[0][ch], index, axis=1)
            high = jnp.take_along_axis(outs[1][ch], index, axis=1)
            both = jnp.where(y_out < 2, low, high)
            first, second = both[:EDGE], both[EDGE:]
            use_first = (y_out[:EDGE] == 0) | (y_out[:EDGE] == 3)
            out_ref[ch, pl.ds(b * EDGE, EDGE), :] = jnp.where(use_first, first, second)
        copies[ch].start()
    for copy in copies:
        copy.wait()


def per_device(coefficients, keep_count, view_flip):
    tiles = lax.axis_size("tile")
    depths = lax.axis_size("depth")
    slots, _, _, columns, rows = coefficients.shape
    strip = columns // tiles
    band = rows // depths
    zblocks = tiles * depths
    vmem = pl.BlockSpec(memory_space=pltpu.VMEM)
    params = pltpu.CompilerParams(vmem_limit_bytes=8 * 1024 * 1024)
    lanes = strip * band
    inputs = (coefficients.reshape(slots, columns, rows), keep_count.reshape(columns, rows))
    outgoing, sign = pl.pallas_call(
        lambda *refs: pack_kernel(*refs, tiles=tiles, depths=depths),
        out_shape=[
            jax.ShapeDtypeStruct((zblocks, 5, 1, lanes), jnp.float32),
            jax.ShapeDtypeStruct((2 * EDGE, lanes), jnp.float32),
        ],
        in_specs=[pl.BlockSpec(memory_space=pltpu.SMEM)] + [pl.BlockSpec(memory_space=pltpu.HBM)] * 2,
        out_specs=[vmem, vmem],
        scratch_shapes=[
            pltpu.VMEM((slots, columns, rows), jnp.float32),
            pltpu.VMEM((columns, rows), jnp.int32),
            pltpu.VMEM((depths, 5, tiles, lanes), jnp.float32),
            pltpu.SemaphoreType.DMA((3,)),
        ],
        compiler_params=params,
        name="pack",
    )(view_flip, *(pltpu.with_memory_space_constraint(x, pltpu.HBM) for x in inputs))
    devices = [(t, d) for d in range(depths) for t in range(tiles)]
    listed = sorted(range(zblocks), key=lambda i: listed_at(*devices[i], tiles, depths))
    chunks = outgoing.reshape(zblocks, 1, 5 * lanes)
    arrived = lax.all_to_all(
        chunks, ("depth", "tile"), split_axis=0, concat_axis=0, tiled=True, axis_index_groups=[listed]
    )
    return pl.pallas_call(
        lambda *refs: render_kernel(*refs, strip=strip, band=band, samples=EDGE * zblocks),
        out_shape=jax.ShapeDtypeStruct((4, strip * EDGE, band * EDGE), jnp.float32),
        in_specs=[pl.BlockSpec(memory_space=pltpu.SMEM), vmem, vmem],
        out_specs=pl.BlockSpec(memory_space=pltpu.HBM),
        scratch_shapes=[
            pltpu.VMEM((slots, zblocks, lanes), jnp.float32),
            pltpu.VMEM((4, strip * EDGE, band * EDGE), jnp.float32),
            pltpu.SemaphoreType.DMA((4,)),
        ],
        compiler_params=params,
        name="render",
    )(view_flip, sign, arrived.reshape(zblocks * 5, lanes))


def solution(mesh):
    placed = (P(None, "depth", "tile", None, None), P("depth", "tile", None, None), P("tile"))
    return jax.shard_map(
        per_device, mesh=mesh, in_specs=placed, out_specs=P(None, "tile", "depth"), check_vma=False
    )
```

```python
import math

import jax
import jax.numpy as jnp
from jax import lax
from jax.experimental import pallas as pl
from jax.experimental.pallas import tpu as pltpu
from jax.sharding import PartitionSpec as P

LOG2E = math.log2(math.e)
EDGE = 4


def cosine(frequency, position):
    factor = 0.5 if frequency == 0 else math.sqrt(0.5)
    return factor * math.cos(math.pi * (2 * position + 1) * frequency / 8.0)


def swap_halves(values):
    half = values.shape[1] // 2
    if values.shape[1] % 128 == 0:
        return pltpu.roll(values, half, 1)
    return jnp.concatenate([values[:, half:], values[:, :half]], axis=1)


def split(values, size):
    if size & (size - 1):
        return values // size, values % size
    return values >> (size.bit_length() - 1), values & (size - 1)


def listed_at(t, d, tiles, depths):
    return tiles * depths - 1 - d * tiles - t


def pack_kernel(
    flip_ref, coef_hbm, keep_hbm, out_ref, sign_ref, coef_ref, keep_ref, rows_ref, arrival, *, tiles, depths
):
    _, columns, rows = coef_ref.shape
    strip = columns // tiles
    band = rows // depths
    moves = [(coef_hbm.at[pl.ds(k, 4)], coef_ref.at[pl.ds(k, 4)]) for k in (0, 4)] + [(keep_hbm, keep_ref)]
    fetches = [pltpu.make_async_copy(a, b, arrival.at[i]) for i, (a, b) in enumerate(moves)]
    for fetch in fetches:
        fetch.start()
    lane = lax.broadcasted_iota(jnp.int32, (tiles, rows), 1)
    odd = split(lane, 2)[1]
    even = odd == 0

    def take(values, index):
        return jnp.take_along_axis(values, index, axis=1)

    other = lane + 1 - 2 * odd
    sign_ref[...] = jnp.full(sign_ref.shape, 1 - 2 * flip_ref[0], jnp.int32).astype(jnp.float32)
    half = strip * band // 2
    chunk, within = split(lane, band // 2)
    parity, column = split(chunk, strip)
    parity = split(parity, 2)[1]
    source = within * 2 + parity
    sources = [source + d * band for d in range(depths)]
    for fetch in fetches:
        fetch.wait()
    packed = []
    for b in range(strip):
        mine = pl.ds(b, tiles, stride=strip)
        keep = keep_ref[mine, :]
        slot = [coef_ref[k, mine, :] for k in range(8)]
        result = [slot[0]]
        for q in (1, 2, 3, 4):
            result.append(jnp.where(keep > q, slot[q], take(slot[8 - q], other)))
        result[4] = jnp.where(even, result[4], (9 - keep).astype(jnp.float32))
        packed.append(result)
    for d in range(depths):
        for q in range(5):
            gathered = [take(packed[b][q], sources[d]) for b in range(strip)]
            merged = gathered[0]
            for b in range(1, strip):
                merged = jnp.where(column == b, gathered[b], merged)
            rows_ref[d, q] = merged[:, : 2 * half]


    for d in range(depths):
        for t in range(tiles):
            out_ref[listed_at(t, d, tiles, depths), :, 0, :] = rows_ref[d, :, t, :]


def unpack(packed_ref, coef_ref, scales):
    zblocks, lanes = packed_ref.shape[0] // 5, packed_ref.shape[1]
    first = lax.broadcasted_iota(jnp.int32, (zblocks, lanes), 1) < lanes // 2
    row = [packed_ref[pl.ds(q, zblocks, stride=5), :] for q in range(5)]
    turned = [None] + [swap_halves(row[q]) for q in (1, 2, 3, 4)]
    keep = jnp.where(first, turned[4], 9.0 - row[4])
    slot = [row[0]] + [jnp.where(keep > q, row[q], 0.0) for q in (1, 2, 3)]
    slot.append(jnp.where(keep > 4, jnp.where(first, row[4], turned[4]), 0.0))
    slot += [jnp.where(keep > k, turned[8 - k], 0.0) for k in (5, 6, 7)]
    for k in range(8):
        coef_ref[k] = slot[k] * scales[k] if k in scales else slot[k]


def render_kernel(
    flip_ref, sign_ref, packed_ref, out_hbm, coef_ref, out_ref, leaving, *, strip, band, samples
):
    slots, zblocks, lanes = coef_ref.shape
    sign = sign_ref[...]
    flipped = flip_ref[0] > 0
    b1 = [cosine(1, i) for i in range(EDGE)]
    unpack(packed_ref, coef_ref, {0: 0.125 * LOG2E, 3: 0.25 * LOG2E * b1[0] * sign[:1]})
    row = lax.broadcasted_iota(jnp.int32, (2 * EDGE, lanes), 0)
    y, x = split(row, EDGE)

    def table(position, values):
        result = jnp.full((2 * EDGE, lanes), values[0], jnp.float32)
        for i in range(1, len(values)):
            result = jnp.where(position == i, jnp.float32(values[i]), result)
        return result

    x1 = table(x, b1)
    x2 = table(x, [cosine(2, i) for i in range(EDGE)])
    y1 = table(y, b1[:2])
    y2 = table(y, [cosine(2, i) for i in range(2)])
    c_x1 = (0.25 * LOG2E) * x1
    c_x2 = (0.25 * LOG2E) * x2
    c_y1 = (0.25 * LOG2E) * y1
    c_y2 = (0.25 * LOG2E) * y2
    c_xy = (0.5 * LOG2E) * x1 * y1
    c_zy = (0.5 * LOG2E * b1[0]) * y1 * sign
    ratio = b1[1] / b1[0]
    blue_factor = math.exp(-1.5)
    fade = -1.5 / samples

    def block(step, state):
        source = jnp.where(flipped, zblocks - 1 - step, step)
        zb = zblocks - 1 - source
        a = [
            jnp.broadcast_to(coef_ref[k, pl.ds(zb, 1), :], (2 * EDGE, lanes)) for k in range(slots)
        ]
        even = a[0] + a[2] * c_x1 + a[4] * c_y2 + a[6] * c_x2
        odd = a[1] * c_y1 + a[5] * c_xy
        g_even = a[3]
        g_odd = a[7] * c_zy
        halves = []
        for h in range(2):
            depth, before, red, green, blue = state[h]
            base = even + odd if h == 0 else even - odd
            g = g_even + g_odd if h == 0 else g_even - g_odd
            near = g * ratio
            for f in (base + g, base + near, base - near, base - g):
                v = jnp.exp2(f)
                one_u = 1.0 + v * v
                depth = depth + jnp.log2(one_u)
                after = jnp.exp2(fade * depth)
                weight = before - after
                before = after
                red = red + weight / one_u
                green = green + weight * jnp.exp2(f * (f * (-1.0 / LOG2E)))
                blue = blue + weight / (1.0 + blue_factor * v)
            halves.append((depth, before, red, green, blue))
        return tuple(halves)

    zero = jnp.zeros((2 * EDGE, lanes), jnp.float32)
    one = jnp.ones((2 * EDGE, lanes), jnp.float32)
    start = (zero, one, zero, zero, zero)
    state = lax.fori_loop(0, zblocks, block, (start, start), unroll=16)

    width = band * EDGE
    pick = lax.broadcasted_iota(jnp.int32, (2 * EDGE, width), 1)
    place, y_out = split(pick, EDGE)
    place, odd = split(place, 2)
    place = odd * (lanes // 2) + place
    outs = []
    for _, before, red, green, blue in state:
        opacity = 1.0 - before
        outs.append((opacity - red, green, blue, opacity))
    copies = [pltpu.make_async_copy(out_ref.at[ch], out_hbm.at[ch], leaving.at[ch]) for ch in range(4)]
    for ch in range(4):
        for b in range(strip):
            index = place + b * (band // 2)
            low = jnp.take_along_axis(outs[0][ch], index, axis=1)
            high = jnp.take_along_axis(outs[1][ch], index, axis=1)
            both = jnp.where(y_out < 2, low, high)
            first, second = both[:EDGE], both[EDGE:]
            use_first = (y_out[:EDGE] == 0) | (y_out[:EDGE] == 3)
            out_ref[ch, pl.ds(b * EDGE, EDGE), :] = jnp.where(use_first, first, second)
        copies[ch].start()
    for copy in copies:
        copy.wait()


def per_device(coefficients, keep_count, view_flip):
    tiles = lax.axis_size("tile")
    depths = lax.axis_size("depth")
    slots, _, _, columns, rows = coefficients.shape
    strip = columns // tiles
    band = rows // depths
    zblocks = tiles * depths
    vmem = pl.BlockSpec(memory_space=pltpu.VMEM)
    params = pltpu.CompilerParams(vmem_limit_bytes=8 * 1024 * 1024)
    lanes = strip * band
    inputs = (coefficients.reshape(slots, columns, rows), keep_count.reshape(columns, rows))
    outgoing, sign = pl.pallas_call(
        lambda *refs: pack_kernel(*refs, tiles=tiles, depths=depths),
        out_shape=[
            jax.ShapeDtypeStruct((zblocks, 5, 1, lanes), jnp.float32),
            jax.ShapeDtypeStruct((2 * EDGE, lanes), jnp.float32),
        ],
        in_specs=[pl.BlockSpec(memory_space=pltpu.SMEM)] + [pl.BlockSpec(memory_space=pltpu.HBM)] * 2,
        out_specs=[vmem, vmem],
        scratch_shapes=[
            pltpu.VMEM((slots, columns, rows), jnp.float32),
            pltpu.VMEM((columns, rows), jnp.int32),
            pltpu.VMEM((depths, 5, tiles, lanes), jnp.float32),
            pltpu.SemaphoreType.DMA((3,)),
        ],
        compiler_params=params,
        name="pack",
    )(view_flip, *(pltpu.with_memory_space_constraint(x, pltpu.HBM) for x in inputs))
    devices = [(t, d) for d in range(depths) for t in range(tiles)]
    listed = sorted(range(zblocks), key=lambda i: listed_at(*devices[i], tiles, depths))
    chunks = outgoing.reshape(zblocks, 1, 5 * lanes)
    arrived = lax.all_to_all(
        chunks, ("depth", "tile"), split_axis=0, concat_axis=0, tiled=True, axis_index_groups=[listed]
    )
    return pl.pallas_call(
        lambda *refs: render_kernel(*refs, strip=strip, band=band, samples=EDGE * zblocks),
        out_shape=jax.ShapeDtypeStruct((4, strip * EDGE, band * EDGE), jnp.float32),
        in_specs=[pl.BlockSpec(memory_space=pltpu.SMEM), vmem, vmem],
        out_specs=pl.BlockSpec(memory_space=pltpu.HBM),
        scratch_shapes=[
            pltpu.VMEM((slots, zblocks, lanes), jnp.float32),
            pltpu.VMEM((4, strip * EDGE, band * EDGE), jnp.float32),
            pltpu.SemaphoreType.DMA((4,)),
        ],
        compiler_params=params,
        name="render",
    )(view_flip, sign, arrived.reshape(zblocks * 5, lanes))


def solution(mesh):
    placed = (P(None, "depth", "tile", None, None), P("depth", "tile", None, None), P("tile"))
    return jax.shard_map(
        per_device, mesh=mesh, in_specs=placed, out_specs=P(None, "tile", "depth"), check_vma=False
    )
```
